32 devices in a mesh: groups: 2 (over x), blk: 16 (over z, y, core).
Axes of the slice: x: 2, y: 2, z: 4, core: 2. Of those that a mesh axis runs over, the one named last changes fastest.
Arguments:
- spectrum: float32 [3, 36, 65536], P(None, None, ('groups', 'blk')), parts along dimension 2, may hold values from 0.1 to 2
- wind_vector: float32 [2, 65536], P(None, ('groups', 'blk')), parts along dimension 1, may hold values from -4 to 4
- dest_cell: int32 [65536], P(('groups', 'blk')), parts along dimension 0, may hold values from 0 to 32767, as said below
- counts: int32 [32], P(('groups', 'blk')), parts along dimension 0, may hold values from 1024 to 2048, as said below
- sea_mask: int32 [65536], P(('groups', 'blk')), parts along dimension 0, may hold values from 0 to 1, as said below
- dia_shift: int32 [2], replicated, may hold values from 1 to 9
Outputs:
- spectrum_next: float32 [3, 36, 65536], P(None, None, ('groups', 'blk')), parts along dimension 2
The draws below stay inside these ranges and needn't reach their ends.
There are 2 independent parts, one for each index of `groups`. The reference program is written for one: setup_inputs(seed, part) draws one part's arguments, and reference() takes and returns one part's arrays. A program takes and returns all parts, laid end to end along the dimension named above; an argument that names none is the same for every part. Nothing has to cross between parts.
Inputs may be any that keep to these rules, and one draw needn't show every extreme that they name: Slots of block d below counts[d] hold sea points, the others are unused; some block has all 2048 slots live. `dest_cell`: distinct over all slots; cell c lies in band c // 2048. Of one block's live slots at most 128 name cells of one band, exactly 128 for some block and band, and some band receives 128 live points from every block. `sea_mask`: 1 exactly at the cells that live slots name.
All inputs are finite; a program needn't handle non-finite values.
Results may differ from the reference program's by a relative error of at most 0.0003.
Values sent between devices are 32-bit elements; how exact they have to be, the bound alone decides.
No kernel may reach another device: no remote copies, remote signals or barrier semaphores. Data moves between devices by JAX's collectives and lax.ppermute only.
A program may use at most 64 MiB of HBM per device.

```python
import math
import jax
import jax.numpy as jnp
from jax import lax

NF = 3
ND = 36
P_DEV = 2048
NLON = 512
SUBSTEPS = 2
BANDS = 16
CAP = 128
SEA = 32768
LATB = 4


def layout_tables(key):
    key = jax.random.fold_in(key, 101)
    keys = jax.random.split(key, 5)
    counts = jax.random.randint(keys[0], (BANDS,), P_DEV // 2, P_DEV + 1, dtype=jnp.int32)
    fullest = jax.random.randint(keys[1], (), 0, BANDS, dtype=jnp.int32)
    counts = counts.at[fullest].set(P_DEV)
    target_band = jax.random.randint(keys[2], (), 0, BANDS, dtype=jnp.int32)
    lagging = jax.random.randint(keys[3], (BANDS,), 0, max(BANDS // 2, 1), dtype=jnp.int32)
    rotation = (target_band - lagging) % BANDS
    slot_index = jnp.arange(P_DEV, dtype=jnp.int32)
    source_ids = jnp.arange(BANDS, dtype=jnp.int32)
    band_of = (slot_index[None, :] // CAP + rotation[:, None]) % BANDS

    def shuffle_one(band_key):
        return jax.random.permutation(band_key, P_DEV).astype(jnp.int32)
    shuffles = jax.vmap(shuffle_one)(jax.random.split(keys[4], BANDS))
    within = source_ids[:, None] * CAP + slot_index[None, :] % CAP
    local_cell = shuffles[band_of, within]
    destination = (band_of * P_DEV + local_cell).reshape(-1).astype(jnp.int32)
    live_slot = (slot_index[None, :] < counts[:, None]).reshape(-1).astype(jnp.int32)
    sea_cells = jnp.zeros((SEA,), jnp.int32).at[destination].set(live_slot)
    return (counts, destination, sea_cells)


def draw_dest_cell(key, part):
    tables = layout_tables(key)
    return tables[1]


def draw_counts(key, part):
    tables = layout_tables(key)
    return tables[0]


def draw_sea_mask(key, part):
    tables = layout_tables(key)
    return tables[2]


def block_levels(stream_key, shape, cuts, low, top_value):
    factor_of, own = 1.0, jax.random.fold_in(stream_key, 6)
    for position, shards_of in cuts:
        draws = jnp.exp(jax.random.uniform(jax.random.fold_in(own, position), (shards_of,), jnp.float32, low / len(cuts), top_value / len(cuts)))
        factor_of = factor_of * jnp.repeat(draws, shape[position] // shards_of).reshape([-1 if axis == position else 1 for axis in range(len(shape))])
    return factor_of


def gaussian(rng, shape, spread, bound, shards=(), kind=jnp.bfloat16):
    level = block_levels(rng, shape, shards, -0.22, 0.18) if shards else 1.0
    entries = jax.random.normal(rng, shape, jnp.float32) * spread * level
    return jnp.minimum(jnp.maximum(entries, -bound), bound).astype(kind)


def setup_inputs(seed: int = 0, part: int = 0) -> dict:
    key_list = jax.random.split(jax.random.key(seed), 7)
    part_splits = jax.random.split(jax.random.fold_in(key_list[6], part), 7)
    spectrum = jnp.clip(jnp.exp(math.log(2.0) - 2.9957323 * jax.random.uniform(part_splits[0], (NF, ND, SEA), jnp.float32) ** block_levels(part_splits[0], (NF, ND, SEA), ((2, 16),), -0.2, 0.2)), 0.1, 2.0)
    wind_vector = gaussian(part_splits[1], (2, SEA), 0.8, 4.0, ((1, 16),), jnp.float32)
    dest_cell = draw_dest_cell(jax.random.fold_in(jax.random.fold_in(key_list[6], part), 71), part)
    counts = draw_counts(jax.random.fold_in(jax.random.fold_in(key_list[6], part), 71), part)
    sea_mask = draw_sea_mask(jax.random.fold_in(jax.random.fold_in(key_list[6], part), 71), part)
    dia_shift = jax.random.randint(key_list[5], (2,), 1, ND // 4 + 1).astype(jnp.int32)
    return dict(spectrum=spectrum, wind_vector=wind_vector, dest_cell=dest_cell, counts=counts, sea_mask=sea_mask, dia_shift=dia_shift)


def source_terms(spectra, wind_field, dia_shift, energy_mean, frequency):
    count_dirs = spectra.shape[1]
    angles = 2.0 * math.pi * jnp.arange(count_dirs, dtype=jnp.int32).astype(jnp.float32) / count_dirs
    along_wind = wind_field[0][None, :] * jnp.cos(angles)[:, None] + wind_field[1][None, :] * jnp.sin(angles)[:, None]
    growth = (0.15 + 0.05 * frequency)[:, None, None] * jnp.maximum(along_wind - 0.3, 0.0)[None]
    decay_rate = (0.2 + 0.1 * frequency)[:, None, None] * energy_mean[None, None, :]
    quadruplet = 0.1 * (jnp.roll(spectra, -dia_shift[0], axis=1) * jnp.roll(spectra, dia_shift[1], axis=1) - spectra * spectra)
    return spectra * jnp.exp(growth - decay_rate) + quadruplet


def advance(wave_field, south_rows, north_rows, latitude, frequency, sea_field):
    count_dirs = wave_field.shape[1]
    angles = 2.0 * math.pi * jnp.arange(count_dirs, dtype=jnp.int32).astype(jnp.float32) / count_dirs
    group_speed = 1.0 / (1.0 + 0.25 * frequency)
    lat_courant = (0.5 * group_speed[:, None] * jnp.sin(angles)[None, :])[:, :, None, None]
    lon_courant = (0.25 * group_speed[:, None, None] * jnp.cos(angles)[None, :, None] / jnp.cos(latitude)[None, None, :])[:, :, :, None]
    turn_courant = (-0.3 * group_speed[:, None, None] * jnp.cos(angles)[None, :, None] * jnp.tan(latitude)[None, None, :])[:, :, :, None]
    west_side = jnp.roll(wave_field, 1, axis=3)
    east_side = jnp.roll(wave_field, -1, axis=3)
    advected = wave_field - (jnp.maximum(lat_courant, 0.0) * (wave_field - south_rows) + jnp.minimum(lat_courant, 0.0) * (north_rows - wave_field))
    advected = advected - (jnp.maximum(lon_courant, 0.0) * (wave_field - west_side) + jnp.minimum(lon_courant, 0.0) * (east_side - wave_field))
    advected = advected * sea_field
    lower_dir = jnp.roll(advected, 1, axis=1)
    upper_dir = jnp.roll(advected, -1, axis=1)
    turned = advected - (jnp.maximum(turn_courant, 0.0) * (advected - lower_dir) + jnp.minimum(turn_courant, 0.0) * (upper_dir - advected))
    return turned * sea_field


def reference(spectrum, wind_vector, dest_cell, counts, sea_mask, dia_shift):
    slot_ids = jnp.arange(SEA, dtype=jnp.int32)
    live_slot = (slot_ids % P_DEV) < counts[slot_ids // P_DEV]
    target = jnp.where(live_slot, dest_cell, SEA).astype(jnp.int32)
    energy_mean = jnp.mean(spectrum, axis=(0, 1))
    rows_all = LATB * BANDS
    latitude = (jnp.arange(rows_all, dtype=jnp.int32).astype(jnp.float32) + 0.5) / rows_all * (2.0 * math.pi / 3.0) - math.pi / 3.0
    sea_field = sea_mask.astype(jnp.float32).reshape(rows_all, NLON)
    live_float = live_slot.astype(jnp.float32)

    def one_frequency(inputs):
        spectra, frequency = inputs
        spectra = spectra[None]
        frequency = frequency[None]
        sourced = source_terms(spectra, wind_vector, dia_shift, energy_mean, frequency)
        wave_field = jnp.zeros((1, ND, SEA + 1), jnp.float32).at[:, :, target].set(sourced)[:, :, :SEA]
        wave_field = wave_field.reshape(1, ND, rows_all, NLON)
        zero_row = jnp.zeros((1, ND, 1, NLON), jnp.float32)
        for substep in range(SUBSTEPS):
            south_rows = jnp.concatenate([zero_row, wave_field[:, :, :-1]], axis=2)
            north_rows = jnp.concatenate([wave_field[:, :, 1:], zero_row], axis=2)
            wave_field = advance(wave_field, south_rows, north_rows, latitude, frequency, sea_field)
        return wave_field.reshape(ND, SEA)[:, dest_cell] * live_float[None, :]

    frequencies = jnp.arange(NF, dtype=jnp.int32).astype(jnp.float32)
    return lax.map(one_frequency, (spectrum, frequencies))
```

```python
import functools
import math

import jax
import jax.numpy as jnp
from jax import lax
from jax.experimental import pallas as pl
from jax.experimental.pallas import tpu as pltpu
from jax.sharding import PartitionSpec as P

NLON = 512
SUBSTEPS = 2
LANES = 128
TILE = 256
STRIDE = 40
F32 = jnp.float32
BF16 = jnp.bfloat16
VMEM_LIMIT = 48 * 1024 * 1024


def snake_row(blocks):
    chips = max(blocks // 2, 1)
    return 1 << ((chips.bit_length() - 1) // 2)


def snake(index, blocks):
    row = snake_row(blocks)
    if blocks % (2 * row):
        return index
    core = lax.rem(index, 2)
    chip = lax.div(index, 2)
    line = lax.div(chip, row)
    place = lax.rem(chip, row)
    place = jnp.where(lax.rem(line, 2) == 1, row - 1 - place, place)
    return (line * row + place) * 2 + core


def halo_pairs(blocks):
    row = snake_row(blocks)
    order = []
    for band in range(blocks):
        if blocks % (2 * row):
            order.append(band)
            continue
        core, chip = band % 2, band // 2
        line, place = chip // row, chip % row
        if line % 2:
            place = row - 1 - place
        order.append((line * row + place) * 2 + core)
    up = [(order[b], order[b + 1]) for b in range(blocks - 1)]
    return up, [(t, s) for s, t in up]


def column(values):
    return jnp.concatenate([jnp.full((1, 1), float(v), F32) for v in values], axis=0)


def split(x):
    high = x.astype(BF16)
    return high, (x - high.astype(F32)).astype(BF16)


def one_hot(row, start, width):
    ids = lax.broadcasted_iota(jnp.int32, (TILE, width), 0)
    return (ids == (row - start)).astype(F32).astype(BF16)


def matmul_nt(data, table):
    return lax.dot_general(
        data, table, (((1,), (1,)), ((), ())), preferred_element_type=F32
    )


def direction_trig(dirs, rows):
    j = lax.broadcasted_iota(jnp.int32, (rows, LANES), 0)
    angles = (2.0 * math.pi / dirs) * j.astype(F32)
    return jnp.cos(angles), jnp.sin(angles)


def source_kernel(
    blocks, cap, shift_ref, count_ref, spec_ref, wind_ref, dest_ref, send_ref, pos_ref, dbl, lhs
):
    freqs, dirs, points = spec_ref.shape
    rows = lhs.shape[0] // 2
    dest = dest_ref[...]
    slot = lax.broadcasted_iota(jnp.int32, (1, points), 1)
    live = slot < count_ref[0]
    band = lax.shift_right_logical(dest, points.bit_length() - 1)
    band = jnp.where(live, band, -1)
    owner_band = snake(lax.broadcasted_iota(jnp.int32, (blocks, 1), 0), blocks)
    hits = (band == owner_band).astype(F32)
    tri_r = lax.broadcasted_iota(jnp.int32, (LANES, LANES), 0)
    tri_c = lax.broadcasted_iota(jnp.int32, (LANES, LANES), 1)
    upper = (tri_r <= tri_c).astype(F32).astype(BF16)
    ones = jnp.ones((LANES, LANES), BF16)
    base = (lax.broadcasted_iota(jnp.int32, (blocks, LANES), 0) * cap).astype(F32)
    for c in range(points // LANES):
        piece = hits[:, c * LANES : (c + 1) * LANES]
        packed = piece.astype(BF16)
        running = jnp.dot(packed, upper, preferred_element_type=F32) + base
        base = base + jnp.dot(packed, ones, preferred_element_type=F32)
        where_to = jnp.sum(piece * running, axis=0, keepdims=True) - 1.0
        pos_ref[:, c * LANES : (c + 1) * LANES] = where_to.astype(jnp.int32)
    total = jnp.zeros((1, points), F32)
    for f in range(freqs):
        x = spec_ref[f]
        dbl[f, 0:dirs, :] = x
        dbl[f, dirs : 2 * dirs, :] = x
        total = total + jnp.sum(x, axis=0, keepdims=True)
    mean = total * (1.0 / (freqs * dirs))
    cos_a, sin_a = direction_trig(dirs, dirs)
    along = wind_ref[0:1, :] * cos_a[:, 0:1] + wind_ref[1:2, :] * sin_a[:, 0:1]
    drive = jnp.maximum(along - 0.3, 0.0)
    for f in range(freqs):
        x = spec_ref[f]
        twice = dbl[f]
        ahead = pltpu.roll(twice, 2 * dirs - shift_ref[0], 0)[0:dirs]
        behind = pltpu.roll(twice, shift_ref[1], 0)[0:dirs]
        out = x * jnp.exp((0.15 + 0.05 * f) * drive - (0.2 + 0.1 * f) * mean) + 0.1 * (
            ahead * behind - x * x
        )
        dbl[f, 0:dirs, :] = out
    extra = rows - freqs * dirs
    local = (lax.bitwise_and(dest, points - 1) + 1).astype(F32)
    whole = jnp.concatenate(
        [dbl[f, 0:dirs, :] for f in range(freqs)] + [jnp.broadcast_to(local, (extra, points))],
        axis=0,
    )
    high, low = split(whole)
    lhs[0:rows, :] = high
    lhs[rows : 2 * rows, :] = low
    pos = pos_ref[...]

    def body(t, carry):
        table = one_hot(pos, t * TILE, points)
        both = matmul_nt(lhs[...], table)
        out = both[0:rows] + both[rows : 2 * rows]
        for h in range(TILE // LANES):
            send_ref[t * (TILE // LANES) + h] = out[:, h * LANES : (h + 1) * LANES]
        return carry

    lax.fori_loop(0, points // TILE, body, 0)


def spread_rows(get, freqs, dirs, points, lhs):
    rows = lhs.shape[0] // 2
    fill = jnp.ones((STRIDE - dirs - 2, LANES), F32)
    for c in range(points // LANES):
        x = get(c)
        pieces = []
        for f in range(freqs):
            one = x[f * dirs : (f + 1) * dirs]
            pieces += [one, one[0:1], fill, one[dirs - 1 : dirs]]
        high, low = split(jnp.concatenate(pieces, axis=0))
        lhs[0:rows, c * LANES : (c + 1) * LANES] = high
        lhs[rows : 2 * rows, c * LANES : (c + 1) * LANES] = low


def place_kernel(freqs, dirs, recv_ref, field_ref, up_ref, down_ref, cell_ref, lhs):
    points = cell_ref.shape[1]
    rows = freqs * STRIDE
    label = freqs * dirs
    for c in range(points // LANES):
        cell_ref[:, c * LANES : (c + 1) * LANES] = (
            recv_ref[c, label : label + 1, :].astype(jnp.int32) - 1
        )
    spread_rows(lambda c: recv_ref[c], freqs, dirs, points, lhs)
    cells = cell_ref[...]

    def body(t, carry):
        table = one_hot(cells, t * TILE, points)
        both = matmul_nt(lhs[...], table)
        where = pl.ds(pl.multiple_of(t * TILE, TILE), TILE)
        field_ref[:, where] = both[0:rows] + both[rows : 2 * rows]
        return carry

    lax.fori_loop(0, points // TILE, body, 0)
    half = dirs // 2
    width = half + 1
    edge = up_ref.shape[1]
    for f in range(freqs):
        top = field_ref[f * STRIDE : f * STRIDE + width, points - edge : points]
        up_ref[f * width : (f + 1) * width, :] = top
        low = field_ref[f * STRIDE + half : f * STRIDE + half + width, 0:edge]
        down_ref[f * width : (f + 1) * width, :] = low
    left = up_ref.shape[0] - freqs * width
    mask = field_ref[dirs + 1 : dirs + 2, :]
    up_ref[freqs * width :, :] = jnp.broadcast_to(mask[:, points - edge : points], (left, edge))
    down_ref[freqs * width :, :] = jnp.broadcast_to(mask[:, 0:edge], (left, edge))


def roll_lanes(x, shift):
    return pltpu.roll(x, shift % x.shape[1], 1)


def step_kernel(
    freqs, dirs, blocks, field_ref, south_ref, north_ref, cell_ref, back_ref, ext, mid, lhs
):
    points = field_ref.shape[1]
    rows = freqs * STRIDE
    row_count = points // NLON
    half = dirs // 2
    width = half + 1
    ghost = SUBSTEPS
    band = snake(lax.axis_index("blk"), blocks)
    rows_all = row_count * blocks

    def lanes(row):
        return slice(row * NLON, (row + 1) * NLON)

    ext[:, 0 : ghost * NLON] = jnp.zeros((rows, ghost * NLON), F32)
    ext[:, (ghost + row_count) * NLON :] = jnp.zeros((rows, ghost * NLON), F32)
    ext[:, ghost * NLON : (ghost + row_count) * NLON] = field_ref[...]
    for f in range(freqs):
        ext[f * STRIDE : f * STRIDE + width, 0 : ghost * NLON] = south_ref[
            f * width : (f + 1) * width, :
        ]
        ext[f * STRIDE + half : f * STRIDE + half + width, (ghost + row_count) * NLON :] = (
            north_ref[f * width : (f + 1) * width, :]
        )
        spot = f * width + dirs - 1 - half
        ext[(f + 1) * STRIDE - 1 : (f + 1) * STRIDE, (ghost + row_count) * NLON :] = north_ref[
            spot : spot + 1, :
        ]
    at = freqs * width
    masks = []
    for row in range(-ghost, row_count + ghost):
        if row < 0:
            masks.append(south_ref[at : at + 1, lanes(row + ghost)])
        elif row < row_count:
            masks.append(field_ref[dirs + 1 : dirs + 2, lanes(row)])
        else:
            masks.append(north_ref[at : at + 1, lanes(row - row_count)])

    j = lax.broadcasted_iota(jnp.int32, (STRIDE, LANES), 0)
    j = jnp.where(j < dirs, j, jnp.where(j < STRIDE - 1, j - dirs, dirs - 1))
    angles = (2.0 * math.pi / dirs) * j.astype(F32)
    sin_a = jnp.where((j == 0) | (j == half), 0.0, jnp.sin(angles))
    cos_a = jnp.cos(angles)
    from_south = (sin_a > 0.0)[:, 0:1]
    from_west = (cos_a > 0.0)[:, 0:1]
    cy_base = 0.5 * jnp.abs(sin_a)
    cx_base = 0.25 * jnp.abs(cos_a)

    def advance(src, dst, first, last, shift):
        for row in range(first, last):
            spot = (band * row_count + row).astype(F32) + 0.5
            lat = jnp.full((STRIDE, LANES), spot / rows_all * (2.0 * math.pi / 3.0) - math.pi / 3.0)
            sec = 1.0 / jnp.cos(lat)
            tan = jnp.sin(lat) * sec
            turn = -0.3 * cos_a * tan
            from_lower = (turn > 0.0)[:, 0:1]
            sea = masks[row + ghost]
            for f in range(freqs):
                speed = 1.0 / (1.0 + 0.25 * f)
                cy = (speed * cy_base)[:, 0:1]
                cx = (speed * cx_base * sec)[:, 0:1]
                ct = (speed * jnp.abs(turn))[:, 0:1]
                piece = slice(f * STRIDE, (f + 1) * STRIDE)
                x = src[piece, lanes(row + shift)]
                meridional = jnp.where(
                    from_south, src[piece, lanes(row + shift - 1)], src[piece, lanes(row + shift + 1)]
                )
                zonal = jnp.where(from_west, roll_lanes(x, 1), roll_lanes(x, -1))
                adv = (x - cy * (x - meridional) - cx * (x - zonal)) * sea
                lower = pltpu.roll(adv, 1, 0)
                upper = pltpu.roll(adv, STRIDE - 1, 0)
                out = (adv - ct * (adv - jnp.where(from_lower, lower, upper))) * sea
                dst(f, row, out)

    def keep(f, row, out):
        out = jnp.concatenate(
            [out[0:dirs], out[0:1], out[dirs + 1 : STRIDE - 1], out[dirs - 1 : dirs]], axis=0
        )
        mid[f * STRIDE : (f + 1) * STRIDE, lanes(row + 1)] = out

    def last(f, row, out):
        high, low = split(out)
        lhs[f * STRIDE : (f + 1) * STRIDE, lanes(row)] = high
        lhs[rows + f * STRIDE : rows + (f + 1) * STRIDE, lanes(row)] = low

    advance(ext, keep, -1, row_count + 1, ghost)
    advance(mid, last, 0, row_count, 1)

    def body(t, carry):
        where = pl.ds(pl.multiple_of(t * TILE, TILE), TILE)
        cells = cell_ref[:, where]
        table = jnp.concatenate(
            [one_hot(cells, k * TILE, TILE) for k in range(points // TILE)], axis=0
        )
        both = jnp.dot(lhs[...], table, preferred_element_type=F32)
        out = both[0:rows] + both[rows : 2 * rows]
        packed = jnp.concatenate(
            [out[f * STRIDE : f * STRIDE + dirs] for f in range(freqs)], axis=0
        )
        for h in range(TILE // LANES):
            back_ref[t * (TILE // LANES) + h] = packed[:, h * LANES : (h + 1) * LANES]
        return carry

    lax.fori_loop(0, points // TILE, body, 0)


def pick_kernel(freqs, dirs, recv_ref, pos_ref, out_ref, lhs):
    points = pos_ref.shape[1]
    rows = freqs * STRIDE
    spread_rows(lambda c: recv_ref[c], freqs, dirs, points, lhs)

    def body(t, carry):
        where = pl.ds(pl.multiple_of(t * TILE, TILE), TILE)
        wanted = pos_ref[:, where]
        table = jnp.concatenate(
            [one_hot(wanted, k * TILE, TILE) for k in range(points // TILE)], axis=0
        )
        both = jnp.dot(lhs[...], table, preferred_element_type=F32)
        out = both[0:rows] + both[rows : 2 * rows]
        for f in range(freqs):
            out_ref[f, :, where] = out[f * STRIDE : f * STRIDE + dirs]
        return carry

    lax.fori_loop(0, points // TILE, body, 0)


def exchange(x, blocks, cap):
    if cap == LANES:
        return lax.all_to_all(x, "blk", split_axis=0, concat_axis=0, tiled=True)
    pieces, rows, lanes = x.shape
    x = jnp.moveaxis(x, 1, 0).reshape(rows, blocks, cap)
    x = lax.all_to_all(x, "blk", split_axis=1, concat_axis=1, tiled=True)
    return jnp.moveaxis(x.reshape(rows, pieces, lanes), 0, 1)


def per_device(spectrum, wind_vector, dest_cell, counts, sea_mask, dia_shift):
    blocks = lax.axis_size("blk")
    freqs, dirs, points = spectrum.shape
    cap = points // blocks
    pieces = points // LANES
    rows = freqs * STRIDE
    send_rows = -(-(freqs * dirs + 1) // 8) * 8
    edge = SUBSTEPS * NLON
    edge_rows = -(-(freqs * (dirs // 2 + 1) + 1) // 8) * 8
    vmem = pl.BlockSpec(memory_space=pltpu.VMEM)
    smem = pl.BlockSpec(memory_space=pltpu.SMEM)
    params = pltpu.CompilerParams(vmem_limit_bytes=VMEM_LIMIT)

    def arr(shape, dtype=F32):
        return jax.ShapeDtypeStruct(shape, dtype)

    send, position = pl.pallas_call(
        functools.partial(source_kernel, blocks, cap),
        out_shape=(arr((pieces, send_rows, LANES)), arr((1, points), jnp.int32)),
        in_specs=[smem, smem, vmem, vmem, vmem],
        out_specs=(vmem, vmem),
        scratch_shapes=[
            pltpu.VMEM((freqs, 2 * dirs, points), F32),
            pltpu.VMEM((2 * send_rows, points), BF16),
        ],
        compiler_params=params,
        name="source",
    )(dia_shift, counts, spectrum, wind_vector, dest_cell.reshape(1, points))
    arrived = exchange(send, blocks, cap)
    field, up, down, cells = pl.pallas_call(
        functools.partial(place_kernel, freqs, dirs),
        out_shape=(
            arr((rows, points)),
            arr((edge_rows, edge)),
            arr((edge_rows, edge)),
            arr((1, points), jnp.int32),
        ),
        in_specs=[vmem],
        out_specs=(vmem, vmem, vmem, vmem),
        scratch_shapes=[pltpu.VMEM((2 * rows, points), BF16)],
        compiler_params=params,
        name="place",
    )(arrived)
    forward, backward = halo_pairs(blocks)
    south = lax.ppermute(up, "blk", forward)
    north = lax.ppermute(down, "blk", backward)
    row_count = points // NLON
    back = pl.pallas_call(
        functools.partial(step_kernel, freqs, dirs, blocks),
        out_shape=arr((pieces, freqs * dirs, LANES)),
        in_specs=[vmem] * 4,
        out_specs=vmem,
        scratch_shapes=[
            pltpu.VMEM((rows, points + 2 * edge), F32),
            pltpu.VMEM((rows, points + 2 * NLON), F32),
            pltpu.VMEM((2 * rows, points), BF16),
        ],
        compiler_params=params,
        name="step",
    )(field, south, north, cells)
    returned = exchange(back, blocks, cap)
    return pl.pallas_call(
        functools.partial(pick_kernel, freqs, dirs),
        out_shape=arr((freqs, dirs, points)),
        in_specs=[vmem, vmem],
        out_specs=vmem,
        scratch_shapes=[pltpu.VMEM((2 * rows, points), BF16)],
        compiler_params=params,
        name="pick",
    )(returned, position)


def solution(mesh):
    placed = (
        P(None, None, ("groups", "blk")),
        P(None, ("groups", "blk")),
        P(("groups", "blk")),
        P(("groups", "blk")),
        P(("groups", "blk")),
        P(),
    )
    return jax.shard_map(
        per_device,
        mesh=mesh,
        in_specs=placed,
        out_specs=P(None, None, ("groups", "blk")),
        check_vma=False,
    )
```

```python
import functools
import math

import jax
import jax.numpy as jnp
from jax import lax
from jax.experimental import pallas as pl
from jax.experimental.pallas import tpu as pltpu
from jax.sharding import PartitionSpec as P

NLON = 512
SUBSTEPS = 2
LANES = 128
TILE = 256
STRIDE = 40
F32 = jnp.float32
BF16 = jnp.bfloat16
VMEM_LIMIT = 40 * 1024 * 1024
SOURCE_LIMIT = 60 * 1024 * 1024


def snake_row(blocks):
    chips = max(blocks // 2, 1)
    return 1 << ((chips.bit_length() - 1) // 2)


def snake(index, blocks):
    row = snake_row(blocks)
    if blocks % (2 * row):
        return index
    core = lax.rem(index, 2)
    chip = lax.div(index, 2)
    line = lax.div(chip, row)
    place = lax.rem(chip, row)
    place = jnp.where(lax.rem(line, 2) == 1, row - 1 - place, place)
    return (line * row + place) * 2 + core


def halo_swaps(blocks):
    row = snake_row(blocks)
    order = []
    for band in range(blocks):
        if blocks % (2 * row):
            order.append(band)
            continue
        core, chip = band % 2, band // 2
        line, place = chip // row, chip % row
        if line % 2:
            place = row - 1 - place
        order.append((line * row + place) * 2 + core)

    def swaps(first):
        pairs = []
        for band in range(first, blocks - 1, 2):
            low, high = order[band], order[band + 1]
            pairs += [(low, high), (high, low)]
        return pairs

    return swaps(0), swaps(1)


def split(x):
    high = x.astype(BF16)
    return high, (x - high.astype(F32)).astype(BF16)


def one_hot(row, start, width):
    ids = lax.broadcasted_iota(jnp.int32, (TILE, width), 0)
    return (ids == (row - start)).astype(F32).astype(BF16)


def matmul_nt(data, table):
    return lax.dot_general(
        data, table, (((1,), (1,)), ((), ())), preferred_element_type=F32
    )


def direction_trig(dirs, rows):
    j = lax.broadcasted_iota(jnp.int32, (rows, LANES), 0)
    angles = (2.0 * math.pi / dirs) * j.astype(F32)
    return jnp.cos(angles), jnp.sin(angles)


def source_kernel(
    blocks,
    cap,
    shift_in,
    count_in,
    spec_in,
    wind_in,
    dest_in,
    send_ref,
    pos_ref,
    shift_ref,
    count_ref,
    spec_ref,
    wind_ref,
    dest_ref,
    dbl,
    lhs,
    sems,
):
    freqs, dirs, points = spec_ref.shape
    rows = lhs.shape[0] // 2
    pairs = (
        (dest_in, dest_ref),
        (count_in, count_ref),
        (shift_in, shift_ref),
        (wind_in, wind_ref),
        (spec_in, spec_ref),
    )
    copies = [pltpu.make_async_copy(a, b, sems.at[i]) for i, (a, b) in enumerate(pairs)]
    for copy in copies:
        copy.start()
    copies[0].wait()
    copies[1].wait()
    dest = dest_ref[...]
    slot = lax.broadcasted_iota(jnp.int32, (1, points), 1)
    live = slot < count_ref[0]
    band = lax.shift_right_logical(dest, points.bit_length() - 1)
    band = jnp.where(live, band, -1)
    owner_band = snake(lax.broadcasted_iota(jnp.int32, (blocks, 1), 0), blocks)
    hits = (band == owner_band).astype(F32)
    tri_r = lax.broadcasted_iota(jnp.int32, (LANES, LANES), 0)
    tri_c = lax.broadcasted_iota(jnp.int32, (LANES, LANES), 1)
    upper = (tri_r <= tri_c).astype(F32).astype(BF16)
    ones = jnp.ones((LANES, LANES), BF16)
    base = (lax.broadcasted_iota(jnp.int32, (blocks, LANES), 0) * cap).astype(F32)
    for c in range(points // LANES):
        piece = hits[:, c * LANES : (c + 1) * LANES]
        packed = piece.astype(BF16)
        running = jnp.dot(packed, upper, preferred_element_type=F32) + base
        base = base + jnp.dot(packed, ones, preferred_element_type=F32)
        where_to = jnp.sum(piece * running, axis=0, keepdims=True) - 1.0
        pos_ref[:, c * LANES : (c + 1) * LANES] = where_to.astype(jnp.int32)
    for copy in copies[2:]:
        copy.wait()
    total = jnp.zeros((1, points), F32)
    for f in range(freqs):
        x = spec_ref[f]
        dbl[f, 0:dirs, :] = x
        dbl[f, dirs : 2 * dirs, :] = x
        total = total + jnp.sum(x, axis=0, keepdims=True)
    mean = total * (1.0 / (freqs * dirs))
    cos_a, sin_a = direction_trig(dirs, dirs)
    along = wind_ref[0:1, :] * cos_a[:, 0:1] + wind_ref[1:2, :] * sin_a[:, 0:1]
    drive = jnp.maximum(along - 0.3, 0.0)
    span = -(-(dirs + dirs // 4) // 8) * 8
    for f in range(freqs):
        x = spec_ref[f]
        ahead = pltpu.roll(dbl[f, 0:span, :], span - shift_ref[0], 0)[0:dirs]
        offset = 2 * dirs - span
        behind = pltpu.roll(dbl[f, offset:, :], shift_ref[1] + span - (dirs - offset), 0)[0:dirs]
        out = x * jnp.exp((0.15 + 0.05 * f) * drive - (0.2 + 0.1 * f) * mean) + 0.1 * (
            ahead * behind - x * x
        )
        dbl[f, 0:dirs, :] = out
    extra = rows - freqs * dirs
    local = (lax.bitwise_and(dest, points - 1) + 1).astype(F32)
    whole = jnp.concatenate(
        [dbl[f, 0:dirs, :] for f in range(freqs)] + [jnp.broadcast_to(local, (extra, points))],
        axis=0,
    )
    high, low = split(whole)
    lhs[0:rows, :] = high
    lhs[rows : 2 * rows, :] = low
    pos = pos_ref[...]

    def body(t, carry):
        table = one_hot(pos, t * TILE, points)
        both = matmul_nt(lhs[...], table)
        out = both[0:rows] + both[rows : 2 * rows]
        for h in range(TILE // LANES):
            send_ref[t * (TILE // LANES) + h] = out[:, h * LANES : (h + 1) * LANES]
        return carry

    lax.fori_loop(0, points // TILE, body, 0, unroll=True)


def spread_rows(get, freqs, dirs, points, lhs):
    rows = lhs.shape[0] // 2
    fill = jnp.ones((STRIDE - dirs - 2, LANES), F32)
    for c in range(points // LANES):
        x = get(c)
        pieces = []
        for f in range(freqs):
            one = x[f * dirs : (f + 1) * dirs]
            pieces += [one, one[0:1], fill, one[dirs - 1 : dirs]]
        high, low = split(jnp.concatenate(pieces, axis=0))
        lhs[0:rows, c * LANES : (c + 1) * LANES] = high
        lhs[rows : 2 * rows, c * LANES : (c + 1) * LANES] = low


def place_kernel(freqs, dirs, blocks, recv_ref, field_ref, first_ref, second_ref, cell_ref, lhs):
    points = cell_ref.shape[1]
    rows = freqs * STRIDE
    label = freqs * dirs
    for c in range(points // LANES):
        cell_ref[:, c * LANES : (c + 1) * LANES] = (
            recv_ref[c, label : label + 1, :].astype(jnp.int32) - 1
        )
    spread_rows(lambda c: recv_ref[c], freqs, dirs, points, lhs)
    cells = cell_ref[...]

    def body(t, carry):
        table = one_hot(cells, t * TILE, points)
        both = matmul_nt(lhs[...], table)
        where = pl.ds(pl.multiple_of(t * TILE, TILE), TILE)
        field_ref[:, where] = both[0:rows] + both[rows : 2 * rows]
        return carry

    lax.fori_loop(0, points // TILE, body, 0, unroll=True)
    half = dirs // 2
    width = half + 1
    last = points - NLON

    def edge(out_ref, near, far, skip):
        at = 0
        for start, extra in ((near, 0), (far, 1)):
            for f in range(freqs):
                low = f * STRIDE + skip + extra
                high = f * STRIDE + skip + width - extra
                out_ref[at : at + high - low, :] = field_ref[low:high, start : start + NLON]
                at += high - low
        mask = field_ref[dirs + 1 : dirs + 2, near : near + NLON]
        out_ref[at:, :] = jnp.broadcast_to(mask, (out_ref.shape[0] - at, NLON))

    even = lax.rem(snake(lax.axis_index("blk"), blocks), 2) == 0

    @pl.when(even)
    def _():
        edge(first_ref, last, last - NLON, 0)
        edge(second_ref, 0, NLON, half)

    @pl.when(jnp.logical_not(even))
    def _():
        edge(second_ref, last, last - NLON, 0)
        edge(first_ref, 0, NLON, half)


def roll_lanes(x, shift):
    return pltpu.roll(x, shift % x.shape[1], 1)


def step_kernel(
    freqs, dirs, blocks, field_ref, first_ref, second_ref, cell_ref, back_ref, ext, mid, ends, lhs
):
    points = field_ref.shape[1]
    rows = freqs * STRIDE
    row_count = points // NLON
    half = dirs // 2
    width = half + 1
    ghost = SUBSTEPS
    band = snake(lax.axis_index("blk"), blocks)
    rows_all = row_count * blocks

    def lanes(row):
        return slice(row * NLON, (row + 1) * NLON)

    ext[:, 0 : ghost * NLON] = jnp.zeros((rows, ghost * NLON), F32)
    ext[:, (ghost + row_count) * NLON :] = jnp.zeros((rows, ghost * NLON), F32)
    ext[:, ghost * NLON : (ghost + row_count) * NLON] = field_ref[...]

    def fill(in_ref, near, far, skip, end):
        at = 0
        for row, extra in ((near, 0), (far, 1)):
            for f in range(freqs):
                low = f * STRIDE + skip + extra
                high = f * STRIDE + skip + width - extra
                ext[low:high, lanes(row)] = in_ref[at : at + high - low, :]
                at += high - low
        if skip:
            for f in range(freqs):
                spot = f * width + dirs - 1 - half
                top = (f + 1) * STRIDE
                ext[top - 1 : top, lanes(near)] = in_ref[spot : spot + 1, :]
        ends[end : end + 1, :] = in_ref[at : at + 1, :]

    even = lax.rem(band, 2) == 0

    @pl.when(even)
    def _():
        fill(second_ref, ghost - 1, ghost - 2, 0, 0)
        fill(first_ref, ghost + row_count, ghost + row_count + 1, half, 1)

    @pl.when(jnp.logical_not(even))
    def _():
        fill(first_ref, ghost - 1, ghost - 2, 0, 0)
        fill(second_ref, ghost + row_count, ghost + row_count + 1, half, 1)

    def sea_of(row):
        if row < 0:
            return ends[0:1, :]
        if row >= row_count:
            return ends[1:2, :]
        return field_ref[dirs + 1 : dirs + 2, lanes(row)]

    j = lax.broadcasted_iota(jnp.int32, (STRIDE, LANES), 0)
    j = jnp.where(j < dirs, j, jnp.where(j < STRIDE - 1, j - dirs, dirs - 1))
    angles = (2.0 * math.pi / dirs) * j.astype(F32)
    sin_a = jnp.where((j == 0) | (j == half), 0.0, jnp.sin(angles))
    cos_a = jnp.cos(angles)
    from_south = (sin_a > 0.0)[:, 0:1]
    from_west = (cos_a > 0.0)[:, 0:1]
    cy_base = 0.5 * jnp.abs(sin_a)
    cx_base = 0.25 * jnp.abs(cos_a)

    def advance(src, dst, first, last, shift):
        for row in range(first, last):
            spot = (band * row_count + row).astype(F32) + 0.5
            lat = jnp.full((STRIDE, LANES), spot / rows_all * (2.0 * math.pi / 3.0) - math.pi / 3.0)
            sec = 1.0 / jnp.cos(lat)
            tan = jnp.sin(lat) * sec
            turn = -0.3 * cos_a * tan
            from_lower = (turn > 0.0)[:, 0:1]
            sea = sea_of(row)
            for f in range(freqs):
                speed = 1.0 / (1.0 + 0.25 * f)
                cy = (speed * cy_base)[:, 0:1]
                cx = (speed * cx_base * sec)[:, 0:1]
                ct = (speed * jnp.abs(turn))[:, 0:1]
                piece = slice(f * STRIDE, (f + 1) * STRIDE)
                x = src[piece, lanes(row + shift)]
                meridional = jnp.where(
                    from_south, src[piece, lanes(row + shift - 1)], src[piece, lanes(row + shift + 1)]
                )
                zonal = jnp.where(from_west, roll_lanes(x, 1), roll_lanes(x, -1))
                adv = (x - cy * (x - meridional) - cx * (x - zonal)) * sea
                lower = pltpu.roll(adv, 1, 0)
                upper = pltpu.roll(adv, STRIDE - 1, 0)
                out = (adv - ct * (adv - jnp.where(from_lower, lower, upper))) * sea
                dst(f, row, out)

    def keep(f, row, out):
        out = jnp.concatenate(
            [out[0:dirs], out[0:1], out[dirs + 1 : STRIDE - 1], out[dirs - 1 : dirs]], axis=0
        )
        mid[f * STRIDE : (f + 1) * STRIDE, lanes(row + 1)] = out

    def last(f, row, out):
        high, low = split(out)
        lhs[f * STRIDE : (f + 1) * STRIDE, lanes(row)] = high
        lhs[rows + f * STRIDE : rows + (f + 1) * STRIDE, lanes(row)] = low

    advance(ext, keep, -1, row_count + 1, ghost)
    advance(mid, last, 0, row_count, 1)

    def body(t, carry):
        where = pl.ds(pl.multiple_of(t * TILE, TILE), TILE)
        cells = cell_ref[:, where]
        table = jnp.concatenate(
            [one_hot(cells, k * TILE, TILE) for k in range(points // TILE)], axis=0
        )
        both = jnp.dot(lhs[...], table, preferred_element_type=F32)
        out = both[0:rows] + both[rows : 2 * rows]
        for h in range(TILE // LANES):
            for q in range(freqs * dirs // 4):
                low = q // (dirs // 4) * STRIDE + q % (dirs // 4) * 4
                back_ref[t * (TILE // LANES) + h, q] = out[
                    low : low + 4, h * LANES : (h + 1) * LANES
                ]
        return carry

    lax.fori_loop(0, points // TILE, body, 0, unroll=True)


def pick_kernel(freqs, dirs, recv_ref, pos_ref, out_ref, result, lhs, sems):
    points = pos_ref.shape[1]
    rows = freqs * STRIDE
    spread_rows(
        lambda c: jnp.concatenate([recv_ref[c, q] for q in range(freqs * dirs // 4)], axis=0),
        freqs,
        dirs,
        points,
        lhs,
    )
    parts = []

    def body(t):
        where = slice(t * TILE, (t + 1) * TILE)
        wanted = pos_ref[:, where]
        table = jnp.concatenate(
            [one_hot(wanted, k * TILE, TILE) for k in range(points // TILE)], axis=0
        )
        both = jnp.dot(lhs[...], table, preferred_element_type=F32)
        out = both[0:rows] + both[rows : 2 * rows]
        for f in range(freqs):
            result[f, :, where] = out[f * STRIDE : f * STRIDE + dirs]
        part = pltpu.make_async_copy(
            result.at[:, :, where], out_ref.at[:, :, where], sems.at[t]
        )
        part.start()
        parts.append(part)

    for t in range(points // TILE):
        body(t)
    for part in parts:
        part.wait()


def exchange(x, blocks, cap):
    if cap == LANES:
        return lax.all_to_all(x, "blk", split_axis=0, concat_axis=0, tiled=True)
    pieces, lanes = x.shape[0], x.shape[-1]
    inner = x.shape[1:-1]
    x = jnp.moveaxis(x, 0, -2).reshape(*inner, blocks, cap)
    dim = len(inner)
    x = lax.all_to_all(x, "blk", split_axis=dim, concat_axis=dim, tiled=True)
    return jnp.moveaxis(x.reshape(*inner, pieces, lanes), -2, 0)


def per_device(spectrum, wind_vector, dest_cell, counts, sea_mask, dia_shift):
    blocks = lax.axis_size("blk")
    freqs, dirs, points = spectrum.shape
    cap = points // blocks
    pieces = points // LANES
    rows = freqs * STRIDE
    send_rows = -(-(freqs * dirs + 1) // 8) * 8
    edge_rows = -(-(2 * freqs * (dirs // 2) + 1) // 8) * 8
    vmem = pl.BlockSpec(memory_space=pltpu.VMEM)
    hbm = pl.BlockSpec(memory_space=pltpu.HBM)
    params = pltpu.CompilerParams(vmem_limit_bytes=VMEM_LIMIT)

    def arr(shape, dtype=F32):
        return jax.ShapeDtypeStruct(shape, dtype)

    send, position = pl.pallas_call(
        functools.partial(source_kernel, blocks, cap),
        out_shape=(arr((pieces, send_rows, LANES)), arr((1, points), jnp.int32)),
        in_specs=[hbm] * 5,
        out_specs=(vmem, vmem),
        scratch_shapes=[
            pltpu.SMEM(dia_shift.shape, jnp.int32),
            pltpu.SMEM(counts.shape, jnp.int32),
            pltpu.VMEM(spectrum.shape, F32),
            pltpu.VMEM(wind_vector.shape, F32),
            pltpu.VMEM((1, points), jnp.int32),
            pltpu.VMEM((freqs, 2 * dirs, points), F32),
            pltpu.VMEM((2 * send_rows, points), BF16),
            pltpu.SemaphoreType.DMA((5,)),
        ],
        compiler_params=pltpu.CompilerParams(vmem_limit_bytes=SOURCE_LIMIT),
        name="source",
    )(dia_shift, counts, spectrum, wind_vector, dest_cell.reshape(1, points))
    arrived = exchange(send, blocks, cap)
    field, first, second, cells = pl.pallas_call(
        functools.partial(place_kernel, freqs, dirs, blocks),
        out_shape=(
            arr((rows, points)),
            arr((edge_rows, NLON)),
            arr((edge_rows, NLON)),
            arr((1, points), jnp.int32),
        ),
        in_specs=[vmem],
        out_specs=(vmem, vmem, vmem, vmem),
        scratch_shapes=[pltpu.VMEM((2 * rows, points), BF16)],
        compiler_params=params,
        name="place",
    )(arrived)
    inner, outer = halo_swaps(blocks)
    mine, theirs = lax.ppermute(first, "blk", inner), lax.ppermute(second, "blk", outer)
    back = pl.pallas_call(
        functools.partial(step_kernel, freqs, dirs, blocks),
        out_shape=arr((pieces, freqs * dirs // 4, 4, LANES)),
        in_specs=[vmem] * 4,
        out_specs=vmem,
        scratch_shapes=[
            pltpu.VMEM((rows, points + 2 * SUBSTEPS * NLON), F32),
            pltpu.VMEM((rows, points + 2 * NLON), F32),
            pltpu.VMEM((8, NLON), F32),
            pltpu.VMEM((2 * rows, points), BF16),
        ],
        compiler_params=params,
        name="step",
    )(field, mine, theirs, cells)
    returned = exchange(back, blocks, cap)
    return pl.pallas_call(
        functools.partial(pick_kernel, freqs, dirs),
        out_shape=arr((freqs, dirs, points)),
        in_specs=[vmem, vmem],
        out_specs=hbm,
        scratch_shapes=[
            pltpu.VMEM((freqs, dirs, points), F32),
            pltpu.VMEM((2 * rows, points), BF16),
            pltpu.SemaphoreType.DMA((points // TILE,)),
        ],
        compiler_params=params,
        name="pick",
    )(returned, position)


def solution(mesh):
    placed = (
        P(None, None, ("groups", "blk")),
        P(None, ("groups", "blk")),
        P(("groups", "blk")),
        P(("groups", "blk")),
        P(("groups", "blk")),
        P(),
    )
    return jax.shard_map(
        per_device,
        mesh=mesh,
        in_specs=placed,
        out_specs=P(None, None, ("groups", "blk")),
        check_vma=False,
    )
```

```python
import functools
import math

import jax
import jax.numpy as jnp
from jax import lax
from jax.experimental import pallas as pl
from jax.experimental.pallas import tpu as pltpu
from jax.sharding import PartitionSpec as P

NLON = 512
SUBSTEPS = 2
LANES = 128
TILE = 256
GROUP = 512
STRIDE = 40
F32 = jnp.float32
BF16 = jnp.bfloat16
VMEM_LIMIT = 40 * 1024 * 1024
SOURCE_LIMIT = 60 * 1024 * 1024


def snake_row(blocks):
    chips = max(blocks // 2, 1)
    return 1 << ((chips.bit_length() - 1) // 2)


def snake(index, blocks):
    row = snake_row(blocks)
    if blocks % (2 * row):
        return index
    core = lax.rem(index, 2)
    chip = lax.div(index, 2)
    line = lax.div(chip, row)
    place = lax.rem(chip, row)
    place = jnp.where(lax.rem(line, 2) == 1, row - 1 - place, place)
    return (line * row + place) * 2 + core


def halo_swaps(blocks):
    row = snake_row(blocks)
    order = []
    for band in range(blocks):
        if blocks % (2 * row):
            order.append(band)
            continue
        core, chip = band % 2, band // 2
        line, place = chip // row, chip % row
        if line % 2:
            place = row - 1 - place
        order.append((line * row + place) * 2 + core)

    def swaps(first):
        pairs = []
        for band in range(first, blocks - 1, 2):
            low, high = order[band], order[band + 1]
            pairs += [(low, high), (high, low)]
        return pairs

    return swaps(0), swaps(1)


def split(x):
    high = x.astype(BF16)
    return high, (x - high.astype(F32)).astype(BF16)


def one_hot(row, start, width):
    ids = lax.broadcasted_iota(jnp.int32, (TILE, width), 0).astype(F32).astype(BF16)
    wanted = (row - start).astype(F32).astype(BF16)
    return jnp.where(ids == wanted, jnp.ones((), BF16), jnp.zeros((), BF16))


def matmul_nt(data, table):
    return lax.dot_general(
        data, table, (((1,), (1,)), ((), ())), preferred_element_type=F32
    )


def direction_trig(dirs, rows):
    j = lax.broadcasted_iota(jnp.int32, (rows, LANES), 0)
    angles = (2.0 * math.pi / dirs) * j.astype(F32)
    return jnp.cos(angles), jnp.sin(angles)


def source_kernel(
    blocks,
    cap,
    shift_in,
    count_in,
    spec_in,
    wind_in,
    dest_in,
    send_ref,
    pos_ref,
    shift_ref,
    count_ref,
    spec_ref,
    wind_ref,
    dest_ref,
    dbl,
    lhs,
    sems,
):
    freqs, dirs, points = spec_ref.shape
    rows = lhs.shape[0] // 2
    pairs = (
        (dest_in, dest_ref),
        (count_in, count_ref),
        (shift_in, shift_ref),
        (wind_in, wind_ref),
        (spec_in, spec_ref),
    )
    copies = [pltpu.make_async_copy(a, b, sems.at[i]) for i, (a, b) in enumerate(pairs)]
    for copy in copies:
        copy.start()
    copies[0].wait()
    copies[1].wait()
    dest = dest_ref[...]
    slot = lax.broadcasted_iota(jnp.int32, (1, points), 1)
    live = slot < count_ref[0]
    band = lax.shift_right_logical(dest, points.bit_length() - 1)
    band = jnp.where(live, band, -1)
    owner_band = snake(lax.broadcasted_iota(jnp.int32, (blocks, 1), 0), blocks)
    hits = (band == owner_band).astype(F32)
    tri_r = lax.broadcasted_iota(jnp.int32, (LANES, LANES), 0)
    tri_c = lax.broadcasted_iota(jnp.int32, (LANES, LANES), 1)
    upper = (tri_r <= tri_c).astype(F32).astype(BF16)
    ones = jnp.ones((LANES, LANES), BF16)
    base = (lax.broadcasted_iota(jnp.int32, (blocks, LANES), 0) * cap).astype(F32)
    for c in range(points // LANES):
        piece = hits[:, c * LANES : (c + 1) * LANES]
        packed = piece.astype(BF16)
        running = jnp.dot(packed, upper, preferred_element_type=F32) + base
        base = base + jnp.dot(packed, ones, preferred_element_type=F32)
        where_to = jnp.sum(piece * running, axis=0, keepdims=True) - 1.0
        pos_ref[:, c * LANES : (c + 1) * LANES] = where_to.astype(jnp.int32)
    for copy in copies[2:]:
        copy.wait()
    cos_a, sin_a = direction_trig(dirs, dirs)
    span = -(-(dirs + dirs // 4) // 8) * 8
    offset = 2 * dirs - span
    extra = rows - freqs * dirs

    def terms(c):
        where = slice(c * LANES, (c + 1) * LANES)
        total = jnp.zeros((1, LANES), F32)
        for f in range(freqs):
            x = spec_ref[f, :, where]
            dbl[f, 0:dirs, where] = x
            dbl[f, dirs : 2 * dirs, where] = x
            total = total + jnp.sum(x, axis=0, keepdims=True)
        mean = total * (1.0 / (freqs * dirs))
        along = wind_ref[0:1, where] * cos_a + wind_ref[1:2, where] * sin_a
        drive = jnp.maximum(along - 0.3, 0.0)
        pieces = []
        for f in range(freqs):
            x = spec_ref[f, :, where]
            ahead = pltpu.roll(dbl[f, 0:span, where], span - shift_ref[0], 0)[0:dirs]
            behind = pltpu.roll(
                dbl[f, offset:, where], shift_ref[1] + span - (dirs - offset), 0
            )[0:dirs]
            pieces.append(
                x * jnp.exp((0.15 + 0.05 * f) * drive - (0.2 + 0.1 * f) * mean)
                + 0.1 * (ahead * behind - x * x)
            )
        local = (lax.bitwise_and(dest_ref[:, where], points - 1) + 1).astype(F32)
        pieces.append(jnp.broadcast_to(local, (extra, LANES)))
        high, low = split(jnp.concatenate(pieces, axis=0))
        lhs[0:rows, where] = high
        lhs[rows : 2 * rows, where] = low

    per_step = TILE // LANES

    def place(t, g):
        where = slice(g * GROUP, (g + 1) * GROUP)
        both = matmul_nt(lhs[:, where], one_hot(pos_ref[:, where], t * TILE, GROUP))
        out = both[0:rows] + both[rows : 2 * rows]
        for h in range(per_step):
            piece = out[:, h * LANES : (h + 1) * LANES]
            if g:
                piece = send_ref[t * per_step + h] + piece
            send_ref[t * per_step + h] = piece

    groups = points // GROUP
    chunks = GROUP // LANES
    steps = points // TILE
    for g in range(groups + 1):
        for c in range(chunks):
            if g < groups:
                terms(g * chunks + c)
            if g > 0:
                for t in range(c * steps // chunks, (c + 1) * steps // chunks):
                    place(t, g - 1)


def spread_rows(get, freqs, dirs, points, lhs):
    rows = lhs.shape[0] // 2
    fill = jnp.ones((STRIDE - dirs - 2, LANES), F32)
    for c in range(points // LANES):
        x = get(c)
        pieces = []
        for f in range(freqs):
            one = x[f * dirs : (f + 1) * dirs]
            pieces += [one, one[0:1], fill, one[dirs - 1 : dirs]]
        high, low = split(jnp.concatenate(pieces, axis=0))
        lhs[0:rows, c * LANES : (c + 1) * LANES] = high
        lhs[rows : 2 * rows, c * LANES : (c + 1) * LANES] = low


def place_kernel(freqs, dirs, blocks, recv_ref, field_ref, first_ref, second_ref, cell_ref, lhs):
    points = cell_ref.shape[1]
    rows = freqs * STRIDE
    label = freqs * dirs
    for c in range(points // LANES):
        cell_ref[:, c * LANES : (c + 1) * LANES] = (
            recv_ref[c, label : label + 1, :].astype(jnp.int32) - 1
        )
    spread_rows(lambda c: recv_ref[c], freqs, dirs, points, lhs)
    cells = cell_ref[...]

    def body(t, carry):
        table = one_hot(cells, t * TILE, points)
        both = matmul_nt(lhs[...], table)
        where = pl.ds(pl.multiple_of(t * TILE, TILE), TILE)
        field_ref[:, where] = both[0:rows] + both[rows : 2 * rows]
        return carry

    lax.fori_loop(0, points // TILE, body, 0, unroll=True)
    half = dirs // 2
    width = half + 1
    last = points - NLON

    def edge(out_ref, near, far, skip):
        at = 0
        for start, extra in ((near, 0), (far, 1)):
            for f in range(freqs):
                low = f * STRIDE + skip + extra
                high = f * STRIDE + skip + width - extra
                out_ref[at : at + high - low, :] = field_ref[low:high, start : start + NLON]
                at += high - low
        mask = field_ref[dirs + 1 : dirs + 2, near : near + NLON]
        out_ref[at:, :] = jnp.broadcast_to(mask, (out_ref.shape[0] - at, NLON))

    even = lax.rem(snake(lax.axis_index("blk"), blocks), 2) == 0

    @pl.when(even)
    def _():
        edge(first_ref, last, last - NLON, 0)
        edge(second_ref, 0, NLON, half)

    @pl.when(jnp.logical_not(even))
    def _():
        edge(second_ref, last, last - NLON, 0)
        edge(first_ref, 0, NLON, half)


def roll_lanes(x, shift):
    return pltpu.roll(x, shift % x.shape[1], 1)


def step_kernel(
    freqs, dirs, blocks, field_ref, first_ref, second_ref, cell_ref, back_ref, ext, mid, ends, acc, lhs
):
    points = field_ref.shape[1]
    rows = freqs * STRIDE
    row_count = points // NLON
    half = dirs // 2
    width = half + 1
    ghost = SUBSTEPS
    band = snake(lax.axis_index("blk"), blocks)
    rows_all = row_count * blocks

    def lanes(row):
        return slice(row * NLON, (row + 1) * NLON)

    ext[:, 0 : ghost * NLON] = jnp.zeros((rows, ghost * NLON), F32)
    ext[:, (ghost + row_count) * NLON :] = jnp.zeros((rows, ghost * NLON), F32)
    ext[:, ghost * NLON : (ghost + row_count) * NLON] = field_ref[...]

    def fill(in_ref, near, far, skip, end):
        at = 0
        for row, extra in ((near, 0), (far, 1)):
            for f in range(freqs):
                low = f * STRIDE + skip + extra
                high = f * STRIDE + skip + width - extra
                ext[low:high, lanes(row)] = in_ref[at : at + high - low, :]
                at += high - low
        if skip:
            for f in range(freqs):
                spot = f * width + dirs - 1 - half
                top = (f + 1) * STRIDE
                ext[top - 1 : top, lanes(near)] = in_ref[spot : spot + 1, :]
        ends[end : end + 1, :] = in_ref[at : at + 1, :]

    even = lax.rem(band, 2) == 0

    @pl.when(even)
    def _():
        fill(second_ref, ghost - 1, ghost - 2, 0, 0)
        fill(first_ref, ghost + row_count, ghost + row_count + 1, half, 1)

    @pl.when(jnp.logical_not(even))
    def _():
        fill(first_ref, ghost - 1, ghost - 2, 0, 0)
        fill(second_ref, ghost + row_count, ghost + row_count + 1, half, 1)

    def sea_of(row):
        if row < 0:
            return ends[0:1, :]
        if row >= row_count:
            return ends[1:2, :]
        return field_ref[dirs + 1 : dirs + 2, lanes(row)]

    j = lax.broadcasted_iota(jnp.int32, (STRIDE, LANES), 0)
    j = jnp.where(j < dirs, j, jnp.where(j < STRIDE - 1, j - dirs, dirs - 1))
    angles = (2.0 * math.pi / dirs) * j.astype(F32)
    sin_a = jnp.where((j == 0) | (j == half), 0.0, jnp.sin(angles))
    cos_a = jnp.cos(angles)
    from_south = (sin_a > 0.0)[:, 0:1]
    from_west = (cos_a > 0.0)[:, 0:1]
    cy_base = 0.5 * jnp.abs(sin_a)
    cx_base = 0.25 * jnp.abs(cos_a)

    def advance(src, dst, row, f, shift):
        spot = (band * row_count + row).astype(F32) + 0.5
        lat = jnp.full((STRIDE, LANES), spot / rows_all * (2.0 * math.pi / 3.0) - math.pi / 3.0)
        sec = 1.0 / jnp.cos(lat)
        tan = jnp.sin(lat) * sec
        turn = -0.3 * cos_a * tan
        from_lower = (turn > 0.0)[:, 0:1]
        sea = sea_of(row)
        speed = 1.0 / (1.0 + 0.25 * f)
        cy = (speed * cy_base)[:, 0:1]
        cx = (speed * cx_base * sec)[:, 0:1]
        ct = (speed * jnp.abs(turn))[:, 0:1]
        piece = slice(f * STRIDE, (f + 1) * STRIDE)
        x = src[piece, lanes(row + shift)]
        meridional = jnp.where(
            from_south, src[piece, lanes(row + shift - 1)], src[piece, lanes(row + shift + 1)]
        )
        zonal = jnp.where(from_west, roll_lanes(x, 1), roll_lanes(x, -1))
        adv = (x - cy * (x - meridional) - cx * (x - zonal)) * sea
        lower = pltpu.roll(adv, 1, 0)
        upper = pltpu.roll(adv, STRIDE - 1, 0)
        dst(f, row, (adv - ct * (adv - jnp.where(from_lower, lower, upper))) * sea)

    def keep(f, row, out):
        out = jnp.concatenate(
            [out[0:dirs], out[0:1], out[dirs + 1 : STRIDE - 1], out[dirs - 1 : dirs]], axis=0
        )
        mid[f * STRIDE : (f + 1) * STRIDE, lanes(row + 1)] = out

    def last(f, row, out):
        high, low = split(out)
        lhs[f * STRIDE : (f + 1) * STRIDE, lanes(row)] = high
        lhs[rows + f * STRIDE : rows + (f + 1) * STRIDE, lanes(row)] = low

    def pick(t, row):
        where = slice(t * TILE, (t + 1) * TILE)
        cells = cell_ref[:, where]
        table = jnp.concatenate(
            [one_hot(cells, row * NLON + k * TILE, TILE) for k in range(NLON // TILE)], axis=0
        )
        both = jnp.dot(lhs[:, lanes(row)], table, preferred_element_type=F32)
        out = both[0:rows] + both[rows : 2 * rows]
        if row:
            out = acc[:, where] + out
        if row < row_count - 1:
            acc[:, where] = out
            return
        for h in range(TILE // LANES):
            for q in range(freqs * dirs // 4):
                low = q // (dirs // 4) * STRIDE + q % (dirs // 4) * 4
                back_ref[t * (TILE // LANES) + h, q] = out[
                    low : low + 4, h * LANES : (h + 1) * LANES
                ]

    steps = points // TILE
    for row in range(-1, 1):
        for f in range(freqs):
            advance(ext, keep, row, f, ghost)
    for row in range(row_count + 1):
        for f in range(freqs):
            if row < row_count:
                advance(ext, keep, row + 1, f, ghost)
                advance(mid, last, row, f, 1)
            if row:
                for t in range(f * steps // freqs, (f + 1) * steps // freqs):
                    pick(t, row - 1)


def pick_kernel(freqs, dirs, recv_ref, pos_ref, out_ref, result, lhs, sems):
    points = pos_ref.shape[1]
    rows = freqs * STRIDE
    spread_rows(
        lambda c: jnp.concatenate([recv_ref[c, q] for q in range(freqs * dirs // 4)], axis=0),
        freqs,
        dirs,
        points,
        lhs,
    )
    parts = []

    def body(t):
        where = slice(t * TILE, (t + 1) * TILE)
        wanted = pos_ref[:, where]
        table = jnp.concatenate(
            [one_hot(wanted, k * TILE, TILE) for k in range(points // TILE)], axis=0
        )
        both = jnp.dot(lhs[...], table, preferred_element_type=F32)
        out = both[0:rows] + both[rows : 2 * rows]
        for f in range(freqs):
            result[f, :, where] = out[f * STRIDE : f * STRIDE + dirs]
        part = pltpu.make_async_copy(
            result.at[:, :, where], out_ref.at[:, :, where], sems.at[t]
        )
        part.start()
        parts.append(part)

    for t in range(points // TILE):
        body(t)
    for part in parts:
        part.wait()


def exchange(x, blocks, cap):
    if cap == LANES:
        return lax.all_to_all(x, "blk", split_axis=0, concat_axis=0, tiled=True)
    pieces, lanes = x.shape[0], x.shape[-1]
    inner = x.shape[1:-1]
    x = jnp.moveaxis(x, 0, -2).reshape(*inner, blocks, cap)
    dim = len(inner)
    x = lax.all_to_all(x, "blk", split_axis=dim, concat_axis=dim, tiled=True)
    return jnp.moveaxis(x.reshape(*inner, pieces, lanes), -2, 0)


def per_device(spectrum, wind_vector, dest_cell, counts, sea_mask, dia_shift):
    blocks = lax.axis_size("blk")
    freqs, dirs, points = spectrum.shape
    cap = points // blocks
    pieces = points // LANES
    rows = freqs * STRIDE
    send_rows = -(-(freqs * dirs + 1) // 8) * 8
    edge_rows = -(-(2 * freqs * (dirs // 2) + 1) // 8) * 8
    vmem = pl.BlockSpec(memory_space=pltpu.VMEM)
    hbm = pl.BlockSpec(memory_space=pltpu.HBM)
    params = pltpu.CompilerParams(vmem_limit_bytes=VMEM_LIMIT)

    def arr(shape, dtype=F32):
        return jax.ShapeDtypeStruct(shape, dtype)

    send, position = pl.pallas_call(
        functools.partial(source_kernel, blocks, cap),
        out_shape=(arr((pieces, send_rows, LANES)), arr((1, points), jnp.int32)),
        in_specs=[hbm] * 5,
        out_specs=(vmem, vmem),
        scratch_shapes=[
            pltpu.SMEM(dia_shift.shape, jnp.int32),
            pltpu.SMEM(counts.shape, jnp.int32),
            pltpu.VMEM(spectrum.shape, F32),
            pltpu.VMEM(wind_vector.shape, F32),
            pltpu.VMEM((1, points), jnp.int32),
            pltpu.VMEM((freqs, 2 * dirs, points), F32),
            pltpu.VMEM((2 * send_rows, points), BF16),
            pltpu.SemaphoreType.DMA((5,)),
        ],
        compiler_params=pltpu.CompilerParams(vmem_limit_bytes=SOURCE_LIMIT),
        name="source",
    )(dia_shift, counts, spectrum, wind_vector, dest_cell.reshape(1, points))
    arrived = exchange(send, blocks, cap)
    field, first, second, cells = pl.pallas_call(
        functools.partial(place_kernel, freqs, dirs, blocks),
        out_shape=(
            arr((rows, points)),
            arr((edge_rows, NLON)),
            arr((edge_rows, NLON)),
            arr((1, points), jnp.int32),
        ),
        in_specs=[vmem],
        out_specs=(vmem, vmem, vmem, vmem),
        scratch_shapes=[pltpu.VMEM((2 * rows, points), BF16)],
        compiler_params=params,
        name="place",
    )(arrived)
    inner, outer = halo_swaps(blocks)
    mine, theirs = lax.ppermute(first, "blk", inner), lax.ppermute(second, "blk", outer)
    back = pl.pallas_call(
        functools.partial(step_kernel, freqs, dirs, blocks),
        out_shape=arr((pieces, freqs * dirs // 4, 4, LANES)),
        in_specs=[vmem] * 4,
        out_specs=vmem,
        scratch_shapes=[
            pltpu.VMEM((rows, points + 2 * SUBSTEPS * NLON), F32),
            pltpu.VMEM((rows, points + 2 * NLON), F32),
            pltpu.VMEM((8, NLON), F32),
            pltpu.VMEM((rows, points), F32),
            pltpu.VMEM((2 * rows, points), BF16),
        ],
        compiler_params=params,
        name="step",
    )(field, mine, theirs, cells)
    returned = exchange(back, blocks, cap)
    return pl.pallas_call(
        functools.partial(pick_kernel, freqs, dirs),
        out_shape=arr((freqs, dirs, points)),
        in_specs=[vmem, vmem],
        out_specs=hbm,
        scratch_shapes=[
            pltpu.VMEM((freqs, dirs, points), F32),
            pltpu.VMEM((2 * rows, points), BF16),
            pltpu.SemaphoreType.DMA((points // TILE,)),
        ],
        compiler_params=params,
        name="pick",
    )(returned, position)


def solution(mesh):
    placed = (
        P(None, None, ("groups", "blk")),
        P(None, ("groups", "blk")),
        P(("groups", "blk")),
        P(("groups", "blk")),
        P(("groups", "blk")),
        P(),
    )
    return jax.shard_map(
        per_device,
        mesh=mesh,
        in_specs=placed,
        out_specs=P(None, None, ("groups", "blk")),
        check_vma=False,
    )
```

```python
import functools
import math

import jax
import jax.numpy as jnp
from jax import lax
from jax.experimental import pallas as pl
from jax.experimental.pallas import tpu as pltpu
from jax.sharding import PartitionSpec as P

NLON = 512
SUBSTEPS = 2
LANES = 128
TILE = 256
GROUP = 512
STRIDE = 40
F32 = jnp.float32
BF16 = jnp.bfloat16
VMEM_LIMIT = 40 * 1024 * 1024
SOURCE_LIMIT = 60 * 1024 * 1024


def snake_row(blocks):
    chips = max(blocks // 2, 1)
    return 1 << ((chips.bit_length() - 1) // 2)


def snake(index, blocks):
    row = snake_row(blocks)
    if blocks % (2 * row):
        return index
    core = lax.rem(index, 2)
    chip = lax.div(index, 2)
    line = lax.div(chip, row)
    place = lax.rem(chip, row)
    place = jnp.where(lax.rem(line, 2) == 1, row - 1 - place, place)
    return (line * row + place) * 2 + core


def halo_swaps(blocks):
    row = snake_row(blocks)
    order = []
    for band in range(blocks):
        if blocks % (2 * row):
            order.append(band)
            continue
        core, chip = band % 2, band // 2
        line, place = chip // row, chip % row
        if line % 2:
            place = row - 1 - place
        order.append((line * row + place) * 2 + core)

    def swaps(first):
        pairs = []
        for band in range(first, blocks - 1, 2):
            low, high = order[band], order[band + 1]
            pairs += [(low, high), (high, low)]
        return pairs

    return swaps(0), swaps(1)


def split(x):
    high = x.astype(BF16)
    return high, (x - high.astype(F32)).astype(BF16)


def one_hot(row, start, width):
    ids = lax.broadcasted_iota(jnp.int32, (TILE, width), 0).astype(F32).astype(BF16)
    wanted = (row - start).astype(F32).astype(BF16)
    return jnp.where(ids == wanted, jnp.ones((), BF16), jnp.zeros((), BF16))


def matmul_nt(data, table):
    return lax.dot_general(
        data, table, (((1,), (1,)), ((), ())), preferred_element_type=F32
    )


def direction_trig(dirs, rows):
    j = lax.broadcasted_iota(jnp.int32, (rows, LANES), 0)
    angles = (2.0 * math.pi / dirs) * j.astype(F32)
    return jnp.cos(angles), jnp.sin(angles)


def shifted(x, shift, size):
    count = x.shape[0] // 8
    fine = lax.rem(shift, 8)
    back = lax.rem(8 - fine, 8)
    keep = lax.broadcasted_iota(jnp.int32, (8, LANES), 0) < 8 - fine
    tiles = [pltpu.roll(x[8 * k : 8 * k + 8], back, 0) for k in range(count)]
    near = [jnp.where(keep, a, b) for a, b in zip(tiles, tiles[1:] + tiles[-1:])]
    out = [jnp.where(shift >= 8, b, a) for a, b in zip(near, near[1:] + near[-1:])]
    return jnp.concatenate(out, axis=0)[0:size]


def source_kernel(
    blocks,
    cap,
    shift_in,
    count_in,
    spec_in,
    wind_in,
    dest_in,
    send_ref,
    pos_ref,
    shift_ref,
    count_ref,
    spec_ref,
    wind_ref,
    dest_ref,
    dbl,
    lhs,
    sems,
):
    freqs, dirs, points = spec_ref.shape
    rows = lhs.shape[0] // 2
    pairs = (
        (dest_in, dest_ref),
        (count_in, count_ref),
        (shift_in, shift_ref),
        (wind_in, wind_ref),
        (spec_in, spec_ref),
    )
    copies = [pltpu.make_async_copy(a, b, sems.at[i]) for i, (a, b) in enumerate(pairs)]
    for copy in copies:
        copy.start()
    copies[0].wait()
    copies[1].wait()
    dest = dest_ref[...]
    slot = lax.broadcasted_iota(jnp.int32, (1, points), 1)
    live = slot < count_ref[0]
    band = lax.shift_right_logical(dest, points.bit_length() - 1)
    band = jnp.where(live, band, -1)
    owner_band = snake(lax.broadcasted_iota(jnp.int32, (blocks, 1), 0), blocks)
    hits = (band == owner_band).astype(F32)
    tri_r = lax.broadcasted_iota(jnp.int32, (LANES, LANES), 0)
    tri_c = lax.broadcasted_iota(jnp.int32, (LANES, LANES), 1)
    upper = (tri_r <= tri_c).astype(F32).astype(BF16)
    ones = jnp.ones((LANES, LANES), BF16)
    base = (lax.broadcasted_iota(jnp.int32, (blocks, LANES), 0) * cap).astype(F32)
    for c in range(points // LANES):
        piece = hits[:, c * LANES : (c + 1) * LANES]
        packed = piece.astype(BF16)
        running = jnp.dot(packed, upper, preferred_element_type=F32) + base
        base = base + jnp.dot(packed, ones, preferred_element_type=F32)
        where_to = jnp.sum(piece * running, axis=0, keepdims=True) - 1.0
        pos_ref[:, c * LANES : (c + 1) * LANES] = where_to.astype(jnp.int32)
    for copy in copies[2:]:
        copy.wait()
    cos_a, sin_a = direction_trig(dirs, dirs)
    span = -(-(dirs + dirs // 4) // 8) * 8
    offset = 2 * dirs - span
    extra = rows - freqs * dirs

    def terms(c):
        where = slice(c * LANES, (c + 1) * LANES)
        total = jnp.zeros((1, LANES), F32)
        for f in range(freqs):
            x = spec_ref[f, :, where]
            dbl[f, 0:dirs, where] = x
            dbl[f, dirs : 2 * dirs, where] = x
            total = total + jnp.sum(x, axis=0, keepdims=True)
        mean = total * (1.0 / (freqs * dirs))
        along = wind_ref[0:1, where] * cos_a + wind_ref[1:2, where] * sin_a
        drive = jnp.maximum(along - 0.3, 0.0)
        pieces = []
        for f in range(freqs):
            x = spec_ref[f, :, where]
            ahead = shifted(dbl[f, 0:span, where], shift_ref[0], dirs)
            behind = shifted(dbl[f, offset:, where], dirs - offset - shift_ref[1], dirs)
            pieces.append(
                x * jnp.exp((0.15 + 0.05 * f) * drive - (0.2 + 0.1 * f) * mean)
                + 0.1 * (ahead * behind - x * x)
            )
        local = (lax.bitwise_and(dest_ref[:, where], points - 1) + 1).astype(F32)
        pieces.append(jnp.broadcast_to(local, (extra, LANES)))
        high, low = split(jnp.concatenate(pieces, axis=0))
        lhs[0:rows, where] = high
        lhs[rows : 2 * rows, where] = low

    per_step = TILE // LANES

    def place(t, g):
        where = slice(g * GROUP, (g + 1) * GROUP)
        both = matmul_nt(lhs[:, where], one_hot(pos_ref[:, where], t * TILE, GROUP))
        out = both[0:rows] + both[rows : 2 * rows]
        for h in range(per_step):
            piece = out[:, h * LANES : (h + 1) * LANES]
            if g:
                piece = send_ref[t * per_step + h] + piece
            send_ref[t * per_step + h] = piece

    groups = points // GROUP
    chunks = GROUP // LANES
    steps = points // TILE
    for g in range(groups + 1):
        for c in range(chunks):
            if g < groups:
                terms(g * chunks + c)
            if g > 0:
                for t in range(c * steps // chunks, (c + 1) * steps // chunks):
                    place(t, g - 1)


def spread_rows(get, freqs, dirs, points, lhs):
    rows = lhs.shape[0] // 2
    fill = jnp.ones((STRIDE - dirs - 2, LANES), F32)
    for c in range(points // LANES):
        x = get(c)
        pieces = []
        for f in range(freqs):
            one = x[f * dirs : (f + 1) * dirs]
            pieces += [one, one[0:1], fill, one[dirs - 1 : dirs]]
        high, low = split(jnp.concatenate(pieces, axis=0))
        lhs[0:rows, c * LANES : (c + 1) * LANES] = high
        lhs[rows : 2 * rows, c * LANES : (c + 1) * LANES] = low


def edge_kernel(
    freqs, dirs, blocks, recv_ref, first_ref, second_ref, cell_ref, south_lhs, north_lhs, wide
):
    points = cell_ref.shape[1]
    label = freqs * dirs
    half = dirs // 2
    rows = south_lhs.shape[0] // 2
    near_rows = freqs * (half + 1) + 1
    fill = jnp.ones((rows - freqs * (half + 1), LANES), F32)
    for c in range(points // LANES):
        where = slice(c * LANES, (c + 1) * LANES)
        own = recv_ref[c, label : label + 1, :].astype(jnp.int32) - 1
        cell_ref[:, where] = own
        wide[where, :] = jnp.broadcast_to(own, (LANES, LANES)).T.astype(jnp.int16)
        x = recv_ref[c]
        for lhs, start, other in ((south_lhs, 0, half), (north_lhs, half, 0)):
            pieces = []
            for f in range(freqs):
                base = f * dirs
                pieces.append(x[base + start : base + start + half])
                pieces.append(x[base + other : base + other + 1])
            high, low = split(jnp.concatenate(pieces + [fill], axis=0))
            lhs[0:rows, where] = high
            lhs[rows : 2 * rows, where] = low
    ids = lax.broadcasted_iota(jnp.int32, (1, LANES), 1)

    def side(out_ref, lhs, row, near):
        for t in range(NLON // TILE):
            start = row * NLON + t * TILE
            table = jnp.concatenate(
                [
                    jnp.where(
                        wide[...] == (ids + (start + h * LANES)).astype(jnp.int16),
                        jnp.ones((), BF16),
                        jnp.zeros((), BF16),
                    )
                    for h in range(TILE // LANES)
                ],
                axis=1,
            )
            both = jnp.dot(lhs[...], table, preferred_element_type=F32)
            out = both[0:rows] + both[rows : 2 * rows]
            where = slice(t * TILE, (t + 1) * TILE)
            if near:
                out_ref[0:near_rows, where] = out[0:near_rows]
                continue
            for f in range(freqs):
                at = near_rows + f * (half - 1)
                low = f * (half + 1) + 1
                out_ref[at : at + half - 1, where] = out[low : low + half - 1]

    top = points // NLON - 1
    even = lax.rem(snake(lax.axis_index("blk"), blocks), 2) == 0

    def sides(up_ref, down_ref):
        side(up_ref, south_lhs, top, True)
        side(up_ref, south_lhs, top - 1, False)
        side(down_ref, north_lhs, 0, True)
        side(down_ref, north_lhs, 1, False)

    @pl.when(even)
    def _():
        sides(first_ref, second_ref)

    @pl.when(jnp.logical_not(even))
    def _():
        sides(second_ref, first_ref)


def lanes(row):
    return slice(row * NLON, (row + 1) * NLON)


def stepper(freqs, dirs, blocks, row_count):
    band = snake(lax.axis_index("blk"), blocks)
    rows_all = row_count * blocks
    half = dirs // 2
    at = lax.broadcasted_iota(jnp.int32, (STRIDE, LANES), 0)
    j = jnp.where(at < dirs, at, jnp.where(at < STRIDE - 1, at - dirs, dirs - 1))
    angles = (2.0 * math.pi / dirs) * j.astype(F32)
    sin_a = jnp.where((j == 0) | (j == half), 0.0, jnp.sin(angles))
    cos_a = jnp.cos(angles)
    from_south = (at <= half)[:, 0:1]
    from_west = (cos_a > 0.0)[:, 0:1]
    cy_base = 0.5 * jnp.abs(sin_a)
    cx_base = 0.25 * jnp.abs(cos_a)

    index = [k if k < dirs else (k - dirs if k < STRIDE - 1 else dirs - 1) for k in range(STRIDE)]
    cosines = [math.cos(2.0 * math.pi * k / dirs) for k in index]

    def by_tile(low, high, values, mask, one, other):
        out = []
        for k in range(low, high, 8):
            signs = {v > 0 for v in values[k : k + 8] if abs(v) > 1e-9}
            if signs == {True}:
                out.append(one(k - low))
            elif signs == {False}:
                out.append(other(k - low))
            else:
                out.append(jnp.where(mask[k : k + 8], one(k - low), other(k - low)))
        return jnp.concatenate(out, axis=0)

    norths = [1 if k <= half else -1 for k in range(STRIDE)]
    latitudes = {}

    def latitude(row):
        if row not in latitudes:
            spot = (band * row_count + row).astype(F32) + 0.5
            lat = jnp.full((8, LANES), spot / rows_all * (2.0 * math.pi / 3.0) - math.pi / 3.0)
            sec = 1.0 / jnp.cos(lat)
            turn = -0.3 * cos_a * (jnp.sin(lat) * sec)[0:1]
            latitudes[row] = (
                (cx_base * sec[0:1])[:, 0:1],
                jnp.abs(turn)[:, 0:1],
                (turn > 0.0)[:, 0:1],
            )
        return latitudes[row]

    def advance(get, row, f, sea, low=0, high=STRIDE):
        part = slice(low, high)
        cx, ct, from_lower = latitude(row)
        speed = 1.0 / (1.0 + 0.25 * f)
        cy = (speed * cy_base)[part, 0:1]
        cx = (speed * cx)[part]
        ct = (speed * ct)[part]
        base = f * STRIDE + low
        x = get(row, slice(base, base + high - low))

        def rows_of(r):
            return lambda k: get(r, slice(base + k, base + k + 8))

        def turned_by(shift):
            return lambda k: pltpu.roll(x[k : k + 8], shift % NLON, 1)

        meridional = by_tile(low, high, norths, from_south, rows_of(row - 1), rows_of(row + 1))
        zonal = by_tile(low, high, cosines, from_west, turned_by(1), turned_by(-1))
        adv = (x - cy * (x - meridional) - cx * (x - zonal)) * sea
        lower = pltpu.roll(adv, 1, 0)
        upper = pltpu.roll(adv, high - low - 1, 0)
        return (adv - ct * (adv - jnp.where(from_lower[part], lower, upper))) * sea

    return advance


def repeat_ends(out, dirs):
    return jnp.concatenate(
        [out[0:dirs], out[0:1], out[dirs + 1 : STRIDE - 1], out[dirs - 1 : dirs]], axis=0
    )


def place_kernel(freqs, dirs, blocks, recv_ref, cell_ref, field_ref, inner_ref, lhs):
    points = cell_ref.shape[1]
    rows = freqs * STRIDE
    row_count = points // NLON
    spread_rows(lambda c: recv_ref[c], freqs, dirs, points, lhs)
    cells = cell_ref[...]
    for t in range(points // TILE):
        both = matmul_nt(lhs[...], one_hot(cells, t * TILE, points))
        field_ref[:, t * TILE : (t + 1) * TILE] = both[0:rows] + both[rows : 2 * rows]
    advance = stepper(freqs, dirs, blocks, row_count)
    for row in range(1, row_count - 1):
        sea = field_ref[dirs + 1 : dirs + 2, lanes(row)]
        for f in range(freqs):
            out = advance(lambda r, piece: field_ref[piece, lanes(r)], row, f, sea)
            inner_ref[f * STRIDE : (f + 1) * STRIDE, lanes(row - 1)] = repeat_ends(out, dirs)


def step_kernel(
    freqs,
    dirs,
    blocks,
    field_ref,
    inner_ref,
    first_ref,
    second_ref,
    cell_ref,
    back_ref,
    south,
    north,
    outer,
    acc,
    lhs,
):
    points = field_ref.shape[1]
    rows = freqs * STRIDE
    row_count = points // NLON
    half = dirs // 2
    inside = half - 1
    near_rows = freqs * (half + 1) + 1
    top = row_count - 1

    def fill(ghost, in_ref, start):
        ghost[0:rows, lanes(1)] = jnp.zeros((rows, NLON), F32)
        for f in range(freqs):
            base = f * STRIDE + start
            at = f * (half + 1)
            ghost[base : base + half + 1, lanes(0)] = in_ref[at : at + half + 1, :]
            if start:
                top_row = (f + 1) * STRIDE - 1
                ghost[top_row : top_row + 1, lanes(0)] = in_ref[at + half - 1 : at + half, :]
            at = near_rows + f * inside
            ghost[base + 1 : base + half, lanes(1)] = in_ref[at : at + inside, :]
        ghost[rows : rows + 1, lanes(0)] = in_ref[near_rows - 1 : near_rows, :]

    even = lax.rem(snake(lax.axis_index("blk"), blocks), 2) == 0

    @pl.when(even)
    def _():
        fill(south, second_ref, 0)
        fill(north, first_ref, half)

    @pl.when(jnp.logical_not(even))
    def _():
        fill(south, first_ref, 0)
        fill(north, second_ref, half)

    def sea_of(row):
        if row < 0:
            return south[rows : rows + 1, lanes(0)]
        if row > top:
            return north[rows : rows + 1, lanes(0)]
        return field_ref[dirs + 1 : dirs + 2, lanes(row)]

    def before(row, piece):
        if row < 0:
            return south[piece, lanes(-1 - row)]
        if row > top:
            return north[piece, lanes(row - top - 1)]
        return field_ref[piece, lanes(row)]

    places = {-1: 0, 0: 1, top: 2, top + 1: 3}

    def between(row, piece):
        if row in places:
            return outer[piece, lanes(places[row])]
        return inner_ref[piece, lanes(row - 1)]

    advance = stepper(freqs, dirs, blocks, row_count)
    south_high = -(-(half + 1) // 8) * 8
    north_low = half // 8 * 8

    def first_step(row, f):
        base = f * STRIDE
        where = lanes(places[row])
        if row < 0:
            out = advance(before, row, f, sea_of(row), 0, south_high)
            outer[base : base + south_high, where] = out
        elif row > top:
            out = advance(before, row, f, sea_of(row), north_low, STRIDE)
            outer[base + north_low : base + STRIDE, where] = out
            spot = dirs - 1 - north_low
            outer[base + STRIDE - 1 : base + STRIDE, where] = out[spot : spot + 1]
        else:
            out = advance(before, row, f, sea_of(row))
            outer[base : base + STRIDE, where] = repeat_ends(out, dirs)

    def second_step(row, f):
        high, low = split(advance(between, row, f, sea_of(row)))
        lhs[f * STRIDE : (f + 1) * STRIDE, lanes(row)] = high
        lhs[rows + f * STRIDE : rows + (f + 1) * STRIDE, lanes(row)] = low

    def pick(t, row):
        where = slice(t * TILE, (t + 1) * TILE)
        cells = cell_ref[:, where]
        table = jnp.concatenate(
            [one_hot(cells, row * NLON + k * TILE, TILE) for k in range(NLON // TILE)], axis=0
        )
        both = jnp.dot(lhs[:, lanes(row)], table, preferred_element_type=F32)
        out = both[0:rows] + both[rows : 2 * rows]
        if row:
            out = acc[:, where] + out
        if row < top:
            acc[:, where] = out
            return
        for h in range(TILE // LANES):
            for q in range(freqs * dirs // 4):
                low = q // (dirs // 4) * STRIDE + q % (dirs // 4) * 4
                back_ref[t * (TILE // LANES) + h, q] = out[
                    low : low + 4, h * LANES : (h + 1) * LANES
                ]

    steps = points // TILE
    for row in places:
        for f in range(freqs):
            first_step(row, f)
    for row in range(row_count + 1):
        for f in range(freqs):
            if row < row_count:
                second_step(row, f)
            if row:
                for t in range(f * steps // freqs, (f + 1) * steps // freqs):
                    pick(t, row - 1)


def pick_kernel(freqs, dirs, recv_ref, pos_ref, out_ref, result, lhs, sems):
    points = pos_ref.shape[1]
    rows = freqs * STRIDE
    spread_rows(
        lambda c: jnp.concatenate([recv_ref[c, q] for q in range(freqs * dirs // 4)], axis=0),
        freqs,
        dirs,
        points,
        lhs,
    )
    parts = []

    def body(t):
        where = slice(t * TILE, (t + 1) * TILE)
        wanted = pos_ref[:, where]
        table = jnp.concatenate(
            [one_hot(wanted, k * TILE, TILE) for k in range(points // TILE)], axis=0
        )
        both = jnp.dot(lhs[...], table, preferred_element_type=F32)
        out = both[0:rows] + both[rows : 2 * rows]
        for f in range(freqs):
            result[f, :, where] = out[f * STRIDE : f * STRIDE + dirs]
        part = pltpu.make_async_copy(
            result.at[:, :, where], out_ref.at[:, :, where], sems.at[t]
        )
        part.start()
        parts.append(part)

    for t in range(points // TILE):
        body(t)
    for part in parts:
        part.wait()


def exchange(x, blocks, cap):
    if cap == LANES:
        return lax.all_to_all(x, "blk", split_axis=0, concat_axis=0, tiled=True)
    pieces, lanes = x.shape[0], x.shape[-1]
    inner = x.shape[1:-1]
    x = jnp.moveaxis(x, 0, -2).reshape(*inner, blocks, cap)
    dim = len(inner)
    x = lax.all_to_all(x, "blk", split_axis=dim, concat_axis=dim, tiled=True)
    return jnp.moveaxis(x.reshape(*inner, pieces, lanes), -2, 0)


def per_device(spectrum, wind_vector, dest_cell, counts, sea_mask, dia_shift):
    blocks = lax.axis_size("blk")
    freqs, dirs, points = spectrum.shape
    cap = points // blocks
    pieces = points // LANES
    rows = freqs * STRIDE
    send_rows = -(-(freqs * dirs + 1) // 8) * 8
    near_rows = freqs * (dirs // 2 + 1) + 1
    far_rows = freqs * (dirs // 2 - 1)
    edge_rows = -(-(near_rows + far_rows) // 8) * 8
    edge_lhs = -(-near_rows // 8) * 8
    vmem = pl.BlockSpec(memory_space=pltpu.VMEM)
    hbm = pl.BlockSpec(memory_space=pltpu.HBM)
    params = pltpu.CompilerParams(vmem_limit_bytes=VMEM_LIMIT)

    def arr(shape, dtype=F32):
        return jax.ShapeDtypeStruct(shape, dtype)

    send, position = pl.pallas_call(
        functools.partial(source_kernel, blocks, cap),
        out_shape=(arr((pieces, send_rows, LANES)), arr((1, points), jnp.int32)),
        in_specs=[hbm] * 5,
        out_specs=(vmem, vmem),
        scratch_shapes=[
            pltpu.SMEM(dia_shift.shape, jnp.int32),
            pltpu.SMEM(counts.shape, jnp.int32),
            pltpu.VMEM(spectrum.shape, F32),
            pltpu.VMEM(wind_vector.shape, F32),
            pltpu.VMEM((1, points), jnp.int32),
            pltpu.VMEM((freqs, 2 * dirs, points), F32),
            pltpu.VMEM((2 * send_rows, points), BF16),
            pltpu.SemaphoreType.DMA((5,)),
        ],
        compiler_params=pltpu.CompilerParams(vmem_limit_bytes=SOURCE_LIMIT),
        name="source",
    )(dia_shift, counts, spectrum, wind_vector, dest_cell.reshape(1, points))
    arrived = exchange(send, blocks, cap)
    first, second, cells = pl.pallas_call(
        functools.partial(edge_kernel, freqs, dirs, blocks),
        out_shape=(
            arr((edge_rows, NLON)),
            arr((edge_rows, NLON)),
            arr((1, points), jnp.int32),
        ),
        in_specs=[vmem],
        out_specs=(vmem,) * 3,
        scratch_shapes=[
            pltpu.VMEM((2 * edge_lhs, points), BF16),
            pltpu.VMEM((2 * edge_lhs, points), BF16),
            pltpu.VMEM((points, LANES), jnp.int16),
        ],
        compiler_params=params,
        name="edges",
    )(arrived)
    inner, outer = halo_swaps(blocks)
    mine, theirs = lax.ppermute(first, "blk", inner), lax.ppermute(second, "blk", outer)
    field, middle = pl.pallas_call(
        functools.partial(place_kernel, freqs, dirs, blocks),
        out_shape=(arr((rows, points)), arr((rows, points - 2 * NLON))),
        in_specs=[vmem] * 2,
        out_specs=(vmem,) * 2,
        scratch_shapes=[pltpu.VMEM((2 * rows, points), BF16)],
        compiler_params=params,
        cost_estimate=pl.CostEstimate(
            flops=4 * rows * points * points, bytes_accessed=8 * rows * points, transcendentals=0
        ),
        name="place",
    )(arrived, cells)
    back = pl.pallas_call(
        functools.partial(step_kernel, freqs, dirs, blocks),
        out_shape=arr((pieces, freqs * dirs // 4, 4, LANES)),
        in_specs=[vmem] * 5,
        out_specs=vmem,
        scratch_shapes=[
            pltpu.VMEM((rows + 8, 2 * NLON), F32),
            pltpu.VMEM((rows + 8, 2 * NLON), F32),
            pltpu.VMEM((rows, 4 * NLON), F32),
            pltpu.VMEM((rows, points), F32),
            pltpu.VMEM((2 * rows, points), BF16),
        ],
        compiler_params=params,
        name="step",
    )(field, middle, mine, theirs, cells)
    returned = exchange(back, blocks, cap)
    return pl.pallas_call(
        functools.partial(pick_kernel, freqs, dirs),
        out_shape=arr((freqs, dirs, points)),
        in_specs=[vmem, vmem],
        out_specs=hbm,
        scratch_shapes=[
            pltpu.VMEM((freqs, dirs, points), F32),
            pltpu.VMEM((2 * rows, points), BF16),
            pltpu.SemaphoreType.DMA((points // TILE,)),
        ],
        compiler_params=params,
        name="pick",
    )(returned, position)


def solution(mesh):
    placed = (
        P(None, None, ("groups", "blk")),
        P(None, ("groups", "blk")),
        P(("groups", "blk")),
        P(("groups", "blk")),
        P(("groups", "blk")),
        P(),
    )
    return jax.shard_map(
        per_device,
        mesh=mesh,
        in_specs=placed,
        out_specs=P(None, None, ("groups", "blk")),
        check_vma=False,
    )
```

```python
import functools
import math

import jax
import jax.numpy as jnp
from jax import lax
from jax.experimental import pallas as pl
from jax.experimental.pallas import tpu as pltpu
from jax.sharding import PartitionSpec as P

NLON = 512
SUBSTEPS = 2
LANES = 128
TILE = 256
GROUP = 512
STRIDE = 40
F32 = jnp.float32
BF16 = jnp.bfloat16
VMEM_LIMIT = 40 * 1024 * 1024
SOURCE_LIMIT = 60 * 1024 * 1024


def snake_row(blocks):
    chips = max(blocks // 2, 1)
    return 1 << ((chips.bit_length() - 1) // 2)


def snake(index, blocks):
    row = snake_row(blocks)
    if blocks % (2 * row):
        return index
    core = lax.rem(index, 2)
    chip = lax.div(index, 2)
    line = lax.div(chip, row)
    place = lax.rem(chip, row)
    place = jnp.where(lax.rem(line, 2) == 1, row - 1 - place, place)
    return (line * row + place) * 2 + core


def halo_swaps(blocks):
    row = snake_row(blocks)
    order = []
    for band in range(blocks):
        if blocks % (2 * row):
            order.append(band)
            continue
        core, chip = band % 2, band // 2
        line, place = chip // row, chip % row
        if line % 2:
            place = row - 1 - place
        order.append((line * row + place) * 2 + core)

    def swaps(first):
        pairs = []
        for band in range(first, blocks - 1, 2):
            low, high = order[band], order[band + 1]
            pairs += [(low, high), (high, low)]
        return pairs

    return swaps(0), swaps(1)


def split(x):
    high = x.astype(BF16)
    return high, (x - high.astype(F32)).astype(BF16)


def one_hot(row, start, width):
    ids = lax.broadcasted_iota(jnp.int32, (TILE, width), 0).astype(F32).astype(BF16)
    wanted = (row - start).astype(F32).astype(BF16)
    return jnp.where(ids == wanted, jnp.ones((), BF16), jnp.zeros((), BF16))


def matmul_nt(data, table):
    return lax.dot_general(
        data, table, (((1,), (1,)), ((), ())), preferred_element_type=F32
    )


def direction_trig(dirs, rows):
    j = lax.broadcasted_iota(jnp.int32, (rows, LANES), 0)
    angles = (2.0 * math.pi / dirs) * j.astype(F32)
    return jnp.cos(angles), jnp.sin(angles)


def shifted(x, shift, size):
    count = x.shape[0] // 8
    fine = lax.rem(shift, 8)
    back = lax.rem(8 - fine, 8)
    keep = lax.broadcasted_iota(jnp.int32, (8, LANES), 0) < 8 - fine
    tiles = [pltpu.roll(x[8 * k : 8 * k + 8], back, 0) for k in range(count)]
    near = [jnp.where(keep, a, b) for a, b in zip(tiles, tiles[1:] + tiles[-1:])]
    out = [jnp.where(shift >= 8, b, a) for a, b in zip(near, near[1:] + near[-1:])]
    return jnp.concatenate(out, axis=0)[0:size]


def source_kernel(
    blocks,
    cap,
    shift_in,
    count_in,
    spec_in,
    wind_in,
    dest_in,
    send_ref,
    pos_ref,
    shift_ref,
    count_ref,
    spec_ref,
    wind_ref,
    dest_ref,
    dbl,
    lhs,
    sems,
):
    freqs, dirs, points = spec_ref.shape
    rows = lhs.shape[0] // 2
    pairs = (
        (dest_in, dest_ref),
        (count_in, count_ref),
        (shift_in, shift_ref),
        (wind_in, wind_ref),
        (spec_in, spec_ref),
    )
    copies = [pltpu.make_async_copy(a, b, sems.at[i]) for i, (a, b) in enumerate(pairs)]
    for copy in copies:
        copy.start()
    copies[0].wait()
    copies[1].wait()
    dest = dest_ref[...]
    slot = lax.broadcasted_iota(jnp.int32, (1, points), 1)
    live = slot < count_ref[0]
    band = lax.shift_right_logical(dest, points.bit_length() - 1)
    band = jnp.where(live, band, -1)
    owner_band = snake(lax.broadcasted_iota(jnp.int32, (blocks, 1), 0), blocks)
    hits = (band == owner_band).astype(F32)
    tri_r = lax.broadcasted_iota(jnp.int32, (LANES, LANES), 0)
    tri_c = lax.broadcasted_iota(jnp.int32, (LANES, LANES), 1)
    upper = (tri_r <= tri_c).astype(F32).astype(BF16)
    ones = jnp.ones((LANES, LANES), BF16)
    base = (lax.broadcasted_iota(jnp.int32, (blocks, LANES), 0) * cap).astype(F32)
    for c in range(points // LANES):
        piece = hits[:, c * LANES : (c + 1) * LANES]
        packed = piece.astype(BF16)
        running = jnp.dot(packed, upper, preferred_element_type=F32) + base
        base = base + jnp.dot(packed, ones, preferred_element_type=F32)
        where_to = jnp.sum(piece * running, axis=0, keepdims=True) - 1.0
        pos_ref[:, c * LANES : (c + 1) * LANES] = where_to.astype(jnp.int32)
    for copy in copies[2:]:
        copy.wait()
    cos_a, sin_a = direction_trig(dirs, dirs)
    span = -(-(dirs + dirs // 4) // 8) * 8
    offset = 2 * dirs - span
    extra = rows - freqs * dirs

    def terms(c):
        where = slice(c * LANES, (c + 1) * LANES)
        total = jnp.zeros((1, LANES), F32)
        for f in range(freqs):
            x = spec_ref[f, :, where]
            dbl[f, 0:dirs, where] = x
            dbl[f, dirs : 2 * dirs, where] = x
            total = total + jnp.sum(x, axis=0, keepdims=True)
        mean = total * (1.0 / (freqs * dirs))
        along = wind_ref[0:1, where] * cos_a + wind_ref[1:2, where] * sin_a
        drive = jnp.maximum(along - 0.3, 0.0)
        pieces = []
        for f in range(freqs):
            x = spec_ref[f, :, where]
            ahead = shifted(dbl[f, 0:span, where], shift_ref[0], dirs)
            behind = shifted(dbl[f, offset:, where], dirs - offset - shift_ref[1], dirs)
            pieces.append(
                x * jnp.exp((0.15 + 0.05 * f) * drive - (0.2 + 0.1 * f) * mean)
                + 0.1 * (ahead * behind - x * x)
            )
        local = (lax.bitwise_and(dest_ref[:, where], points - 1) + 1).astype(F32)
        pieces.append(jnp.broadcast_to(local, (extra, LANES)))
        high, low = split(jnp.concatenate(pieces, axis=0))
        lhs[0:rows, where] = high
        lhs[rows : 2 * rows, where] = low

    per_step = TILE // LANES

    def place(t, g):
        where = slice(g * GROUP, (g + 1) * GROUP)
        both = matmul_nt(lhs[:, where], one_hot(pos_ref[:, where], t * TILE, GROUP))
        out = both[0:rows] + both[rows : 2 * rows]
        for h in range(per_step):
            piece = out[:, h * LANES : (h + 1) * LANES]
            if g:
                piece = send_ref[t * per_step + h] + piece
            send_ref[t * per_step + h] = piece

    groups = points // GROUP
    chunks = GROUP // LANES
    steps = points // TILE
    for g in range(groups + 1):
        for c in range(chunks):
            if g < groups:
                terms(g * chunks + c)
            if g > 0:
                for t in range(c * steps // chunks, (c + 1) * steps // chunks):
                    place(t, g - 1)


def spread_rows(get, freqs, dirs, points, lhs):
    rows = lhs.shape[0] // 2
    fill = jnp.ones((STRIDE - dirs - 2, LANES), F32)
    for c in range(points // LANES):
        x = get(c)
        pieces = []
        for f in range(freqs):
            one = x[f * dirs : (f + 1) * dirs]
            pieces += [one, one[0:1], fill, one[dirs - 1 : dirs]]
        high, low = split(jnp.concatenate(pieces, axis=0))
        lhs[0:rows, c * LANES : (c + 1) * LANES] = high
        lhs[rows : 2 * rows, c * LANES : (c + 1) * LANES] = low


def edge_kernel(freqs, dirs, blocks, recv_ref, first_ref, second_ref, cell_ref, lhs, fold_ref, out_ref):
    points = cell_ref.shape[1]
    label = freqs * dirs
    half = dirs // 2
    rows = lhs.shape[0] // 4
    near_rows = freqs * (half + 1) + 1
    edge = 2 * NLON
    fill = jnp.ones((rows - freqs * (half + 1), LANES), F32)
    for c in range(points // LANES):
        where = slice(c * LANES, (c + 1) * LANES)
        own = recv_ref[c, label : label + 1, :].astype(jnp.int32) - 1
        cell_ref[:, where] = own
        upper = own >= points - edge
        lower = (own >= 0) & (own < edge)
        fold_ref[:, where] = jnp.where(upper, own - (points - edge), jnp.where(lower, own, -1))
        x = recv_ref[c]
        for side, start, other, mine in ((0, 0, half, upper), (1, half, 0, lower)):
            pieces = []
            for f in range(freqs):
                base = f * dirs
                pieces.append(x[base + start : base + start + half])
                pieces.append(x[base + other : base + other + 1])
            high, low = split(jnp.where(mine, jnp.concatenate(pieces + [fill], axis=0), 0.0))
            lhs[side * rows : (side + 1) * rows, where] = high
            lhs[(2 + side) * rows : (3 + side) * rows, where] = low
    cells = fold_ref[...]
    even = lax.rem(snake(lax.axis_index("blk"), blocks), 2) == 0

    def keep(edge_ref, out, t, near):
        where = slice(t * TILE % NLON, t * TILE % NLON + TILE)
        if near:
            edge_ref[0:near_rows, where] = out[0:near_rows]
            return
        for f in range(freqs):
            at = near_rows + f * (half - 1)
            low = f * (half + 1) + 1
            edge_ref[at : at + half - 1, where] = out[low : low + half - 1]

    for t in range(edge // TILE):
        both = matmul_nt(lhs[...], one_hot(cells, t * TILE, points))
        out_ref[:, t * TILE : (t + 1) * TILE] = both[0 : 2 * rows] + both[2 * rows : 4 * rows]

    def store(up_ref, down_ref):
        for t in range(edge // TILE):
            out = out_ref[:, t * TILE : (t + 1) * TILE]
            second_row = t * TILE >= NLON
            keep(up_ref, out[0:rows], t, second_row)
            keep(down_ref, out[rows : 2 * rows], t, not second_row)

    @pl.when(even)
    def _():
        store(first_ref, second_ref)

    @pl.when(jnp.logical_not(even))
    def _():
        store(second_ref, first_ref)


def lanes(row):
    return slice(row * NLON, (row + 1) * NLON)


def stepper(freqs, dirs, blocks, row_count):
    band = snake(lax.axis_index("blk"), blocks)
    rows_all = row_count * blocks
    half = dirs // 2
    at = lax.broadcasted_iota(jnp.int32, (STRIDE, LANES), 0)
    j = jnp.where(at < dirs, at, jnp.where(at < STRIDE - 1, at - dirs, dirs - 1))
    angles = (2.0 * math.pi / dirs) * j.astype(F32)
    sin_a = jnp.where((j == 0) | (j == half), 0.0, jnp.sin(angles))
    cos_a = jnp.cos(angles)
    from_south = (at <= half)[:, 0:1]
    from_west = (cos_a > 0.0)[:, 0:1]
    cy_base = 0.5 * jnp.abs(sin_a)
    cx_base = 0.25 * jnp.abs(cos_a)

    index = [k if k < dirs else (k - dirs if k < STRIDE - 1 else dirs - 1) for k in range(STRIDE)]
    cosines = [math.cos(2.0 * math.pi * k / dirs) for k in index]

    def by_tile(low, high, values, mask, one, other):
        out = []
        for k in range(low, high, 8):
            signs = {v > 0 for v in values[k : k + 8] if abs(v) > 1e-9}
            if signs == {True}:
                out.append(one(k - low))
            elif signs == {False}:
                out.append(other(k - low))
            else:
                out.append(jnp.where(mask[k : k + 8], one(k - low), other(k - low)))
        return jnp.concatenate(out, axis=0)

    norths = [1 if k <= half else -1 for k in range(STRIDE)]
    latitudes = {}

    def latitude(row):
        if row not in latitudes:
            spot = (band * row_count + row).astype(F32) + 0.5
            lat = jnp.full((8, LANES), spot / rows_all * (2.0 * math.pi / 3.0) - math.pi / 3.0)
            sec = 1.0 / jnp.cos(lat)
            turn = -0.3 * cos_a * (jnp.sin(lat) * sec)[0:1]
            latitudes[row] = (
                (cx_base * sec[0:1])[:, 0:1],
                jnp.abs(turn)[:, 0:1],
                (turn > 0.0)[:, 0:1],
            )
        return latitudes[row]

    def advance(get, row, f, sea, low=0, high=STRIDE):
        part = slice(low, high)
        cx, ct, from_lower = latitude(row)
        speed = 1.0 / (1.0 + 0.25 * f)
        cy = (speed * cy_base)[part, 0:1]
        cx = (speed * cx)[part]
        ct = (speed * ct)[part]
        base = f * STRIDE + low
        x = get(row, slice(base, base + high - low))

        def rows_of(r):
            return lambda k: get(r, slice(base + k, base + k + 8))

        def turned_by(shift):
            return lambda k: pltpu.roll(x[k : k + 8], shift % NLON, 1)

        meridional = by_tile(low, high, norths, from_south, rows_of(row - 1), rows_of(row + 1))
        zonal = by_tile(low, high, cosines, from_west, turned_by(1), turned_by(-1))
        adv = (x - cy * (x - meridional) - cx * (x - zonal)) * sea
        lower = pltpu.roll(adv, 1, 0)
        upper = pltpu.roll(adv, high - low - 1, 0)
        return (adv - ct * (adv - jnp.where(from_lower[part], lower, upper))) * sea

    return advance


def repeat_ends(out, dirs):
    return jnp.concatenate(
        [out[0:dirs], out[0:1], out[dirs + 1 : STRIDE - 1], out[dirs - 1 : dirs]], axis=0
    )


def place_kernel(freqs, dirs, blocks, recv_ref, cell_ref, field_ref, inner_ref, lhs):
    points = cell_ref.shape[1]
    rows = freqs * STRIDE
    row_count = points // NLON
    spread_rows(lambda c: recv_ref[c], freqs, dirs, points, lhs)
    cells = cell_ref[...]
    for t in range(points // TILE):
        both = matmul_nt(lhs[...], one_hot(cells, t * TILE, points))
        field_ref[:, t * TILE : (t + 1) * TILE] = both[0:rows] + both[rows : 2 * rows]
    advance = stepper(freqs, dirs, blocks, row_count)
    for row in range(1, row_count - 1):
        sea = field_ref[dirs + 1 : dirs + 2, lanes(row)]
        for f in range(freqs):
            out = advance(lambda r, piece: field_ref[piece, lanes(r)], row, f, sea)
            inner_ref[f * STRIDE : (f + 1) * STRIDE, lanes(row - 1)] = repeat_ends(out, dirs)


def step_kernel(
    freqs,
    dirs,
    blocks,
    field_ref,
    inner_ref,
    first_ref,
    second_ref,
    cell_ref,
    back_ref,
    south,
    north,
    outer,
    acc,
    lhs,
):
    points = field_ref.shape[1]
    rows = freqs * STRIDE
    row_count = points // NLON
    half = dirs // 2
    inside = half - 1
    near_rows = freqs * (half + 1) + 1
    top = row_count - 1

    def fill(ghost, in_ref, start):
        ghost[0:rows, lanes(1)] = jnp.zeros((rows, NLON), F32)
        for f in range(freqs):
            base = f * STRIDE + start
            at = f * (half + 1)
            ghost[base : base + half + 1, lanes(0)] = in_ref[at : at + half + 1, :]
            if start:
                top_row = (f + 1) * STRIDE - 1
                ghost[top_row : top_row + 1, lanes(0)] = in_ref[at + half - 1 : at + half, :]
            at = near_rows + f * inside
            ghost[base + 1 : base + half, lanes(1)] = in_ref[at : at + inside, :]
        ghost[rows : rows + 1, lanes(0)] = in_ref[near_rows - 1 : near_rows, :]

    even = lax.rem(snake(lax.axis_index("blk"), blocks), 2) == 0

    @pl.when(even)
    def _():
        fill(south, second_ref, 0)
        fill(north, first_ref, half)

    @pl.when(jnp.logical_not(even))
    def _():
        fill(south, first_ref, 0)
        fill(north, second_ref, half)

    def sea_of(row):
        if row < 0:
            return south[rows : rows + 1, lanes(0)]
        if row > top:
            return north[rows : rows + 1, lanes(0)]
        return field_ref[dirs + 1 : dirs + 2, lanes(row)]

    def before(row, piece):
        if row < 0:
            return south[piece, lanes(-1 - row)]
        if row > top:
            return north[piece, lanes(row - top - 1)]
        return field_ref[piece, lanes(row)]

    places = {-1: 0, 0: 1, top: 2, top + 1: 3}

    def between(row, piece):
        if row in places:
            return outer[piece, lanes(places[row])]
        return inner_ref[piece, lanes(row - 1)]

    advance = stepper(freqs, dirs, blocks, row_count)
    south_high = -(-(half + 1) // 8) * 8
    north_low = half // 8 * 8

    def first_step(row, f):
        base = f * STRIDE
        where = lanes(places[row])
        if row < 0:
            out = advance(before, row, f, sea_of(row), 0, south_high)
            outer[base : base + south_high, where] = out
        elif row > top:
            out = advance(before, row, f, sea_of(row), north_low, STRIDE)
            outer[base + north_low : base + STRIDE, where] = out
            spot = dirs - 1 - north_low
            outer[base + STRIDE - 1 : base + STRIDE, where] = out[spot : spot + 1]
        else:
            out = advance(before, row, f, sea_of(row))
            outer[base : base + STRIDE, where] = repeat_ends(out, dirs)

    def second_step(row, f):
        high, low = split(advance(between, row, f, sea_of(row)))
        lhs[f * STRIDE : (f + 1) * STRIDE, lanes(row)] = high
        lhs[rows + f * STRIDE : rows + (f + 1) * STRIDE, lanes(row)] = low

    def pick(t, row):
        where = slice(t * TILE, (t + 1) * TILE)
        cells = cell_ref[:, where]
        table = jnp.concatenate(
            [one_hot(cells, row * NLON + k * TILE, TILE) for k in range(NLON // TILE)], axis=0
        )
        both = jnp.dot(lhs[:, lanes(row)], table, preferred_element_type=F32)
        out = both[0:rows] + both[rows : 2 * rows]
        if row:
            out = acc[:, where] + out
        if row < top:
            acc[:, where] = out
            return
        for h in range(TILE // LANES):
            for q in range(freqs * dirs // 4):
                low = q // (dirs // 4) * STRIDE + q % (dirs // 4) * 4
                back_ref[t * (TILE // LANES) + h, q] = out[
                    low : low + 4, h * LANES : (h + 1) * LANES
                ]

    steps = points // TILE
    for row in places:
        for f in range(freqs):
            first_step(row, f)
    for row in range(row_count + 1):
        for f in range(freqs):
            if row < row_count:
                second_step(row, f)
            if row:
                for t in range(f * steps // freqs, (f + 1) * steps // freqs):
                    pick(t, row - 1)


def pick_kernel(freqs, dirs, recv_ref, pos_ref, out_ref, result, lhs, sems):
    points = pos_ref.shape[1]
    rows = freqs * STRIDE
    spread_rows(
        lambda c: jnp.concatenate([recv_ref[c, q] for q in range(freqs * dirs // 4)], axis=0),
        freqs,
        dirs,
        points,
        lhs,
    )
    parts = []

    def body(t):
        where = slice(t * TILE, (t + 1) * TILE)
        wanted = pos_ref[:, where]
        table = jnp.concatenate(
            [one_hot(wanted, k * TILE, TILE) for k in range(points // TILE)], axis=0
        )
        both = jnp.dot(lhs[...], table, preferred_element_type=F32)
        out = both[0:rows] + both[rows : 2 * rows]
        for f in range(freqs):
            result[f, :, where] = out[f * STRIDE : f * STRIDE + dirs]
        part = pltpu.make_async_copy(
            result.at[:, :, where], out_ref.at[:, :, where], sems.at[t]
        )
        part.start()
        parts.append(part)

    for t in range(points // TILE):
        body(t)
    for part in parts:
        part.wait()


def exchange(x, blocks, cap):
    if cap == LANES:
        return lax.all_to_all(x, "blk", split_axis=0, concat_axis=0, tiled=True)
    pieces, lanes = x.shape[0], x.shape[-1]
    inner = x.shape[1:-1]
    x = jnp.moveaxis(x, 0, -2).reshape(*inner, blocks, cap)
    dim = len(inner)
    x = lax.all_to_all(x, "blk", split_axis=dim, concat_axis=dim, tiled=True)
    return jnp.moveaxis(x.reshape(*inner, pieces, lanes), -2, 0)


def per_device(spectrum, wind_vector, dest_cell, counts, sea_mask, dia_shift):
    blocks = lax.axis_size("blk")
    freqs, dirs, points = spectrum.shape
    cap = points // blocks
    pieces = points // LANES
    rows = freqs * STRIDE
    send_rows = -(-(freqs * dirs + 1) // 8) * 8
    near_rows = freqs * (dirs // 2 + 1) + 1
    far_rows = freqs * (dirs // 2 - 1)
    edge_rows = -(-(near_rows + far_rows) // 8) * 8
    edge_lhs = -(-near_rows // 8) * 8
    vmem = pl.BlockSpec(memory_space=pltpu.VMEM)
    hbm = pl.BlockSpec(memory_space=pltpu.HBM)
    params = pltpu.CompilerParams(vmem_limit_bytes=VMEM_LIMIT)

    def arr(shape, dtype=F32):
        return jax.ShapeDtypeStruct(shape, dtype)

    send, position = pl.pallas_call(
        functools.partial(source_kernel, blocks, cap),
        out_shape=(arr((pieces, send_rows, LANES)), arr((1, points), jnp.int32)),
        in_specs=[hbm] * 5,
        out_specs=(vmem, vmem),
        scratch_shapes=[
            pltpu.SMEM(dia_shift.shape, jnp.int32),
            pltpu.SMEM(counts.shape, jnp.int32),
            pltpu.VMEM(spectrum.shape, F32),
            pltpu.VMEM(wind_vector.shape, F32),
            pltpu.VMEM((1, points), jnp.int32),
            pltpu.VMEM((freqs, 2 * dirs, points), F32),
            pltpu.VMEM((2 * send_rows, points), BF16),
            pltpu.SemaphoreType.DMA((5,)),
        ],
        compiler_params=pltpu.CompilerParams(vmem_limit_bytes=SOURCE_LIMIT),
        name="source",
    )(dia_shift, counts, spectrum, wind_vector, dest_cell.reshape(1, points))
    arrived = exchange(send, blocks, cap)
    first, second, cells = pl.pallas_call(
        functools.partial(edge_kernel, freqs, dirs, blocks),
        out_shape=(
            arr((edge_rows, NLON)),
            arr((edge_rows, NLON)),
            arr((1, points), jnp.int32),
        ),
        in_specs=[vmem],
        out_specs=(vmem,) * 3,
        scratch_shapes=[
            pltpu.VMEM((4 * edge_lhs, points), BF16),
            pltpu.VMEM((1, points), jnp.int32),
            pltpu.VMEM((2 * edge_lhs, 2 * NLON), F32),
        ],
        compiler_params=params,
        name="edges",
    )(arrived)
    inner, outer = halo_swaps(blocks)
    mine, theirs = lax.ppermute(first, "blk", inner), lax.ppermute(second, "blk", outer)
    field, middle = pl.pallas_call(
        functools.partial(place_kernel, freqs, dirs, blocks),
        out_shape=(arr((rows, points)), arr((rows, points - 2 * NLON))),
        in_specs=[vmem] * 2,
        out_specs=(vmem,) * 2,
        scratch_shapes=[pltpu.VMEM((2 * rows, points), BF16)],
        compiler_params=params,
        cost_estimate=pl.CostEstimate(
            flops=4 * rows * points * points, bytes_accessed=8 * rows * points, transcendentals=0
        ),
        name="place",
    )(arrived, cells)
    back = pl.pallas_call(
        functools.partial(step_kernel, freqs, dirs, blocks),
        out_shape=arr((pieces, freqs * dirs // 4, 4, LANES)),
        in_specs=[vmem] * 5,
        out_specs=vmem,
        scratch_shapes=[
            pltpu.VMEM((rows + 8, 2 * NLON), F32),
            pltpu.VMEM((rows + 8, 2 * NLON), F32),
            pltpu.VMEM((rows, 4 * NLON), F32),
            pltpu.VMEM((rows, points), F32),
            pltpu.VMEM((2 * rows, points), BF16),
        ],
        compiler_params=params,
        name="step",
    )(field, middle, mine, theirs, cells)
    returned = exchange(back, blocks, cap)
    return pl.pallas_call(
        functools.partial(pick_kernel, freqs, dirs),
        out_shape=arr((freqs, dirs, points)),
        in_specs=[vmem, vmem],
        out_specs=hbm,
        scratch_shapes=[
            pltpu.VMEM((freqs, dirs, points), F32),
            pltpu.VMEM((2 * rows, points), BF16),
            pltpu.SemaphoreType.DMA((points // TILE,)),
        ],
        compiler_params=params,
        name="pick",
    )(returned, position)


def solution(mesh):
    placed = (
        P(None, None, ("groups", "blk")),
        P(None, ("groups", "blk")),
        P(("groups", "blk")),
        P(("groups", "blk")),
        P(("groups", "blk")),
        P(),
    )
    return jax.shard_map(
        per_device,
        mesh=mesh,
        in_specs=placed,
        out_specs=P(None, None, ("groups", "blk")),
        check_vma=False,
    )
```

```python
import functools
import math

import jax
import jax.numpy as jnp
from jax import lax
from jax.experimental import pallas as pl
from jax.experimental.pallas import tpu as pltpu
from jax.sharding import PartitionSpec as P

NLON = 512
SUBSTEPS = 2
LANES = 128
TILE = 256
GROUP = 512
STRIDE = 40
F32 = jnp.float32
BF16 = jnp.bfloat16
VMEM_LIMIT = 40 * 1024 * 1024
SOURCE_LIMIT = 60 * 1024 * 1024


def snake_row(blocks):
    chips = max(blocks // 2, 1)
    return 1 << ((chips.bit_length() - 1) // 2)


def snake(index, blocks):
    row = snake_row(blocks)
    if blocks % (2 * row):
        return index
    core = lax.rem(index, 2)
    chip = lax.div(index, 2)
    line = lax.div(chip, row)
    place = lax.rem(chip, row)
    place = jnp.where(lax.rem(line, 2) == 1, row - 1 - place, place)
    return (line * row + place) * 2 + core


def halo_swaps(blocks):
    row = snake_row(blocks)
    order = []
    for band in range(blocks):
        if blocks % (2 * row):
            order.append(band)
            continue
        core, chip = band % 2, band // 2
        line, place = chip // row, chip % row
        if line % 2:
            place = row - 1 - place
        order.append((line * row + place) * 2 + core)

    def swaps(first):
        pairs = []
        for band in range(first, blocks - 1, 2):
            low, high = order[band], order[band + 1]
            pairs += [(low, high), (high, low)]
        return pairs

    return swaps(0), swaps(1)


def split(x):
    high = x.astype(BF16)
    return high, (x - high.astype(F32)).astype(BF16)


def one_hot(row, start, width):
    ids = lax.broadcasted_iota(jnp.int32, (TILE, width), 0).astype(F32).astype(BF16)
    wanted = (row - start).astype(F32).astype(BF16)
    return jnp.where(ids == wanted, jnp.ones((), BF16), jnp.zeros((), BF16))


def matmul_nt(data, table):
    return lax.dot_general(
        data, table, (((1,), (1,)), ((), ())), preferred_element_type=F32
    )


def direction_trig(dirs, rows):
    j = lax.broadcasted_iota(jnp.int32, (rows, LANES), 0)
    angles = (2.0 * math.pi / dirs) * j.astype(F32)
    return jnp.cos(angles), jnp.sin(angles)


def shifted(x, shift, size):
    count = x.shape[0] // 8
    fine = lax.rem(shift, 8)
    back = lax.rem(8 - fine, 8)
    keep = lax.broadcasted_iota(jnp.int32, (8, LANES), 0) < 8 - fine
    tiles = [pltpu.roll(x[8 * k : 8 * k + 8], back, 0) for k in range(count)]
    near = [jnp.where(keep, a, b) for a, b in zip(tiles, tiles[1:] + tiles[-1:])]
    out = [jnp.where(shift >= 8, b, a) for a, b in zip(near, near[1:] + near[-1:])]
    return jnp.concatenate(out, axis=0)[0:size]


def source_kernel(
    blocks,
    cap,
    shift_in,
    count_in,
    spec_in,
    wind_in,
    dest_in,
    send_ref,
    pos_ref,
    shift_ref,
    count_ref,
    spec_ref,
    wind_ref,
    dest_ref,
    dbl,
    lhs,
    sems,
):
    freqs, dirs, points = spec_ref.shape
    rows = lhs.shape[0] // 2
    pairs = (
        (dest_in, dest_ref),
        (count_in, count_ref),
        (shift_in, shift_ref),
        (wind_in, wind_ref),
        (spec_in, spec_ref),
    )
    copies = [pltpu.make_async_copy(a, b, sems.at[i]) for i, (a, b) in enumerate(pairs)]
    for copy in copies:
        copy.start()
    copies[0].wait()
    copies[1].wait()
    dest = dest_ref[...]
    slot = lax.broadcasted_iota(jnp.int32, (1, points), 1)
    live = slot < count_ref[0]
    band = lax.shift_right_logical(dest, points.bit_length() - 1)
    band = jnp.where(live, band, -1)
    owner_band = snake(lax.broadcasted_iota(jnp.int32, (blocks, 1), 0), blocks)
    hits = (band == owner_band).astype(F32)
    tri_r = lax.broadcasted_iota(jnp.int32, (LANES, LANES), 0)
    tri_c = lax.broadcasted_iota(jnp.int32, (LANES, LANES), 1)
    upper = (tri_r <= tri_c).astype(F32).astype(BF16)
    ones = jnp.ones((LANES, LANES), BF16)
    base = (lax.broadcasted_iota(jnp.int32, (blocks, LANES), 0) * cap).astype(F32)
    for c in range(points // LANES):
        piece = hits[:, c * LANES : (c + 1) * LANES]
        packed = piece.astype(BF16)
        running = jnp.dot(packed, upper, preferred_element_type=F32) + base
        base = base + jnp.dot(packed, ones, preferred_element_type=F32)
        where_to = jnp.sum(piece * running, axis=0, keepdims=True) - 1.0
        pos_ref[:, c * LANES : (c + 1) * LANES] = where_to.astype(jnp.int32)
    for copy in copies[2:]:
        copy.wait()
    cos_a, sin_a = direction_trig(dirs, dirs)
    span = -(-(dirs + dirs // 4) // 8) * 8
    offset = 2 * dirs - span
    extra = rows - freqs * dirs

    def terms(c):
        where = slice(c * LANES, (c + 1) * LANES)
        total = jnp.zeros((1, LANES), F32)
        for f in range(freqs):
            x = spec_ref[f, :, where]
            dbl[f, 0:dirs, where] = x
            dbl[f, dirs : 2 * dirs, where] = x
            total = total + jnp.sum(x, axis=0, keepdims=True)
        mean = total * (1.0 / (freqs * dirs))
        along = wind_ref[0:1, where] * cos_a + wind_ref[1:2, where] * sin_a
        drive = jnp.maximum(along - 0.3, 0.0)
        pieces = []
        for f in range(freqs):
            x = spec_ref[f, :, where]
            ahead = shifted(dbl[f, 0:span, where], shift_ref[0], dirs)
            behind = shifted(dbl[f, offset:, where], dirs - offset - shift_ref[1], dirs)
            pieces.append(
                x * jnp.exp((0.15 + 0.05 * f) * drive - (0.2 + 0.1 * f) * mean)
                + 0.1 * (ahead * behind - x * x)
            )
        local = (lax.bitwise_and(dest_ref[:, where], points - 1) + 1).astype(F32)
        pieces.append(jnp.broadcast_to(local, (extra, LANES)))
        high, low = split(jnp.concatenate(pieces, axis=0))
        lhs[0:rows, where] = high
        lhs[rows : 2 * rows, where] = low

    per_step = TILE // LANES

    def place(t, g):
        where = slice(g * GROUP, (g + 1) * GROUP)
        both = matmul_nt(lhs[:, where], one_hot(pos_ref[:, where], t * TILE, GROUP))
        out = both[0:rows] + both[rows : 2 * rows]
        for h in range(per_step):
            piece = out[:, h * LANES : (h + 1) * LANES]
            if g:
                piece = send_ref[t * per_step + h] + piece
            send_ref[t * per_step + h] = piece

    groups = points // GROUP
    chunks = GROUP // LANES
    steps = points // TILE
    for g in range(groups + 1):
        for c in range(chunks):
            if g < groups:
                terms(g * chunks + c)
            if g > 0:
                for t in range(c * steps // chunks, (c + 1) * steps // chunks):
                    place(t, g - 1)


def spread_rows(get, freqs, dirs, points, lhs):
    rows = lhs.shape[0] // 2
    fill = jnp.ones((STRIDE - dirs - 2, LANES), F32)
    for c in range(points // LANES):
        x = get(c)
        pieces = []
        for f in range(freqs):
            one = x[f * dirs : (f + 1) * dirs]
            pieces += [one, one[0:1], fill, one[dirs - 1 : dirs]]
        high, low = split(jnp.concatenate(pieces, axis=0))
        lhs[0:rows, c * LANES : (c + 1) * LANES] = high
        lhs[rows : 2 * rows, c * LANES : (c + 1) * LANES] = low


def edge_kernel(freqs, dirs, blocks, recv_ref, first_ref, second_ref, cell_ref, lhs, fold_ref, out_ref):
    points = cell_ref.shape[1]
    label = freqs * dirs
    half = dirs // 2
    rows = lhs.shape[0] // 4
    near_rows = freqs * (half + 1) + 1
    edge = 2 * NLON
    fill = jnp.ones((rows - freqs * (half + 1), LANES), F32)
    for c in range(points // LANES):
        where = slice(c * LANES, (c + 1) * LANES)
        own = recv_ref[c, label : label + 1, :].astype(jnp.int32) - 1
        cell_ref[:, where] = own
        upper = own >= points - edge
        lower = (own >= 0) & (own < edge)
        fold_ref[:, where] = jnp.where(upper, own - (points - edge), jnp.where(lower, own, -1))
        x = recv_ref[c]
        for side, start, other, mine in ((0, 0, half, upper), (1, half, 0, lower)):
            pieces = []
            for f in range(freqs):
                base = f * dirs
                pieces.append(x[base + start : base + start + half])
                pieces.append(x[base + other : base + other + 1])
            high, low = split(jnp.where(mine, jnp.concatenate(pieces + [fill], axis=0), 0.0))
            lhs[side * rows : (side + 1) * rows, where] = high
            lhs[(2 + side) * rows : (3 + side) * rows, where] = low
    cells = fold_ref[...]
    even = lax.rem(snake(lax.axis_index("blk"), blocks), 2) == 0

    def keep(edge_ref, out, t, near):
        where = slice(t * TILE % NLON, t * TILE % NLON + TILE)
        if near:
            edge_ref[0:near_rows, where] = out[0:near_rows]
            return
        for f in range(freqs):
            at = near_rows + f * (half - 1)
            low = f * (half + 1) + 1
            edge_ref[at : at + half - 1, where] = out[low : low + half - 1]

    for t in range(edge // TILE):
        both = matmul_nt(lhs[...], one_hot(cells, t * TILE, points))
        out_ref[:, t * TILE : (t + 1) * TILE] = both[0 : 2 * rows] + both[2 * rows : 4 * rows]

    def store(up_ref, down_ref):
        for t in range(edge // TILE):
            out = out_ref[:, t * TILE : (t + 1) * TILE]
            second_row = t * TILE >= NLON
            keep(up_ref, out[0:rows], t, second_row)
            keep(down_ref, out[rows : 2 * rows], t, not second_row)

    @pl.when(even)
    def _():
        store(first_ref, second_ref)

    @pl.when(jnp.logical_not(even))
    def _():
        store(second_ref, first_ref)


def lanes(row):
    return slice(row * NLON, (row + 1) * NLON)


def stepper(freqs, dirs, blocks, row_count):
    band = snake(lax.axis_index("blk"), blocks)
    rows_all = row_count * blocks
    half = dirs // 2
    at = lax.broadcasted_iota(jnp.int32, (STRIDE, LANES), 0)
    j = jnp.where(at < dirs, at, jnp.where(at < STRIDE - 1, at - dirs, dirs - 1))
    angles = (2.0 * math.pi / dirs) * j.astype(F32)
    sin_a = jnp.where((j == 0) | (j == half), 0.0, jnp.sin(angles))
    cos_a = jnp.cos(angles)
    from_south = (at <= half)[:, 0:1]
    from_west = (cos_a > 0.0)[:, 0:1]
    cy_base = 0.5 * jnp.abs(sin_a)
    cx_base = 0.25 * jnp.abs(cos_a)

    index = [k if k < dirs else (k - dirs if k < STRIDE - 1 else dirs - 1) for k in range(STRIDE)]
    cosines = [math.cos(2.0 * math.pi * k / dirs) for k in index]

    def by_tile(low, high, values, mask, one, other):
        out = []
        for k in range(low, high, 8):
            signs = {v > 0 for v in values[k : k + 8] if abs(v) > 1e-9}
            if signs == {True}:
                out.append(one(k - low))
            elif signs == {False}:
                out.append(other(k - low))
            else:
                out.append(jnp.where(mask[k : k + 8], one(k - low), other(k - low)))
        return jnp.concatenate(out, axis=0)

    norths = [1 if k <= half else -1 for k in range(STRIDE)]
    latitudes = {}

    def latitude(row):
        if row not in latitudes:
            spot = (band * row_count + row).astype(F32) + 0.5
            lat = jnp.full((8, LANES), spot / rows_all * (2.0 * math.pi / 3.0) - math.pi / 3.0)
            sec = 1.0 / jnp.cos(lat)
            turn = -0.3 * cos_a * (jnp.sin(lat) * sec)[0:1]
            latitudes[row] = (
                (cx_base * sec[0:1])[:, 0:1],
                jnp.abs(turn)[:, 0:1],
                (turn > 0.0)[:, 0:1],
            )
        return latitudes[row]

    def advance(get, row, f, sea, low=0, high=STRIDE):
        part = slice(low, high)
        cx, ct, from_lower = latitude(row)
        speed = 1.0 / (1.0 + 0.25 * f)
        cy = (speed * cy_base)[part, 0:1]
        cx = (speed * cx)[part]
        ct = (speed * ct)[part]
        base = f * STRIDE + low
        x = get(row, slice(base, base + high - low))

        def rows_of(r):
            return lambda k: get(r, slice(base + k, base + k + 8))

        def turned_by(shift):
            return lambda k: pltpu.roll(x[k : k + 8], shift % NLON, 1)

        meridional = by_tile(low, high, norths, from_south, rows_of(row - 1), rows_of(row + 1))
        zonal = by_tile(low, high, cosines, from_west, turned_by(1), turned_by(-1))
        adv = (x - cy * (x - meridional) - cx * (x - zonal)) * sea
        return turned(adv, ct, from_lower[part]) * sea

    def turned(adv, ct, from_lower):
        lower = pltpu.roll(adv, 1, 0)
        upper = pltpu.roll(adv, adv.shape[0] - 1, 0)
        return adv - ct * (adv - jnp.where(from_lower, lower, upper))

    def answer(x, row, f, sea, low, high, valid):
        part = slice(low, high)
        _, ct, from_lower = latitude(row)
        speed = 1.0 / (1.0 + 0.25 * f)
        adv = jnp.where(valid[part], (speed * cy_base)[part, 0:1] * x, 0.0) * sea
        return turned(adv, (speed * ct)[part], from_lower[part]) * sea

    south_side = from_south
    north_side = jnp.logical_not(from_south) & (at <= dirs)[:, 0:1]
    return advance, answer, south_side, north_side


def repeat_ends(out, dirs):
    return jnp.concatenate(
        [out[0:dirs], out[0:1], out[dirs + 1 : STRIDE - 1], out[dirs - 1 : dirs]], axis=0
    )


def blank(row, piece):
    return jnp.zeros((piece.stop - piece.start, NLON), F32)


def pick_rows(lhs, cells, first, count, where):
    table = jnp.concatenate(
        [
            one_hot(cells[:, where], first * NLON + k * TILE, TILE)
            for k in range(count * NLON // TILE)
        ],
        axis=0,
    )
    both = jnp.dot(lhs[...], table, preferred_element_type=F32)
    half = lhs.shape[0] // 2
    return both[0:half] + both[half : 2 * half]


def place_kernel(freqs, dirs, blocks, recv_ref, cell_ref, field_ref, mid_ref, pre_ref, lhs, lhs2):
    points = cell_ref.shape[1]
    rows = freqs * STRIDE
    row_count = points // NLON
    spread_rows(lambda c: recv_ref[c], freqs, dirs, points, lhs)
    cells = cell_ref[...]
    for t in range(points // TILE):
        both = matmul_nt(lhs[...], one_hot(cells, t * TILE, points))
        field_ref[:, t * TILE : (t + 1) * TILE] = both[0:rows] + both[rows : 2 * rows]
    advance = stepper(freqs, dirs, blocks, row_count)[0]

    def sea_of(row):
        return field_ref[dirs + 1 : dirs + 2, lanes(row)]

    def before(row, piece):
        if row < 0 or row >= row_count:
            return blank(row, piece)
        return field_ref[piece, lanes(row)]

    for row in range(row_count):
        for f in range(freqs):
            out = advance(before, row, f, sea_of(row))
            mid_ref[f * STRIDE : (f + 1) * STRIDE, lanes(row)] = repeat_ends(out, dirs)
    for row in range(1, row_count - 1):
        for f in range(freqs):
            out = advance(lambda r, piece: mid_ref[piece, lanes(r)], row, f, sea_of(row))
            high, low = split(out)
            base = f * STRIDE
            lhs2[base : base + STRIDE, lanes(row - 1)] = high
            lhs2[rows + base : rows + base + STRIDE, lanes(row - 1)] = low
    for t in range(points // TILE):
        where = slice(t * TILE, (t + 1) * TILE)
        pre_ref[:, where] = pick_rows(lhs2, cell_ref, 1, row_count - 2, where)


def step_kernel(
    freqs,
    dirs,
    blocks,
    field_ref,
    mid_ref,
    pre_ref,
    first_ref,
    second_ref,
    cell_ref,
    back_ref,
    south,
    north,
    outer,
    cross,
    lhs,
    lhs_low,
    lhs_high,
):
    points = field_ref.shape[1]
    rows = freqs * STRIDE
    row_count = points // NLON
    half = dirs // 2
    inside = half - 1
    near_rows = freqs * (half + 1) + 1
    top = row_count - 1

    def fill(ghost, in_ref, start):
        ghost[0:rows, lanes(1)] = jnp.zeros((rows, NLON), F32)
        for f in range(freqs):
            base = f * STRIDE + start
            at = f * (half + 1)
            ghost[base : base + half + 1, lanes(0)] = in_ref[at : at + half + 1, :]
            if start:
                top_row = (f + 1) * STRIDE - 1
                ghost[top_row : top_row + 1, lanes(0)] = in_ref[at + half - 1 : at + half, :]
            at = near_rows + f * inside
            ghost[base + 1 : base + half, lanes(1)] = in_ref[at : at + inside, :]
        ghost[rows : rows + 1, lanes(0)] = in_ref[near_rows - 1 : near_rows, :]

    even = lax.rem(snake(lax.axis_index("blk"), blocks), 2) == 0

    @pl.when(even)
    def _():
        fill(south, second_ref, 0)
        fill(north, first_ref, half)

    @pl.when(jnp.logical_not(even))
    def _():
        fill(south, first_ref, 0)
        fill(north, second_ref, half)

    def sea_of(row):
        if row < 0:
            return south[rows : rows + 1, lanes(0)]
        if row > top:
            return north[rows : rows + 1, lanes(0)]
        return field_ref[dirs + 1 : dirs + 2, lanes(row)]

    def before(row, piece):
        if row < 0:
            return south[piece, lanes(-1 - row)]
        if row > top:
            return north[piece, lanes(row - top - 1)]
        return field_ref[piece, lanes(row)]

    places = {-1: 0, 0: 1, top: 2, top + 1: 3}

    def between(row, piece):
        if row in places:
            return outer[piece, lanes(places[row])]
        return mid_ref[piece, lanes(row)]

    advance, answer, south_side, north_side = stepper(freqs, dirs, blocks, row_count)
    high = -(-(half + 1) // 8) * 8
    low = half // 8 * 8
    wide = STRIDE - low

    def first_step(f):
        base = f * STRIDE
        out = advance(before, -1, f, sea_of(-1), 0, high)
        outer[base : base + high, lanes(places[-1])] = out
        out = advance(before, top + 1, f, sea_of(top + 1), low, STRIDE)
        outer[base + low : base + STRIDE, lanes(places[top + 1])] = out
        spot = dirs - 1 - low
        outer[base + STRIDE - 1 : base + STRIDE, lanes(places[top + 1])] = out[spot : spot + 1]
        more = answer(
            south[base : base + high, lanes(0)], 0, f, sea_of(0), 0, high, south_side
        )
        cross[f * high : (f + 1) * high, :] = more
        old = mid_ref[base : base + STRIDE, lanes(0)]
        outer[base : base + STRIDE, lanes(places[0])] = jnp.concatenate(
            [
                old[0:high] + more,
                old[high:dirs],
                old[dirs : dirs + 1] + more[0:1],
                old[dirs + 1 : STRIDE],
            ],
            axis=0,
        )
        more = answer(
            north[base + low : base + STRIDE, lanes(0)], top, f, sea_of(top), low, STRIDE, north_side
        )
        at = freqs * high + f * wide
        cross[at : at + wide, :] = more
        old = mid_ref[base : base + STRIDE, lanes(top)]
        zero, last = more[dirs - low : dirs - low + 1], more[dirs - 1 - low : dirs - low]
        outer[base : base + STRIDE, lanes(places[top])] = jnp.concatenate(
            [
                old[0:1] + zero,
                old[1:low],
                old[low:dirs] + more[0 : dirs - low],
                old[dirs : dirs + 1] + zero,
                old[dirs + 1 : STRIDE - 1],
                old[STRIDE - 1 : STRIDE] + last,
            ],
            axis=0,
        )

    def second_step(f):
        base = f * STRIDE
        for row, out_lhs in ((0, lhs_low), (top, lhs_high)):
            upper, lower = split(advance(between, row, f, sea_of(row)))
            out_lhs[base : base + STRIDE, :] = upper
            out_lhs[rows + base : rows + base + STRIDE, :] = lower
        total = freqs * (high + wide)
        at = f * high
        upper, lower = split(
            answer(cross[at : at + high, :], 1, f, sea_of(1), 0, high, south_side)
        )
        lhs[at : at + high, :] = upper
        lhs[total + at : total + at + high, :] = lower
        at = freqs * high + f * wide
        upper, lower = split(
            answer(cross[at : at + wide, :], top - 1, f, sea_of(top - 1), low, STRIDE, north_side)
        )
        lhs[at : at + wide, :] = upper
        lhs[total + at : total + at + wide, :] = lower

    def pick(t):
        where = slice(t * TILE, (t + 1) * TILE)
        cells = cell_ref[:, where]
        out = pre_ref[:, where]
        out = out + pick_rows(lhs_low, cell_ref, 0, 1, where)
        out = out + pick_rows(lhs_high, cell_ref, top, 1, where)
        row = lax.shift_right_arithmetic(cells, NLON.bit_length() - 1)
        inside = jnp.where(
            row == 1, cells - NLON, jnp.where(row == top - 1, cells - (top - 1) * NLON, -1)
        )
        table = jnp.concatenate(
            [one_hot(inside, k * TILE, TILE) for k in range(NLON // TILE)], axis=0
        )
        both = jnp.dot(lhs[...], table, preferred_element_type=F32)
        total = freqs * (high + wide)
        both = both[0:total] + both[total : 2 * total]
        from_below = jnp.where(row == 1, both[0 : freqs * high], 0.0)
        from_above = jnp.where(row == top - 1, both[freqs * high : total], 0.0)
        for f in range(freqs):
            base = f * STRIDE
            below = from_below[f * high : (f + 1) * high]
            above = from_above[f * wide : (f + 1) * wide]
            sums = jnp.concatenate(
                [
                    out[base : base + low] + below[0:low],
                    out[base + low : base + high] + below[low:high] + above[0 : high - low],
                    out[base + high : base + STRIDE] + above[high - low : wide],
                ],
                axis=0,
            )
            first = sums[0:1] + above[dirs - low : dirs - low + 1]
            sums = jnp.concatenate([first, sums[1:dirs]], axis=0)
            for h in range(TILE // LANES):
                for q in range(dirs // 4):
                    back_ref[t * (TILE // LANES) + h, f * (dirs // 4) + q] = sums[
                        4 * q : 4 * q + 4, h * LANES : (h + 1) * LANES
                    ]

    for f in range(freqs):
        first_step(f)
    for f in range(freqs):
        second_step(f)
    for t in range(points // TILE):
        pick(t)


def pick_kernel(freqs, dirs, recv_ref, pos_ref, out_ref, result, lhs, sems):
    points = pos_ref.shape[1]
    rows = freqs * STRIDE
    spread_rows(
        lambda c: jnp.concatenate([recv_ref[c, q] for q in range(freqs * dirs // 4)], axis=0),
        freqs,
        dirs,
        points,
        lhs,
    )
    parts = []

    def body(t):
        where = slice(t * TILE, (t + 1) * TILE)
        wanted = pos_ref[:, where]
        table = jnp.concatenate(
            [one_hot(wanted, k * TILE, TILE) for k in range(points // TILE)], axis=0
        )
        both = jnp.dot(lhs[...], table, preferred_element_type=F32)
        out = both[0:rows] + both[rows : 2 * rows]
        for f in range(freqs):
            result[f, :, where] = out[f * STRIDE : f * STRIDE + dirs]
        part = pltpu.make_async_copy(
            result.at[:, :, where], out_ref.at[:, :, where], sems.at[t]
        )
        part.start()
        parts.append(part)

    for t in range(points // TILE):
        body(t)
    for part in parts:
        part.wait()


def exchange(x, blocks, cap):
    if cap == LANES:
        return lax.all_to_all(x, "blk", split_axis=0, concat_axis=0, tiled=True)
    pieces, lanes = x.shape[0], x.shape[-1]
    inner = x.shape[1:-1]
    x = jnp.moveaxis(x, 0, -2).reshape(*inner, blocks, cap)
    dim = len(inner)
    x = lax.all_to_all(x, "blk", split_axis=dim, concat_axis=dim, tiled=True)
    return jnp.moveaxis(x.reshape(*inner, pieces, lanes), -2, 0)


def per_device(spectrum, wind_vector, dest_cell, counts, sea_mask, dia_shift):
    blocks = lax.axis_size("blk")
    freqs, dirs, points = spectrum.shape
    cap = points // blocks
    pieces = points // LANES
    rows = freqs * STRIDE
    send_rows = -(-(freqs * dirs + 1) // 8) * 8
    near_rows = freqs * (dirs // 2 + 1) + 1
    far_rows = freqs * (dirs // 2 - 1)
    edge_rows = -(-(near_rows + far_rows) // 8) * 8
    edge_lhs = -(-near_rows // 8) * 8
    vmem = pl.BlockSpec(memory_space=pltpu.VMEM)
    hbm = pl.BlockSpec(memory_space=pltpu.HBM)
    params = pltpu.CompilerParams(vmem_limit_bytes=VMEM_LIMIT)

    def arr(shape, dtype=F32):
        return jax.ShapeDtypeStruct(shape, dtype)

    send, position = pl.pallas_call(
        functools.partial(source_kernel, blocks, cap),
        out_shape=(arr((pieces, send_rows, LANES)), arr((1, points), jnp.int32)),
        in_specs=[hbm] * 5,
        out_specs=(vmem, vmem),
        scratch_shapes=[
            pltpu.SMEM(dia_shift.shape, jnp.int32),
            pltpu.SMEM(counts.shape, jnp.int32),
            pltpu.VMEM(spectrum.shape, F32),
            pltpu.VMEM(wind_vector.shape, F32),
            pltpu.VMEM((1, points), jnp.int32),
            pltpu.VMEM((freqs, 2 * dirs, points), F32),
            pltpu.VMEM((2 * send_rows, points), BF16),
            pltpu.SemaphoreType.DMA((5,)),
        ],
        compiler_params=pltpu.CompilerParams(vmem_limit_bytes=SOURCE_LIMIT),
        name="source",
    )(dia_shift, counts, spectrum, wind_vector, dest_cell.reshape(1, points))
    arrived = exchange(send, blocks, cap)
    first, second, cells = pl.pallas_call(
        functools.partial(edge_kernel, freqs, dirs, blocks),
        out_shape=(
            arr((edge_rows, NLON)),
            arr((edge_rows, NLON)),
            arr((1, points), jnp.int32),
        ),
        in_specs=[vmem],
        out_specs=(vmem,) * 3,
        scratch_shapes=[
            pltpu.VMEM((4 * edge_lhs, points), BF16),
            pltpu.VMEM((1, points), jnp.int32),
            pltpu.VMEM((2 * edge_lhs, 2 * NLON), F32),
        ],
        compiler_params=params,
        name="edges",
    )(arrived)
    inner, outer = halo_swaps(blocks)
    mine, theirs = lax.ppermute(first, "blk", inner), lax.ppermute(second, "blk", outer)
    field, middle, inner_part = pl.pallas_call(
        functools.partial(place_kernel, freqs, dirs, blocks),
        out_shape=(arr((rows, points)),) * 3,
        in_specs=[vmem] * 2,
        out_specs=(vmem,) * 3,
        scratch_shapes=[
            pltpu.VMEM((2 * rows, points), BF16),
            pltpu.VMEM((2 * rows, points - 2 * NLON), BF16),
        ],
        compiler_params=params,
        cost_estimate=pl.CostEstimate(
            flops=6 * rows * points * points, bytes_accessed=8 * rows * points, transcendentals=0
        ),
        name="place",
    )(arrived, cells)
    half = dirs // 2
    cross_rows = freqs * (-(-(half + 1) // 8) * 8 + STRIDE - half // 8 * 8)
    back = pl.pallas_call(
        functools.partial(step_kernel, freqs, dirs, blocks),
        out_shape=arr((pieces, freqs * dirs // 4, 4, LANES)),
        in_specs=[vmem] * 6,
        out_specs=vmem,
        scratch_shapes=[
            pltpu.VMEM((rows + 8, 2 * NLON), F32),
            pltpu.VMEM((rows + 8, 2 * NLON), F32),
            pltpu.VMEM((rows, 4 * NLON), F32),
            pltpu.VMEM((cross_rows, NLON), F32),
            pltpu.VMEM((2 * cross_rows, NLON), BF16),
            pltpu.VMEM((2 * rows, NLON), BF16),
            pltpu.VMEM((2 * rows, NLON), BF16),
        ],
        compiler_params=params,
        name="step",
    )(field, middle, inner_part, mine, theirs, cells)
    returned = exchange(back, blocks, cap)
    return pl.pallas_call(
        functools.partial(pick_kernel, freqs, dirs),
        out_shape=arr((freqs, dirs, points)),
        in_specs=[vmem, vmem],
        out_specs=hbm,
        scratch_shapes=[
            pltpu.VMEM((freqs, dirs, points), F32),
            pltpu.VMEM((2 * rows, points), BF16),
            pltpu.SemaphoreType.DMA((points // TILE,)),
        ],
        compiler_params=params,
        name="pick",
    )(returned, position)


def solution(mesh):
    placed = (
        P(None, None, ("groups", "blk")),
        P(None, ("groups", "blk")),
        P(("groups", "blk")),
        P(("groups", "blk")),
        P(("groups", "blk")),
        P(),
    )
    return jax.shard_map(
        per_device,
        mesh=mesh,
        in_specs=placed,
        out_specs=P(None, None, ("groups", "blk")),
        check_vma=False,
    )
```

```python
import functools
import math

import jax
import jax.numpy as jnp
from jax import lax
from jax.experimental import pallas as pl
from jax.experimental.pallas import tpu as pltpu
from jax.sharding import PartitionSpec as P

NLON = 512
SUBSTEPS = 2
LANES = 128
TILE = 256
GROUP = 512
STRIDE = 40
F32 = jnp.float32
BF16 = jnp.bfloat16
VMEM_LIMIT = 40 * 1024 * 1024
SOURCE_LIMIT = 60 * 1024 * 1024


def snake_row(blocks):
    chips = max(blocks // 2, 1)
    return 1 << ((chips.bit_length() - 1) // 2)


def snake(index, blocks):
    row = snake_row(blocks)
    if blocks % (2 * row):
        return index
    core = lax.rem(index, 2)
    chip = lax.div(index, 2)
    line = lax.div(chip, row)
    place = lax.rem(chip, row)
    place = jnp.where(lax.rem(line, 2) == 1, row - 1 - place, place)
    return (line * row + place) * 2 + core


def halo_swaps(blocks):
    row = snake_row(blocks)
    order = []
    for band in range(blocks):
        if blocks % (2 * row):
            order.append(band)
            continue
        core, chip = band % 2, band // 2
        line, place = chip // row, chip % row
        if line % 2:
            place = row - 1 - place
        order.append((line * row + place) * 2 + core)

    def swaps(first):
        pairs = []
        for band in range(first, blocks - 1, 2):
            low, high = order[band], order[band + 1]
            pairs += [(low, high), (high, low)]
        return pairs

    return swaps(0), swaps(1)


def split(x):
    high = x.astype(BF16)
    return high, (x - high.astype(F32)).astype(BF16)


def one_hot(row, start, width):
    ids = lax.broadcasted_iota(jnp.int32, (TILE, width), 0).astype(F32).astype(BF16)
    wanted = (row - start).astype(F32).astype(BF16)
    return jnp.where(ids == wanted, jnp.ones((), BF16), jnp.zeros((), BF16))


def matmul_nt(data, table):
    return lax.dot_general(
        data, table, (((1,), (1,)), ((), ())), preferred_element_type=F32
    )


def direction_trig(dirs, rows):
    j = lax.broadcasted_iota(jnp.int32, (rows, LANES), 0)
    angles = (2.0 * math.pi / dirs) * j.astype(F32)
    return jnp.cos(angles), jnp.sin(angles)


def shifted(x, shift, size):
    count = x.shape[0] // 8
    fine = lax.rem(shift, 8)
    back = lax.rem(8 - fine, 8)
    keep = lax.broadcasted_iota(jnp.int32, (8, LANES), 0) < 8 - fine
    tiles = [pltpu.roll(x[8 * k : 8 * k + 8], back, 0) for k in range(count)]
    near = [jnp.where(keep, a, b) for a, b in zip(tiles, tiles[1:] + tiles[-1:])]
    out = [jnp.where(shift >= 8, b, a) for a, b in zip(near, near[1:] + near[-1:])]
    return jnp.concatenate(out, axis=0)[0:size]


def source_kernel(
    blocks,
    cap,
    shift_in,
    count_in,
    spec_in,
    wind_in,
    dest_in,
    send_ref,
    pos_ref,
    shift_ref,
    count_ref,
    spec_ref,
    wind_ref,
    dest_ref,
    dbl,
    lhs,
    acc,
    sems,
):
    freqs, dirs, points = spec_ref.shape
    rows = lhs.shape[0] // 2
    pairs = (
        (dest_in, dest_ref),
        (count_in, count_ref),
        (shift_in, shift_ref),
        (wind_in, wind_ref),
        (spec_in, spec_ref),
    )
    copies = [pltpu.make_async_copy(a, b, sems.at[i]) for i, (a, b) in enumerate(pairs)]
    for copy in copies:
        copy.start()
    copies[0].wait()
    copies[1].wait()
    dest = dest_ref[...]
    slot = lax.broadcasted_iota(jnp.int32, (1, points), 1)
    live = slot < count_ref[0]
    band = lax.shift_right_logical(dest, points.bit_length() - 1)
    band = jnp.where(live, band, -1)
    owner_band = snake(lax.broadcasted_iota(jnp.int32, (blocks, 1), 0), blocks)
    hits = (band == owner_band).astype(F32)
    tri_r = lax.broadcasted_iota(jnp.int32, (LANES, LANES), 0)
    tri_c = lax.broadcasted_iota(jnp.int32, (LANES, LANES), 1)
    upper = (tri_r <= tri_c).astype(F32).astype(BF16)
    ones = jnp.ones((LANES, LANES), BF16)
    base = (lax.broadcasted_iota(jnp.int32, (blocks, LANES), 0) * cap).astype(F32)
    for c in range(points // LANES):
        piece = hits[:, c * LANES : (c + 1) * LANES]
        packed = piece.astype(BF16)
        running = jnp.dot(packed, upper, preferred_element_type=F32) + base
        base = base + jnp.dot(packed, ones, preferred_element_type=F32)
        where_to = jnp.sum(piece * running, axis=0, keepdims=True) - 1.0
        pos_ref[:, c * LANES : (c + 1) * LANES] = where_to.astype(jnp.int32)
    for copy in copies[2:]:
        copy.wait()
    cos_a, sin_a = direction_trig(dirs, dirs)
    span = -(-(dirs + dirs // 4) // 8) * 8
    offset = 2 * dirs - span
    extra = rows - freqs * dirs

    def terms(c):
        where = slice(c * LANES, (c + 1) * LANES)
        total = jnp.zeros((1, LANES), F32)
        for f in range(freqs):
            x = spec_ref[f, :, where]
            dbl[f, 0:dirs, where] = x
            dbl[f, dirs : 2 * dirs, where] = x
            total = total + jnp.sum(x, axis=0, keepdims=True)
        mean = total * (1.0 / (freqs * dirs))
        along = wind_ref[0:1, where] * cos_a + wind_ref[1:2, where] * sin_a
        drive = jnp.maximum(along - 0.3, 0.0)
        pieces = []
        for f in range(freqs):
            x = spec_ref[f, :, where]
            ahead = shifted(dbl[f, 0:span, where], shift_ref[0], dirs)
            behind = shifted(dbl[f, offset:, where], dirs - offset - shift_ref[1], dirs)
            pieces.append(
                x * jnp.exp((0.15 + 0.05 * f) * drive - (0.2 + 0.1 * f) * mean)
                + 0.1 * (ahead * behind - x * x)
            )
        local = (lax.bitwise_and(dest_ref[:, where], points - 1) + 1).astype(F32)
        pieces.append(jnp.broadcast_to(local, (extra, LANES)))
        high, low = split(jnp.concatenate(pieces, axis=0))
        lhs[0:rows, where] = high
        lhs[rows : 2 * rows, where] = low

    per_step = TILE // LANES
    send_rows = freqs * dirs + 1

    def place(t, g):
        where = slice(g * GROUP, (g + 1) * GROUP)
        both = matmul_nt(lhs[:, where], one_hot(pos_ref[:, where], t * TILE, GROUP))
        out = both[0:rows] + both[rows : 2 * rows]
        for h in range(per_step):
            piece = out[:, h * LANES : (h + 1) * LANES]
            k = t * per_step + h
            if g:
                piece = acc[k] + piece
            if g < groups - 1:
                acc[k] = piece
            else:
                send_ref[k * send_rows : (k + 1) * send_rows, :] = piece[0:send_rows]

    groups = points // GROUP
    chunks = GROUP // LANES
    steps = points // TILE
    for g in range(groups + 1):
        for c in range(chunks):
            if g < groups:
                terms(g * chunks + c)
            if g > 0:
                for t in range(c * steps // chunks, (c + 1) * steps // chunks):
                    place(t, g - 1)


def spread_rows(get, freqs, dirs, points, lhs):
    rows = lhs.shape[0] // 2
    fill = jnp.ones((STRIDE - dirs - 2, LANES), F32)
    for c in range(points // LANES):
        x = get(c)
        pieces = []
        for f in range(freqs):
            one = x[f * dirs : (f + 1) * dirs]
            pieces += [one, one[0:1], fill, one[dirs - 1 : dirs]]
        high, low = split(jnp.concatenate(pieces, axis=0))
        lhs[0:rows, c * LANES : (c + 1) * LANES] = high
        lhs[rows : 2 * rows, c * LANES : (c + 1) * LANES] = low


def edge_kernel(freqs, dirs, blocks, recv_ref, first_ref, second_ref, cell_ref, lhs, fold_ref, out_ref):
    points = cell_ref.shape[1]
    label = freqs * dirs
    half = dirs // 2
    rows = lhs.shape[0] // 4
    near_rows = freqs * (half + 1) + 1
    edge = 2 * NLON
    fill = jnp.ones((rows - freqs * (half + 1), LANES), F32)
    for c in range(points // LANES):
        where = slice(c * LANES, (c + 1) * LANES)
        x = recv_ref[c * (label + 1) : (c + 1) * (label + 1), :]
        own = x[label : label + 1].astype(jnp.int32) - 1
        cell_ref[:, where] = own
        upper = own >= points - edge
        lower = (own >= 0) & (own < edge)
        fold_ref[:, where] = jnp.where(upper, own - (points - edge), jnp.where(lower, own, -1))
        for side, start, other, mine in ((0, 0, half, upper), (1, half, 0, lower)):
            pieces = []
            for f in range(freqs):
                base = f * dirs
                pieces.append(x[base + start : base + start + half])
                pieces.append(x[base + other : base + other + 1])
            high, low = split(jnp.where(mine, jnp.concatenate(pieces + [fill], axis=0), 0.0))
            lhs[side * rows : (side + 1) * rows, where] = high
            lhs[(2 + side) * rows : (3 + side) * rows, where] = low
    cells = fold_ref[...]
    even = lax.rem(snake(lax.axis_index("blk"), blocks), 2) == 0

    def keep(edge_ref, out, t, near):
        where = slice(t * TILE % NLON, t * TILE % NLON + TILE)
        if near:
            edge_ref[0:near_rows, where] = out[0:near_rows]
            return
        for f in range(freqs):
            at = near_rows + f * (half - 1)
            low = f * (half + 1) + 1
            edge_ref[at : at + half - 1, where] = out[low : low + half - 1]

    for t in range(edge // TILE):
        both = matmul_nt(lhs[...], one_hot(cells, t * TILE, points))
        out_ref[:, t * TILE : (t + 1) * TILE] = both[0 : 2 * rows] + both[2 * rows : 4 * rows]

    def store(up_ref, down_ref):
        for t in range(edge // TILE):
            out = out_ref[:, t * TILE : (t + 1) * TILE]
            second_row = t * TILE >= NLON
            keep(up_ref, out[0:rows], t, second_row)
            keep(down_ref, out[rows : 2 * rows], t, not second_row)

    @pl.when(even)
    def _():
        store(first_ref, second_ref)

    @pl.when(jnp.logical_not(even))
    def _():
        store(second_ref, first_ref)


def lanes(row):
    return slice(row * NLON, (row + 1) * NLON)


def stepper(freqs, dirs, blocks, row_count):
    band = snake(lax.axis_index("blk"), blocks)
    rows_all = row_count * blocks
    half = dirs // 2
    at = lax.broadcasted_iota(jnp.int32, (STRIDE, LANES), 0)
    j = jnp.where(at < dirs, at, jnp.where(at < STRIDE - 1, at - dirs, dirs - 1))
    angles = (2.0 * math.pi / dirs) * j.astype(F32)
    sin_a = jnp.where((j == 0) | (j == half), 0.0, jnp.sin(angles))
    cos_a = jnp.cos(angles)
    from_south = (at <= half)[:, 0:1]
    from_west = (cos_a > 0.0)[:, 0:1]
    cy_base = 0.5 * jnp.abs(sin_a)
    cx_base = 0.25 * jnp.abs(cos_a)

    index = [k if k < dirs else (k - dirs if k < STRIDE - 1 else dirs - 1) for k in range(STRIDE)]
    cosines = [math.cos(2.0 * math.pi * k / dirs) for k in index]

    def by_tile(low, high, values, mask, one, other):
        out = []
        for k in range(low, high, 8):
            signs = {v > 0 for v in values[k : k + 8] if abs(v) > 1e-9}
            if signs == {True}:
                out.append(one(k - low))
            elif signs == {False}:
                out.append(other(k - low))
            else:
                out.append(jnp.where(mask[k : k + 8], one(k - low), other(k - low)))
        return jnp.concatenate(out, axis=0)

    norths = [1 if k <= half else -1 for k in range(STRIDE)]
    latitudes = {}

    def latitude(row):
        if row not in latitudes:
            spot = (band * row_count + row).astype(F32) + 0.5
            lat = jnp.full((8, LANES), spot / rows_all * (2.0 * math.pi / 3.0) - math.pi / 3.0)
            sec = 1.0 / jnp.cos(lat)
            turn = -0.3 * cos_a * (jnp.sin(lat) * sec)[0:1]
            latitudes[row] = (
                (cx_base * sec[0:1])[:, 0:1],
                jnp.abs(turn)[:, 0:1],
                (turn > 0.0)[:, 0:1],
            )
        return latitudes[row]

    def advance(get, row, f, sea, low=0, high=STRIDE):
        part = slice(low, high)
        cx, ct, from_lower = latitude(row)
        speed = 1.0 / (1.0 + 0.25 * f)
        cy = (speed * cy_base)[part, 0:1]
        cx = (speed * cx)[part]
        ct = (speed * ct)[part]
        base = f * STRIDE + low
        x = get(row, slice(base, base + high - low))

        def rows_of(r):
            return lambda k: get(r, slice(base + k, base + k + 8))

        def turned_by(shift):
            return lambda k: pltpu.roll(x[k : k + 8], shift % NLON, 1)

        meridional = by_tile(low, high, norths, from_south, rows_of(row - 1), rows_of(row + 1))
        zonal = by_tile(low, high, cosines, from_west, turned_by(1), turned_by(-1))
        adv = (x - cy * (x - meridional) - cx * (x - zonal)) * sea
        return turned(adv, ct, from_lower[part]) * sea

    def turned(adv, ct, from_lower):
        lower = pltpu.roll(adv, 1, 0)
        upper = pltpu.roll(adv, adv.shape[0] - 1, 0)
        return adv - ct * (adv - jnp.where(from_lower, lower, upper))

    def answer(x, row, f, sea, low, high, valid):
        part = slice(low, high)
        _, ct, from_lower = latitude(row)
        speed = 1.0 / (1.0 + 0.25 * f)
        adv = jnp.where(valid[part], (speed * cy_base)[part, 0:1] * x, 0.0) * sea
        return turned(adv, (speed * ct)[part], from_lower[part]) * sea

    south_side = from_south
    north_side = jnp.logical_not(from_south) & (at <= dirs)[:, 0:1]
    return advance, answer, south_side, north_side


def repeat_ends(out, dirs):
    return jnp.concatenate(
        [out[0:dirs], out[0:1], out[dirs + 1 : STRIDE - 1], out[dirs - 1 : dirs]], axis=0
    )


def blank(row, piece):
    return jnp.zeros((piece.stop - piece.start, NLON), F32)


def pick_rows(lhs, cells, first, count, where):
    table = jnp.concatenate(
        [
            one_hot(cells[:, where], first * NLON + k * TILE, TILE)
            for k in range(count * NLON // TILE)
        ],
        axis=0,
    )
    both = jnp.dot(lhs[...], table, preferred_element_type=F32)
    half = lhs.shape[0] // 2
    return both[0:half] + both[half : 2 * half]


def place_kernel(freqs, dirs, blocks, recv_ref, cell_ref, field_ref, mid_ref, pre_ref, lhs, lhs2):
    points = cell_ref.shape[1]
    rows = freqs * STRIDE
    row_count = points // NLON
    count = freqs * dirs
    spread_rows(
        lambda c: recv_ref[c * (count + 1) : c * (count + 1) + count, :], freqs, dirs, points, lhs
    )
    cells = cell_ref[...]
    for t in range(points // TILE):
        both = matmul_nt(lhs[...], one_hot(cells, t * TILE, points))
        field_ref[:, t * TILE : (t + 1) * TILE] = both[0:rows] + both[rows : 2 * rows]
    advance = stepper(freqs, dirs, blocks, row_count)[0]

    def sea_of(row):
        return field_ref[dirs + 1 : dirs + 2, lanes(row)]

    def before(row, piece):
        if row < 0 or row >= row_count:
            return blank(row, piece)
        return field_ref[piece, lanes(row)]

    for row in range(row_count):
        for f in range(freqs):
            out = advance(before, row, f, sea_of(row))
            mid_ref[f * STRIDE : (f + 1) * STRIDE, lanes(row)] = repeat_ends(out, dirs)
    for row in range(1, row_count - 1):
        for f in range(freqs):
            out = advance(lambda r, piece: mid_ref[piece, lanes(r)], row, f, sea_of(row))
            high, low = split(out)
            base = f * STRIDE
            lhs2[base : base + STRIDE, lanes(row - 1)] = high
            lhs2[rows + base : rows + base + STRIDE, lanes(row - 1)] = low
    for t in range(points // TILE):
        where = slice(t * TILE, (t + 1) * TILE)
        pre_ref[:, where] = pick_rows(lhs2, cell_ref, 1, row_count - 2, where)


def step_kernel(
    freqs,
    dirs,
    blocks,
    field_ref,
    mid_ref,
    pre_ref,
    first_ref,
    second_ref,
    cell_ref,
    back_ref,
    south,
    north,
    outer,
    cross,
    lhs,
    lhs_low,
    lhs_high,
):
    points = field_ref.shape[1]
    rows = freqs * STRIDE
    row_count = points // NLON
    half = dirs // 2
    inside = half - 1
    near_rows = freqs * (half + 1) + 1
    top = row_count - 1

    def fill(ghost, in_ref, start):
        ghost[0:rows, lanes(1)] = jnp.zeros((rows, NLON), F32)
        for f in range(freqs):
            base = f * STRIDE + start
            at = f * (half + 1)
            ghost[base : base + half + 1, lanes(0)] = in_ref[at : at + half + 1, :]
            if start:
                top_row = (f + 1) * STRIDE - 1
                ghost[top_row : top_row + 1, lanes(0)] = in_ref[at + half - 1 : at + half, :]
            at = near_rows + f * inside
            ghost[base + 1 : base + half, lanes(1)] = in_ref[at : at + inside, :]
        ghost[rows : rows + 1, lanes(0)] = in_ref[near_rows - 1 : near_rows, :]

    even = lax.rem(snake(lax.axis_index("blk"), blocks), 2) == 0

    @pl.when(even)
    def _():
        fill(south, second_ref, 0)
        fill(north, first_ref, half)

    @pl.when(jnp.logical_not(even))
    def _():
        fill(south, first_ref, 0)
        fill(north, second_ref, half)

    def sea_of(row):
        if row < 0:
            return south[rows : rows + 1, lanes(0)]
        if row > top:
            return north[rows : rows + 1, lanes(0)]
        return field_ref[dirs + 1 : dirs + 2, lanes(row)]

    def before(row, piece):
        if row < 0:
            return south[piece, lanes(-1 - row)]
        if row > top:
            return north[piece, lanes(row - top - 1)]
        return field_ref[piece, lanes(row)]

    places = {-1: 0, 0: 1, top: 2, top + 1: 3}

    def between(row, piece):
        if row in places:
            return outer[piece, lanes(places[row])]
        return mid_ref[piece, lanes(row)]

    advance, answer, south_side, north_side = stepper(freqs, dirs, blocks, row_count)
    high = -(-(half + 1) // 8) * 8
    low = half // 8 * 8
    wide = STRIDE - low

    def first_step(f):
        base = f * STRIDE
        out = advance(before, -1, f, sea_of(-1), 0, high)
        outer[base : base + high, lanes(places[-1])] = out
        out = advance(before, top + 1, f, sea_of(top + 1), low, STRIDE)
        outer[base + low : base + STRIDE, lanes(places[top + 1])] = out
        spot = dirs - 1 - low
        outer[base + STRIDE - 1 : base + STRIDE, lanes(places[top + 1])] = out[spot : spot + 1]
        more = answer(
            south[base : base + high, lanes(0)], 0, f, sea_of(0), 0, high, south_side
        )
        cross[f * high : (f + 1) * high, :] = more
        old = mid_ref[base : base + STRIDE, lanes(0)]
        outer[base : base + STRIDE, lanes(places[0])] = jnp.concatenate(
            [
                old[0:high] + more,
                old[high:dirs],
                old[dirs : dirs + 1] + more[0:1],
                old[dirs + 1 : STRIDE],
            ],
            axis=0,
        )
        more = answer(
            north[base + low : base + STRIDE, lanes(0)], top, f, sea_of(top), low, STRIDE, north_side
        )
        at = freqs * high + f * wide
        cross[at : at + wide, :] = more
        old = mid_ref[base : base + STRIDE, lanes(top)]
        zero, last = more[dirs - low : dirs - low + 1], more[dirs - 1 - low : dirs - low]
        outer[base : base + STRIDE, lanes(places[top])] = jnp.concatenate(
            [
                old[0:1] + zero,
                old[1:low],
                old[low:dirs] + more[0 : dirs - low],
                old[dirs : dirs + 1] + zero,
                old[dirs + 1 : STRIDE - 1],
                old[STRIDE - 1 : STRIDE] + last,
            ],
            axis=0,
        )

    def second_step(f):
        base = f * STRIDE
        for row, out_lhs in ((0, lhs_low), (top, lhs_high)):
            upper, lower = split(advance(between, row, f, sea_of(row)))
            out_lhs[base : base + STRIDE, :] = upper
            out_lhs[rows + base : rows + base + STRIDE, :] = lower
        total = freqs * (high + wide)
        at = f * high
        upper, lower = split(
            answer(cross[at : at + high, :], 1, f, sea_of(1), 0, high, south_side)
        )
        lhs[at : at + high, :] = upper
        lhs[total + at : total + at + high, :] = lower
        at = freqs * high + f * wide
        upper, lower = split(
            answer(cross[at : at + wide, :], top - 1, f, sea_of(top - 1), low, STRIDE, north_side)
        )
        lhs[at : at + wide, :] = upper
        lhs[total + at : total + at + wide, :] = lower

    def pick(t):
        where = slice(t * TILE, (t + 1) * TILE)
        cells = cell_ref[:, where]
        out = pre_ref[:, where]
        out = out + pick_rows(lhs_low, cell_ref, 0, 1, where)
        out = out + pick_rows(lhs_high, cell_ref, top, 1, where)
        row = lax.shift_right_arithmetic(cells, NLON.bit_length() - 1)
        inside = jnp.where(
            row == 1, cells - NLON, jnp.where(row == top - 1, cells - (top - 1) * NLON, -1)
        )
        table = jnp.concatenate(
            [one_hot(inside, k * TILE, TILE) for k in range(NLON // TILE)], axis=0
        )
        both = jnp.dot(lhs[...], table, preferred_element_type=F32)
        total = freqs * (high + wide)
        both = both[0:total] + both[total : 2 * total]
        from_below = jnp.where(row == 1, both[0 : freqs * high], 0.0)
        from_above = jnp.where(row == top - 1, both[freqs * high : total], 0.0)
        for f in range(freqs):
            base = f * STRIDE
            below = from_below[f * high : (f + 1) * high]
            above = from_above[f * wide : (f + 1) * wide]
            sums = jnp.concatenate(
                [
                    out[base : base + low] + below[0:low],
                    out[base + low : base + high] + below[low:high] + above[0 : high - low],
                    out[base + high : base + STRIDE] + above[high - low : wide],
                ],
                axis=0,
            )
            first = sums[0:1] + above[dirs - low : dirs - low + 1]
            sums = jnp.concatenate([first, sums[1:dirs]], axis=0)
            for h in range(TILE // LANES):
                at = ((t * (TILE // LANES) + h) * freqs + f) * dirs
                back_ref[at : at + dirs, :] = sums[:, h * LANES : (h + 1) * LANES]

    for f in range(freqs):
        first_step(f)
    for f in range(freqs):
        second_step(f)
    for t in range(points // TILE):
        pick(t)


def pick_kernel(freqs, dirs, recv_ref, pos_ref, out_ref, result, lhs, sems):
    points = pos_ref.shape[1]
    rows = freqs * STRIDE
    count = freqs * dirs
    spread_rows(
        lambda c: recv_ref[c * count : (c + 1) * count, :], freqs, dirs, points, lhs
    )
    parts = []

    def body(t):
        where = slice(t * TILE, (t + 1) * TILE)
        wanted = pos_ref[:, where]
        table = jnp.concatenate(
            [one_hot(wanted, k * TILE, TILE) for k in range(points // TILE)], axis=0
        )
        both = jnp.dot(lhs[...], table, preferred_element_type=F32)
        out = both[0:rows] + both[rows : 2 * rows]
        for f in range(freqs):
            result[f, :, where] = out[f * STRIDE : f * STRIDE + dirs]
        part = pltpu.make_async_copy(
            result.at[:, :, where], out_ref.at[:, :, where], sems.at[t]
        )
        part.start()
        parts.append(part)

    for t in range(points // TILE):
        body(t)
    for part in parts:
        part.wait()


def exchange(x, blocks, cap):
    pieces = blocks * cap // LANES
    rows = x.shape[0] // pieces
    if cap == LANES:
        parts = x.reshape(blocks, rows, 1, LANES)
        parts = lax.all_to_all(parts, "blk", split_axis=0, concat_axis=0, tiled=True)
        return parts.reshape(x.shape)
    parts = jnp.moveaxis(x.reshape(pieces, rows, LANES), 1, 0).reshape(rows, blocks, cap)
    parts = lax.all_to_all(parts, "blk", split_axis=1, concat_axis=1, tiled=True)
    return jnp.moveaxis(parts.reshape(rows, pieces, LANES), 0, 1).reshape(x.shape)


def per_device(spectrum, wind_vector, dest_cell, counts, sea_mask, dia_shift):
    blocks = lax.axis_size("blk")
    freqs, dirs, points = spectrum.shape
    cap = points // blocks
    pieces = points // LANES
    rows = freqs * STRIDE
    lhs_rows = -(-(freqs * dirs + 1) // 8) * 8
    near_rows = freqs * (dirs // 2 + 1) + 1
    far_rows = freqs * (dirs // 2 - 1)
    edge_rows = -(-(near_rows + far_rows) // 8) * 8
    edge_lhs = -(-near_rows // 8) * 8
    vmem = pl.BlockSpec(memory_space=pltpu.VMEM)
    hbm = pl.BlockSpec(memory_space=pltpu.HBM)
    params = pltpu.CompilerParams(vmem_limit_bytes=VMEM_LIMIT)

    def arr(shape, dtype=F32):
        return jax.ShapeDtypeStruct(shape, dtype)

    send, position = pl.pallas_call(
        functools.partial(source_kernel, blocks, cap),
        out_shape=(arr((pieces * (freqs * dirs + 1), LANES)), arr((1, points), jnp.int32)),
        in_specs=[hbm] * 5,
        out_specs=(vmem, vmem),
        scratch_shapes=[
            pltpu.SMEM(dia_shift.shape, jnp.int32),
            pltpu.SMEM(counts.shape, jnp.int32),
            pltpu.VMEM(spectrum.shape, F32),
            pltpu.VMEM(wind_vector.shape, F32),
            pltpu.VMEM((1, points), jnp.int32),
            pltpu.VMEM((freqs, 2 * dirs, points), F32),
            pltpu.VMEM((2 * lhs_rows, points), BF16),
            pltpu.VMEM((pieces, lhs_rows, LANES), F32),
            pltpu.SemaphoreType.DMA((5,)),
        ],
        compiler_params=pltpu.CompilerParams(vmem_limit_bytes=SOURCE_LIMIT),
        name="source",
    )(dia_shift, counts, spectrum, wind_vector, dest_cell.reshape(1, points))
    arrived = exchange(send, blocks, cap)
    first, second, cells = pl.pallas_call(
        functools.partial(edge_kernel, freqs, dirs, blocks),
        out_shape=(
            arr((edge_rows, NLON)),
            arr((edge_rows, NLON)),
            arr((1, points), jnp.int32),
        ),
        in_specs=[vmem],
        out_specs=(vmem,) * 3,
        scratch_shapes=[
            pltpu.VMEM((4 * edge_lhs, points), BF16),
            pltpu.VMEM((1, points), jnp.int32),
            pltpu.VMEM((2 * edge_lhs, 2 * NLON), F32),
        ],
        compiler_params=params,
        name="edges",
    )(arrived)
    inner, outer = halo_swaps(blocks)
    mine, theirs = lax.ppermute(first, "blk", inner), lax.ppermute(second, "blk", outer)
    field, middle, inner_part = pl.pallas_call(
        functools.partial(place_kernel, freqs, dirs, blocks),
        out_shape=(arr((rows, points)),) * 3,
        in_specs=[vmem] * 2,
        out_specs=(vmem,) * 3,
        scratch_shapes=[
            pltpu.VMEM((2 * rows, points), BF16),
            pltpu.VMEM((2 * rows, points - 2 * NLON), BF16),
        ],
        compiler_params=params,
        cost_estimate=pl.CostEstimate(
            flops=6 * rows * points * points, bytes_accessed=8 * rows * points, transcendentals=0
        ),
        name="place",
    )(arrived, cells)
    half = dirs // 2
    cross_rows = freqs * (-(-(half + 1) // 8) * 8 + STRIDE - half // 8 * 8)
    back = pl.pallas_call(
        functools.partial(step_kernel, freqs, dirs, blocks),
        out_shape=arr((pieces * freqs * dirs, LANES)),
        in_specs=[vmem] * 6,
        out_specs=vmem,
        scratch_shapes=[
            pltpu.VMEM((rows + 8, 2 * NLON), F32),
            pltpu.VMEM((rows + 8, 2 * NLON), F32),
            pltpu.VMEM((rows, 4 * NLON), F32),
            pltpu.VMEM((cross_rows, NLON), F32),
            pltpu.VMEM((2 * cross_rows, NLON), BF16),
            pltpu.VMEM((2 * rows, NLON), BF16),
            pltpu.VMEM((2 * rows, NLON), BF16),
        ],
        compiler_params=params,
        name="step",
    )(field, middle, inner_part, mine, theirs, cells)
    returned = exchange(back, blocks, cap)
    return pl.pallas_call(
        functools.partial(pick_kernel, freqs, dirs),
        out_shape=arr((freqs, dirs, points)),
        in_specs=[vmem, vmem],
        out_specs=hbm,
        scratch_shapes=[
            pltpu.VMEM((freqs, dirs, points), F32),
            pltpu.VMEM((2 * rows, points), BF16),
            pltpu.SemaphoreType.DMA((points // TILE,)),
        ],
        compiler_params=params,
        name="pick",
    )(returned, position)


def solution(mesh):
    placed = (
        P(None, None, ("groups", "blk")),
        P(None, ("groups", "blk")),
        P(("groups", "blk")),
        P(("groups", "blk")),
        P(("groups", "blk")),
        P(),
    )
    return jax.shard_map(
        per_device,
        mesh=mesh,
        in_specs=placed,
        out_specs=P(None, None, ("groups", "blk")),
        check_vma=False,
    )
```

```python
import functools
import math

import jax
import jax.numpy as jnp
from jax import lax
from jax.experimental import pallas as pl
from jax.experimental.pallas import tpu as pltpu
from jax.sharding import PartitionSpec as P

NLON = 512
SUBSTEPS = 2
LANES = 128
TILE = 256
GROUP = 512
STRIDE = 40
F32 = jnp.float32
BF16 = jnp.bfloat16
VMEM_LIMIT = 40 * 1024 * 1024
SOURCE_LIMIT = 60 * 1024 * 1024


def snake_row(blocks):
    chips = max(blocks // 2, 1)
    return 1 << ((chips.bit_length() - 1) // 2)


def snake(index, blocks):
    row = snake_row(blocks)
    if blocks % (2 * row):
        return index
    core = lax.rem(index, 2)
    chip = lax.div(index, 2)
    line = lax.div(chip, row)
    place = lax.rem(chip, row)
    place = jnp.where(lax.rem(line, 2) == 1, row - 1 - place, place)
    return (line * row + place) * 2 + core


def halo_swaps(blocks):
    row = snake_row(blocks)
    order = []
    for band in range(blocks):
        if blocks % (2 * row):
            order.append(band)
            continue
        core, chip = band % 2, band // 2
        line, place = chip // row, chip % row
        if line % 2:
            place = row - 1 - place
        order.append((line * row + place) * 2 + core)

    def swaps(first):
        pairs = []
        for band in range(first, blocks - 1, 2):
            low, high = order[band], order[band + 1]
            pairs += [(low, high), (high, low)]
        return pairs

    return swaps(0), swaps(1)


def split(x):
    high = x.astype(BF16)
    return high, (x - high.astype(F32)).astype(BF16)


def one_hot(row, start, width):
    ids = lax.broadcasted_iota(jnp.int32, (TILE, width), 0).astype(F32).astype(BF16)
    wanted = (row - start).astype(F32).astype(BF16)
    return jnp.where(ids == wanted, jnp.ones((), BF16), jnp.zeros((), BF16))


def matmul_nt(data, table):
    return lax.dot_general(
        data, table, (((1,), (1,)), ((), ())), preferred_element_type=F32
    )


def direction_trig(dirs, rows):
    j = lax.broadcasted_iota(jnp.int32, (rows, LANES), 0)
    angles = (2.0 * math.pi / dirs) * j.astype(F32)
    return jnp.cos(angles), jnp.sin(angles)


def shifted(x, shift, size):
    count = x.shape[0] // 8
    fine = lax.rem(shift, 8)
    back = lax.rem(8 - fine, 8)
    keep = lax.broadcasted_iota(jnp.int32, (8, LANES), 0) < 8 - fine
    tiles = [pltpu.roll(x[8 * k : 8 * k + 8], back, 0) for k in range(count)]
    near = [jnp.where(keep, a, b) for a, b in zip(tiles, tiles[1:] + tiles[-1:])]
    out = [jnp.where(shift >= 8, b, a) for a, b in zip(near, near[1:] + near[-1:])]
    return jnp.concatenate(out, axis=0)[0:size]


def source_kernel(
    blocks,
    cap,
    shift_in,
    count_in,
    spec_in,
    wind_in,
    dest_in,
    send_ref,
    pos_ref,
    shift_ref,
    count_ref,
    spec_ref,
    wind_ref,
    dest_ref,
    dbl,
    lhs,
    acc,
    sems,
):
    freqs, dirs, points = spec_ref.shape
    rows = lhs.shape[0] // 2
    pairs = (
        (dest_in, dest_ref),
        (count_in, count_ref),
        (shift_in, shift_ref),
        (wind_in, wind_ref),
        (spec_in, spec_ref),
    )
    copies = [pltpu.make_async_copy(a, b, sems.at[i]) for i, (a, b) in enumerate(pairs)]
    for copy in copies:
        copy.start()
    copies[0].wait()
    copies[1].wait()
    dest = dest_ref[...]
    slot = lax.broadcasted_iota(jnp.int32, (1, points), 1)
    live = slot < count_ref[0]
    band = lax.shift_right_logical(dest, points.bit_length() - 1)
    band = jnp.where(live, band, -1)
    owner_band = snake(lax.broadcasted_iota(jnp.int32, (blocks, 1), 0), blocks)
    hits = (band == owner_band).astype(F32)
    tri_r = lax.broadcasted_iota(jnp.int32, (LANES, LANES), 0)
    tri_c = lax.broadcasted_iota(jnp.int32, (LANES, LANES), 1)
    upper = (tri_r <= tri_c).astype(F32).astype(BF16)
    ones = jnp.ones((LANES, LANES), BF16)
    base = (lax.broadcasted_iota(jnp.int32, (blocks, LANES), 0) * cap).astype(F32)
    for c in range(points // LANES):
        piece = hits[:, c * LANES : (c + 1) * LANES]
        packed = piece.astype(BF16)
        running = jnp.dot(packed, upper, preferred_element_type=F32) + base
        base = base + jnp.dot(packed, ones, preferred_element_type=F32)
        where_to = jnp.sum(piece * running, axis=0, keepdims=True) - 1.0
        pos_ref[:, c * LANES : (c + 1) * LANES] = where_to.astype(jnp.int32)
    for copy in copies[2:]:
        copy.wait()
    cos_a, sin_a = direction_trig(dirs, dirs)
    span = -(-(dirs + dirs // 4) // 8) * 8
    offset = 2 * dirs - span
    extra = rows - freqs * dirs

    def terms(c):
        where = slice(c * LANES, (c + 1) * LANES)
        total = jnp.zeros((1, LANES), F32)
        for f in range(freqs):
            x = spec_ref[f, :, where]
            dbl[f, 0:dirs, where] = x
            dbl[f, dirs : 2 * dirs, where] = x
            total = total + jnp.sum(x, axis=0, keepdims=True)
        mean = total * (1.0 / (freqs * dirs))
        along = wind_ref[0:1, where] * cos_a + wind_ref[1:2, where] * sin_a
        drive = jnp.maximum(along - 0.3, 0.0)
        pieces = []
        for f in range(freqs):
            x = spec_ref[f, :, where]
            ahead = shifted(dbl[f, 0:span, where], shift_ref[0], dirs)
            behind = shifted(dbl[f, offset:, where], dirs - offset - shift_ref[1], dirs)
            pieces.append(
                x * jnp.exp((0.15 + 0.05 * f) * drive - (0.2 + 0.1 * f) * mean)
                + 0.1 * (ahead * behind - x * x)
            )
        local = (lax.bitwise_and(dest_ref[:, where], points - 1) + 1).astype(F32)
        pieces.append(jnp.broadcast_to(local, (extra, LANES)))
        high, low = split(jnp.concatenate(pieces, axis=0))
        lhs[0:rows, where] = high
        lhs[rows : 2 * rows, where] = low

    per_step = TILE // LANES
    send_rows = freqs * dirs + 1

    def place(t, g):
        where = slice(g * GROUP, (g + 1) * GROUP)
        both = matmul_nt(lhs[:, where], one_hot(pos_ref[:, where], t * TILE, GROUP))
        out = both[0:rows] + both[rows : 2 * rows]
        for h in range(per_step):
            piece = out[:, h * LANES : (h + 1) * LANES]
            k = t * per_step + h
            if g:
                piece = acc[k] + piece
            if g < groups - 1:
                acc[k] = piece
            else:
                send_ref[k * send_rows : (k + 1) * send_rows, :] = piece[0:send_rows]

    groups = points // GROUP
    chunks = GROUP // LANES
    steps = points // TILE
    for g in range(groups + 1):
        for c in range(chunks):
            if g < groups:
                terms(g * chunks + c)
            if g > 0:
                for t in range(c * steps // chunks, (c + 1) * steps // chunks):
                    place(t, g - 1)


def spread_rows(get, freqs, dirs, points, lhs):
    rows = lhs.shape[0] // 2
    fill = jnp.ones((STRIDE - dirs - 2, LANES), F32)
    for c in range(points // LANES):
        x = get(c)
        pieces = []
        for f in range(freqs):
            one = x[f * dirs : (f + 1) * dirs]
            pieces += [one, one[0:1], fill, one[dirs - 1 : dirs]]
        high, low = split(jnp.concatenate(pieces, axis=0))
        lhs[0:rows, c * LANES : (c + 1) * LANES] = high
        lhs[rows : 2 * rows, c * LANES : (c + 1) * LANES] = low


def edge_kernel(freqs, dirs, blocks, recv_ref, first_ref, second_ref, cell_ref, lhs, fold_ref, out_ref):
    points = cell_ref.shape[1]
    label = freqs * dirs
    half = dirs // 2
    rows = lhs.shape[0] // 4
    near_rows = freqs * (half + 1) + 1
    edge = 2 * NLON
    fill = jnp.ones((rows - freqs * (half + 1), LANES), F32)
    for c in range(points // LANES):
        where = slice(c * LANES, (c + 1) * LANES)
        x = recv_ref[c * (label + 1) : (c + 1) * (label + 1), :]
        own = x[label : label + 1].astype(jnp.int32) - 1
        cell_ref[:, where] = own
        upper = own >= points - edge
        lower = (own >= 0) & (own < edge)
        fold_ref[:, where] = jnp.where(upper, own - (points - edge), jnp.where(lower, own, -1))
        for side, start, other, mine in ((0, 0, half, upper), (1, half, 0, lower)):
            pieces = []
            for f in range(freqs):
                base = f * dirs
                pieces.append(x[base + start : base + start + half])
                pieces.append(x[base + other : base + other + 1])
            high, low = split(jnp.where(mine, jnp.concatenate(pieces + [fill], axis=0), 0.0))
            lhs[side * rows : (side + 1) * rows, where] = high
            lhs[(2 + side) * rows : (3 + side) * rows, where] = low
    cells = fold_ref[...]
    even = lax.rem(snake(lax.axis_index("blk"), blocks), 2) == 0

    def keep(edge_ref, out, t, near):
        where = slice(t * TILE % NLON, t * TILE % NLON + TILE)
        if near:
            edge_ref[0:near_rows, where] = out[0:near_rows]
            return
        for f in range(freqs):
            at = near_rows + f * (half - 1)
            low = f * (half + 1) + 1
            edge_ref[at : at + half - 1, where] = out[low : low + half - 1]

    for t in range(edge // TILE):
        both = matmul_nt(lhs[...], one_hot(cells, t * TILE, points))
        out_ref[:, t * TILE : (t + 1) * TILE] = both[0 : 2 * rows] + both[2 * rows : 4 * rows]

    def store(up_ref, down_ref):
        for t in range(edge // TILE):
            out = out_ref[:, t * TILE : (t + 1) * TILE]
            second_row = t * TILE >= NLON
            keep(up_ref, out[0:rows], t, second_row)
            keep(down_ref, out[rows : 2 * rows], t, not second_row)

    @pl.when(even)
    def _():
        store(first_ref, second_ref)

    @pl.when(jnp.logical_not(even))
    def _():
        store(second_ref, first_ref)


def lanes(row):
    return slice(row * NLON, (row + 1) * NLON)


def stepper(freqs, dirs, blocks, row_count):
    band = snake(lax.axis_index("blk"), blocks)
    rows_all = row_count * blocks
    half = dirs // 2
    at = lax.broadcasted_iota(jnp.int32, (STRIDE, LANES), 0)
    j = jnp.where(at < dirs, at, jnp.where(at < STRIDE - 1, at - dirs, dirs - 1))
    angles = (2.0 * math.pi / dirs) * j.astype(F32)
    sin_a = jnp.where((j == 0) | (j == half), 0.0, jnp.sin(angles))
    cos_a = jnp.cos(angles)
    from_south = (at <= half)[:, 0:1]
    from_west = (cos_a > 0.0)[:, 0:1]
    cy_base = 0.5 * jnp.abs(sin_a)
    cx_base = 0.25 * jnp.abs(cos_a)

    index = [k if k < dirs else (k - dirs if k < STRIDE - 1 else dirs - 1) for k in range(STRIDE)]
    cosines = [math.cos(2.0 * math.pi * k / dirs) for k in index]

    def by_tile(low, high, values, mask, one, other):
        out = []
        for k in range(low, high, 8):
            signs = {v > 0 for v in values[k : k + 8] if abs(v) > 1e-9}
            if signs == {True}:
                out.append(one(k - low))
            elif signs == {False}:
                out.append(other(k - low))
            else:
                out.append(jnp.where(mask[k : k + 8], one(k - low), other(k - low)))
        return jnp.concatenate(out, axis=0)

    norths = [1 if k <= half else -1 for k in range(STRIDE)]
    latitudes = {}

    def latitude(row):
        if row not in latitudes:
            spot = (band * row_count + row).astype(F32) + 0.5
            lat = jnp.full((8, LANES), spot / rows_all * (2.0 * math.pi / 3.0) - math.pi / 3.0)
            sec = 1.0 / jnp.cos(lat)
            turn = -0.3 * cos_a * (jnp.sin(lat) * sec)[0:1]
            latitudes[row] = (
                (cx_base * sec[0:1])[:, 0:1],
                jnp.abs(turn)[:, 0:1],
                (turn > 0.0)[:, 0:1],
            )
        return latitudes[row]

    def advance(get, row, f, sea, low=0, high=STRIDE):
        part = slice(low, high)
        cx, ct, from_lower = latitude(row)
        speed = 1.0 / (1.0 + 0.25 * f)
        cy = (speed * cy_base)[part, 0:1]
        cx = (speed * cx)[part]
        ct = (speed * ct)[part]
        base = f * STRIDE + low
        x = get(row, slice(base, base + high - low))

        def rows_of(r):
            return lambda k: get(r, slice(base + k, base + k + 8))

        def turned_by(shift):
            return lambda k: pltpu.roll(x[k : k + 8], shift % NLON, 1)

        meridional = by_tile(low, high, norths, from_south, rows_of(row - 1), rows_of(row + 1))
        zonal = by_tile(low, high, cosines, from_west, turned_by(1), turned_by(-1))
        adv = (x - cy * (x - meridional) - cx * (x - zonal)) * sea
        return turned(adv, ct, from_lower[part]) * sea

    def turned(adv, ct, from_lower):
        lower = pltpu.roll(adv, 1, 0)
        upper = pltpu.roll(adv, adv.shape[0] - 1, 0)
        return adv - ct * (adv - jnp.where(from_lower, lower, upper))

    def answer(x, row, f, sea, low, high, valid):
        part = slice(low, high)
        _, ct, from_lower = latitude(row)
        speed = 1.0 / (1.0 + 0.25 * f)
        adv = jnp.where(valid[part], (speed * cy_base)[part, 0:1] * x, 0.0) * sea
        return turned(adv, (speed * ct)[part], from_lower[part]) * sea

    south_side = from_south
    north_side = jnp.logical_not(from_south) & (at <= dirs)[:, 0:1]
    return advance, answer, south_side, north_side


def repeat_ends(out, dirs):
    return jnp.concatenate(
        [out[0:dirs], out[0:1], out[dirs + 1 : STRIDE - 1], out[dirs - 1 : dirs]], axis=0
    )


def blank(row, piece):
    return jnp.zeros((piece.stop - piece.start, NLON), F32)


def pick_rows(lhs, cells, first, count, where):
    table = jnp.concatenate(
        [
            one_hot(cells[:, where], first * NLON + k * TILE, TILE)
            for k in range(count * NLON // TILE)
        ],
        axis=0,
    )
    both = jnp.dot(lhs[...], table, preferred_element_type=F32)
    half = lhs.shape[0] // 2
    return both[0:half] + both[half : 2 * half]


def place_kernel(freqs, dirs, blocks, recv_ref, cell_ref, field_ref, mid_ref, pre_ref, lhs, lhs2):
    points = cell_ref.shape[1]
    rows = freqs * STRIDE
    row_count = points // NLON
    count = freqs * dirs
    spread_rows(
        lambda c: recv_ref[c * (count + 1) : c * (count + 1) + count, :], freqs, dirs, points, lhs
    )
    cells = cell_ref[...]
    for t in range(points // TILE):
        both = matmul_nt(lhs[...], one_hot(cells, t * TILE, points))
        field_ref[:, t * TILE : (t + 1) * TILE] = both[0:rows] + both[rows : 2 * rows]
    advance = stepper(freqs, dirs, blocks, row_count)[0]

    def sea_of(row):
        return field_ref[dirs + 1 : dirs + 2, lanes(row)]

    def before(row, piece):
        if row < 0 or row >= row_count:
            return blank(row, piece)
        return field_ref[piece, lanes(row)]

    for row in range(row_count):
        for f in range(freqs):
            out = advance(before, row, f, sea_of(row))
            mid_ref[f * STRIDE : (f + 1) * STRIDE, lanes(row)] = repeat_ends(out, dirs)
    for row in range(1, row_count - 1):
        for f in range(freqs):
            out = advance(lambda r, piece: mid_ref[piece, lanes(r)], row, f, sea_of(row))
            high, low = split(out)
            base = f * STRIDE
            lhs2[base : base + STRIDE, lanes(row - 1)] = high
            lhs2[rows + base : rows + base + STRIDE, lanes(row - 1)] = low
    for t in range(points // TILE):
        where = slice(t * TILE, (t + 1) * TILE)
        pre_ref[:, where] = pick_rows(lhs2, cell_ref, 1, row_count - 2, where)


def step_kernel(
    freqs,
    dirs,
    blocks,
    field_ref,
    mid_ref,
    pre_ref,
    first_ref,
    second_ref,
    cell_ref,
    back_ref,
    south,
    north,
    outer,
    cross,
    lhs,
    lhs_low,
    lhs_high,
):
    points = field_ref.shape[1]
    rows = freqs * STRIDE
    row_count = points // NLON
    half = dirs // 2
    inside = half - 1
    near_rows = freqs * (half + 1) + 1
    top = row_count - 1

    def fill(ghost, in_ref, start):
        ghost[...] = jnp.zeros(ghost.shape, F32)
        for f in range(freqs):
            base = f * STRIDE + start
            at = f * (half + 1)
            ghost[base : base + half + 1, lanes(0)] = in_ref[at : at + half + 1, :]
            if start:
                top_row = (f + 1) * STRIDE - 1
                ghost[top_row : top_row + 1, lanes(0)] = in_ref[at + half - 1 : at + half, :]
            at = near_rows + f * inside
            ghost[base + 1 : base + half, lanes(1)] = in_ref[at : at + inside, :]
        ghost[rows : rows + 1, lanes(0)] = in_ref[near_rows - 1 : near_rows, :]

    even = lax.rem(snake(lax.axis_index("blk"), blocks), 2) == 0

    @pl.when(even)
    def _():
        fill(south, second_ref, 0)
        fill(north, first_ref, half)

    @pl.when(jnp.logical_not(even))
    def _():
        fill(south, first_ref, 0)
        fill(north, second_ref, half)

    def sea_of(row):
        if row < 0:
            return south[rows : rows + 1, lanes(0)]
        if row > top:
            return north[rows : rows + 1, lanes(0)]
        return field_ref[dirs + 1 : dirs + 2, lanes(row)]

    def before(row, piece):
        if row < 0:
            return south[piece, lanes(-1 - row)]
        if row > top:
            return north[piece, lanes(row - top - 1)]
        return field_ref[piece, lanes(row)]

    places = {-1: 0, 0: 1, top: 2, top + 1: 3}

    def between(row, piece):
        if row in places:
            return outer[piece, lanes(places[row])]
        return mid_ref[piece, lanes(row)]

    advance, answer, south_side, north_side = stepper(freqs, dirs, blocks, row_count)
    high = -(-(half + 1) // 8) * 8
    low = half // 8 * 8
    wide = STRIDE - low

    def first_step(f):
        base = f * STRIDE
        out = advance(before, -1, f, sea_of(-1), 0, high)
        outer[base : base + high, lanes(places[-1])] = out
        out = advance(before, top + 1, f, sea_of(top + 1), low, STRIDE)
        outer[base + low : base + STRIDE, lanes(places[top + 1])] = out
        spot = dirs - 1 - low
        outer[base + STRIDE - 1 : base + STRIDE, lanes(places[top + 1])] = out[spot : spot + 1]
        more = answer(
            south[base : base + high, lanes(0)], 0, f, sea_of(0), 0, high, south_side
        )
        cross[f * high : (f + 1) * high, :] = more
        old = mid_ref[base : base + STRIDE, lanes(0)]
        outer[base : base + STRIDE, lanes(places[0])] = jnp.concatenate(
            [
                old[0:high] + more,
                old[high:dirs],
                old[dirs : dirs + 1] + more[0:1],
                old[dirs + 1 : STRIDE],
            ],
            axis=0,
        )
        more = answer(
            north[base + low : base + STRIDE, lanes(0)], top, f, sea_of(top), low, STRIDE, north_side
        )
        at = freqs * high + f * wide
        cross[at : at + wide, :] = more
        old = mid_ref[base : base + STRIDE, lanes(top)]
        zero, last = more[dirs - low : dirs - low + 1], more[dirs - 1 - low : dirs - low]
        outer[base : base + STRIDE, lanes(places[top])] = jnp.concatenate(
            [
                old[0:1] + zero,
                old[1:low],
                old[low:dirs] + more[0 : dirs - low],
                old[dirs : dirs + 1] + zero,
                old[dirs + 1 : STRIDE - 1],
                old[STRIDE - 1 : STRIDE] + last,
            ],
            axis=0,
        )

    def second_step(f):
        base = f * STRIDE
        for row, out_lhs in ((0, lhs_low), (top, lhs_high)):
            upper, lower = split(advance(between, row, f, sea_of(row)))
            out_lhs[base : base + STRIDE, :] = upper
            out_lhs[rows + base : rows + base + STRIDE, :] = lower
        total = freqs * (high + wide)
        at = f * high
        upper, lower = split(
            answer(cross[at : at + high, :], 1, f, sea_of(1), 0, high, south_side)
        )
        lhs[at : at + high, :] = upper
        lhs[total + at : total + at + high, :] = lower
        at = freqs * high + f * wide
        upper, lower = split(
            answer(cross[at : at + wide, :], top - 1, f, sea_of(top - 1), low, STRIDE, north_side)
        )
        lhs[at : at + wide, :] = upper
        lhs[total + at : total + at + wide, :] = lower

    def pick(t):
        where = slice(t * TILE, (t + 1) * TILE)
        cells = cell_ref[:, where]
        out = pre_ref[:, where]
        out = out + pick_rows(lhs_low, cell_ref, 0, 1, where)
        out = out + pick_rows(lhs_high, cell_ref, top, 1, where)
        row = lax.shift_right_arithmetic(cells, NLON.bit_length() - 1)
        inside = jnp.where(
            row == 1, cells - NLON, jnp.where(row == top - 1, cells - (top - 1) * NLON, -1)
        )
        table = jnp.concatenate(
            [one_hot(inside, k * TILE, TILE) for k in range(NLON // TILE)], axis=0
        )
        both = jnp.dot(lhs[...], table, preferred_element_type=F32)
        total = freqs * (high + wide)
        both = both[0:total] + both[total : 2 * total]
        from_below = jnp.where(row == 1, both[0 : freqs * high], 0.0)
        from_above = jnp.where(row == top - 1, both[freqs * high : total], 0.0)
        for f in range(freqs):
            base = f * STRIDE
            below = from_below[f * high : (f + 1) * high]
            above = from_above[f * wide : (f + 1) * wide]
            sums = jnp.concatenate(
                [
                    out[base : base + low] + below[0:low],
                    out[base + low : base + high] + below[low:high] + above[0 : high - low],
                    out[base + high : base + STRIDE] + above[high - low : wide],
                ],
                axis=0,
            )
            first = sums[0:1] + above[dirs - low : dirs - low + 1]
            sums = jnp.concatenate([first, sums[1:dirs]], axis=0)
            for h in range(TILE // LANES):
                at = ((t * (TILE // LANES) + h) * freqs + f) * dirs
                back_ref[at : at + dirs, :] = sums[:, h * LANES : (h + 1) * LANES]

    for f in range(freqs):
        first_step(f)
    for f in range(freqs):
        second_step(f)
    for t in range(points // TILE):
        pick(t)


def pick_kernel(freqs, dirs, recv_ref, pos_ref, out_ref, result, lhs, sems):
    points = pos_ref.shape[1]
    rows = lhs.shape[0] // 2
    count = freqs * dirs
    fill = jnp.zeros((rows - count, LANES), F32)
    for c in range(points // LANES):
        x = jnp.concatenate([recv_ref[c * count : (c + 1) * count, :], fill], axis=0)
        high, low = split(x)
        lhs[0:rows, c * LANES : (c + 1) * LANES] = high
        lhs[rows : 2 * rows, c * LANES : (c + 1) * LANES] = low
    parts = []

    def body(t):
        where = slice(t * TILE, (t + 1) * TILE)
        wanted = pos_ref[:, where]
        table = jnp.concatenate(
            [one_hot(wanted, k * TILE, TILE) for k in range(points // TILE)], axis=0
        )
        both = jnp.dot(lhs[...], table, preferred_element_type=F32)
        out = both[0:rows] + both[rows : 2 * rows]
        for f in range(freqs):
            result[f, :, where] = out[f * dirs : (f + 1) * dirs]
        part = pltpu.make_async_copy(
            result.at[:, :, where], out_ref.at[:, :, where], sems.at[t]
        )
        part.start()
        parts.append(part)

    for t in range(points // TILE):
        body(t)
    for part in parts:
        part.wait()


def exchange(x, blocks, cap):
    pieces = blocks * cap // LANES
    rows = x.shape[0] // pieces
    if cap == LANES:
        parts = x.reshape(blocks, rows, 1, LANES)
        parts = lax.all_to_all(parts, "blk", split_axis=0, concat_axis=0, tiled=True)
        return parts.reshape(x.shape)
    parts = jnp.moveaxis(x.reshape(pieces, rows, LANES), 1, 0).reshape(rows, blocks, cap)
    parts = lax.all_to_all(parts, "blk", split_axis=1, concat_axis=1, tiled=True)
    return jnp.moveaxis(parts.reshape(rows, pieces, LANES), 0, 1).reshape(x.shape)


def per_device(spectrum, wind_vector, dest_cell, counts, sea_mask, dia_shift):
    blocks = lax.axis_size("blk")
    freqs, dirs, points = spectrum.shape
    cap = points // blocks
    pieces = points // LANES
    rows = freqs * STRIDE
    lhs_rows = -(-(freqs * dirs + 1) // 8) * 8
    near_rows = freqs * (dirs // 2 + 1) + 1
    far_rows = freqs * (dirs // 2 - 1)
    edge_rows = -(-(near_rows + far_rows) // 8) * 8
    edge_lhs = -(-near_rows // 8) * 8
    vmem = pl.BlockSpec(memory_space=pltpu.VMEM)
    hbm = pl.BlockSpec(memory_space=pltpu.HBM)
    params = pltpu.CompilerParams(vmem_limit_bytes=VMEM_LIMIT)

    def arr(shape, dtype=F32):
        return jax.ShapeDtypeStruct(shape, dtype)

    send, position = pl.pallas_call(
        functools.partial(source_kernel, blocks, cap),
        out_shape=(arr((pieces * (freqs * dirs + 1), LANES)), arr((1, points), jnp.int32)),
        in_specs=[hbm] * 5,
        out_specs=(vmem, vmem),
        scratch_shapes=[
            pltpu.SMEM(dia_shift.shape, jnp.int32),
            pltpu.SMEM(counts.shape, jnp.int32),
            pltpu.VMEM(spectrum.shape, F32),
            pltpu.VMEM(wind_vector.shape, F32),
            pltpu.VMEM((1, points), jnp.int32),
            pltpu.VMEM((freqs, 2 * dirs, points), F32),
            pltpu.VMEM((2 * lhs_rows, points), BF16),
            pltpu.VMEM((pieces, lhs_rows, LANES), F32),
            pltpu.SemaphoreType.DMA((5,)),
        ],
        compiler_params=pltpu.CompilerParams(vmem_limit_bytes=SOURCE_LIMIT),
        name="source",
    )(dia_shift, counts, spectrum, wind_vector, dest_cell.reshape(1, points))
    arrived = exchange(send, blocks, cap)
    first, second, cells = pl.pallas_call(
        functools.partial(edge_kernel, freqs, dirs, blocks),
        out_shape=(
            arr((edge_rows, NLON)),
            arr((edge_rows, NLON)),
            arr((1, points), jnp.int32),
        ),
        in_specs=[vmem],
        out_specs=(vmem,) * 3,
        scratch_shapes=[
            pltpu.VMEM((4 * edge_lhs, points), BF16),
            pltpu.VMEM((1, points), jnp.int32),
            pltpu.VMEM((2 * edge_lhs, 2 * NLON), F32),
        ],
        compiler_params=params,
        name="edges",
    )(arrived)
    inner, outer = halo_swaps(blocks)
    mine, theirs = lax.ppermute(first, "blk", inner), lax.ppermute(second, "blk", outer)
    field, middle, inner_part = pl.pallas_call(
        functools.partial(place_kernel, freqs, dirs, blocks),
        out_shape=(arr((rows, points)),) * 3,
        in_specs=[vmem] * 2,
        out_specs=(vmem,) * 3,
        scratch_shapes=[
            pltpu.VMEM((2 * rows, points), BF16),
            pltpu.VMEM((2 * rows, points - 2 * NLON), BF16),
        ],
        compiler_params=params,
        cost_estimate=pl.CostEstimate(
            flops=6 * rows * points * points, bytes_accessed=8 * rows * points, transcendentals=0
        ),
        name="place",
    )(arrived, cells)
    half = dirs // 2
    cross_rows = freqs * (-(-(half + 1) // 8) * 8 + STRIDE - half // 8 * 8)
    back = pl.pallas_call(
        functools.partial(step_kernel, freqs, dirs, blocks),
        out_shape=arr((pieces * freqs * dirs, LANES)),
        in_specs=[vmem] * 6,
        out_specs=vmem,
        scratch_shapes=[
            pltpu.VMEM((rows + 8, 2 * NLON), F32),
            pltpu.VMEM((rows + 8, 2 * NLON), F32),
            pltpu.VMEM((rows, 4 * NLON), F32),
            pltpu.VMEM((cross_rows, NLON), F32),
            pltpu.VMEM((2 * cross_rows, NLON), BF16),
            pltpu.VMEM((2 * rows, NLON), BF16),
            pltpu.VMEM((2 * rows, NLON), BF16),
        ],
        compiler_params=params,
        name="step",
    )(field, middle, inner_part, mine, theirs, cells)
    returned = exchange(back, blocks, cap)
    return pl.pallas_call(
        functools.partial(pick_kernel, freqs, dirs),
        out_shape=arr((freqs, dirs, points)),
        in_specs=[vmem, vmem],
        out_specs=hbm,
        scratch_shapes=[
            pltpu.VMEM((freqs, dirs, points), F32),
            pltpu.VMEM((2 * lhs_rows, points), BF16),
            pltpu.SemaphoreType.DMA((points // TILE,)),
        ],
        compiler_params=params,
        name="pick",
    )(returned, position)


def solution(mesh):
    placed = (
        P(None, None, ("groups", "blk")),
        P(None, ("groups", "blk")),
        P(("groups", "blk")),
        P(("groups", "blk")),
        P(("groups", "blk")),
        P(),
    )
    return jax.shard_map(
        per_device,
        mesh=mesh,
        in_specs=placed,
        out_specs=P(None, None, ("groups", "blk")),
        check_vma=False,
    )
```

```python
import functools
import math

import jax
import jax.numpy as jnp
from jax import lax
from jax.experimental import pallas as pl
from jax.experimental.pallas import tpu as pltpu
from jax.sharding import PartitionSpec as P

NLON = 512
SUBSTEPS = 2
LANES = 128
TILE = 256
GROUP = 2048
STRIDE = 40
F32 = jnp.float32
BF16 = jnp.bfloat16
VMEM_LIMIT = 40 * 1024 * 1024
SOURCE_LIMIT = 60 * 1024 * 1024


def snake_row(blocks):
    chips = max(blocks // 2, 1)
    return 1 << ((chips.bit_length() - 1) // 2)


def snake(index, blocks):
    row = snake_row(blocks)
    if blocks % (2 * row):
        return index
    core = lax.rem(index, 2)
    chip = lax.div(index, 2)
    line = lax.div(chip, row)
    place = lax.rem(chip, row)
    place = jnp.where(lax.rem(line, 2) == 1, row - 1 - place, place)
    return (line * row + place) * 2 + core


def halo_swaps(blocks):
    row = snake_row(blocks)
    order = []
    for band in range(blocks):
        if blocks % (2 * row):
            order.append(band)
            continue
        core, chip = band % 2, band // 2
        line, place = chip // row, chip % row
        if line % 2:
            place = row - 1 - place
        order.append((line * row + place) * 2 + core)

    def swaps(first):
        pairs = []
        for band in range(first, blocks - 1, 2):
            low, high = order[band], order[band + 1]
            pairs += [(low, high), (high, low)]
        return pairs

    return swaps(0), swaps(1)


def split(x):
    high = x.astype(BF16)
    return high, (x - high.astype(F32)).astype(BF16)


def one_hot(row, start, width):
    ids = lax.broadcasted_iota(jnp.int32, (TILE, width), 0).astype(F32).astype(BF16)
    wanted = (row - start).astype(F32).astype(BF16)
    return jnp.where(ids == wanted, jnp.ones((), BF16), jnp.zeros((), BF16))


def matmul_nt(data, table):
    return lax.dot_general(
        data, table, (((1,), (1,)), ((), ())), preferred_element_type=F32
    )


def direction_trig(dirs, rows):
    j = lax.broadcasted_iota(jnp.int32, (rows, LANES), 0)
    angles = (2.0 * math.pi / dirs) * j.astype(F32)
    return jnp.cos(angles), jnp.sin(angles)


def shifted(x, shift, size):
    count = x.shape[0] // 8
    fine = lax.rem(shift, 8)
    back = lax.rem(8 - fine, 8)
    keep = lax.broadcasted_iota(jnp.int32, (8, LANES), 0) < 8 - fine
    tiles = [pltpu.roll(x[8 * k : 8 * k + 8], back, 0) for k in range(count)]
    near = [jnp.where(keep, a, b) for a, b in zip(tiles, tiles[1:] + tiles[-1:])]
    out = [jnp.where(shift >= 8, b, a) for a, b in zip(near, near[1:] + near[-1:])]
    return jnp.concatenate(out, axis=0)[0:size]


def source_kernel(
    blocks,
    cap,
    shift_in,
    count_in,
    spec_in,
    wind_in,
    dest_in,
    send_ref,
    pos_ref,
    shift_ref,
    count_ref,
    spec_ref,
    wind_ref,
    dest_ref,
    dbl,
    lhs,
    acc,
    sems,
):
    freqs, dirs, points = spec_ref.shape
    rows = lhs.shape[0] // 2
    pairs = (
        (dest_in, dest_ref),
        (count_in, count_ref),
        (shift_in, shift_ref),
        (wind_in, wind_ref),
        (spec_in, spec_ref),
    )
    copies = [pltpu.make_async_copy(a, b, sems.at[i]) for i, (a, b) in enumerate(pairs)]
    for copy in copies:
        copy.start()
    copies[0].wait()
    copies[1].wait()
    dest = dest_ref[...]
    slot = lax.broadcasted_iota(jnp.int32, (1, points), 1)
    live = slot < count_ref[0]
    band = lax.shift_right_logical(dest, points.bit_length() - 1)
    band = jnp.where(live, band, -1)
    owner_band = snake(lax.broadcasted_iota(jnp.int32, (blocks, 1), 0), blocks)
    hits = (band == owner_band).astype(F32)
    tri_r = lax.broadcasted_iota(jnp.int32, (LANES, LANES), 0)
    tri_c = lax.broadcasted_iota(jnp.int32, (LANES, LANES), 1)
    upper = (tri_r <= tri_c).astype(F32).astype(BF16)
    ones = jnp.ones((LANES, LANES), BF16)
    base = (lax.broadcasted_iota(jnp.int32, (blocks, LANES), 0) * cap).astype(F32)
    for c in range(points // LANES):
        piece = hits[:, c * LANES : (c + 1) * LANES]
        packed = piece.astype(BF16)
        running = jnp.dot(packed, upper, preferred_element_type=F32) + base
        base = base + jnp.dot(packed, ones, preferred_element_type=F32)
        where_to = jnp.sum(piece * running, axis=0, keepdims=True) - 1.0
        pos_ref[:, c * LANES : (c + 1) * LANES] = where_to.astype(jnp.int32)
    for copy in copies[2:]:
        copy.wait()
    cos_a, sin_a = direction_trig(dirs, dirs)
    span = -(-(dirs + dirs // 4) // 8) * 8
    offset = 2 * dirs - span
    extra = rows - freqs * dirs

    def terms(c):
        where = slice(c * LANES, (c + 1) * LANES)
        total = jnp.zeros((1, LANES), F32)
        for f in range(freqs):
            x = spec_ref[f, :, where]
            dbl[f, 0:dirs, where] = x
            dbl[f, dirs : 2 * dirs, where] = x
            total = total + jnp.sum(x, axis=0, keepdims=True)
        mean = total * (1.0 / (freqs * dirs))
        along = wind_ref[0:1, where] * cos_a + wind_ref[1:2, where] * sin_a
        drive = jnp.maximum(along - 0.3, 0.0)
        pieces = []
        for f in range(freqs):
            x = spec_ref[f, :, where]
            ahead = shifted(dbl[f, 0:span, where], shift_ref[0], dirs)
            behind = shifted(dbl[f, offset:, where], dirs - offset - shift_ref[1], dirs)
            pieces.append(
                x * jnp.exp((0.15 + 0.05 * f) * drive - (0.2 + 0.1 * f) * mean)
                + 0.1 * (ahead * behind - x * x)
            )
        local = (lax.bitwise_and(dest_ref[:, where], points - 1) + 1).astype(F32)
        pieces.append(jnp.broadcast_to(local, (extra, LANES)))
        high, low = split(jnp.concatenate(pieces, axis=0))
        lhs[0:rows, where] = high
        lhs[rows : 2 * rows, where] = low

    per_step = TILE // LANES
    send_rows = freqs * dirs + 1

    def place(t, g):
        where = slice(g * GROUP, (g + 1) * GROUP)
        both = matmul_nt(lhs[:, where], one_hot(pos_ref[:, where], t * TILE, GROUP))
        out = both[0:rows] + both[rows : 2 * rows]
        for h in range(per_step):
            piece = out[:, h * LANES : (h + 1) * LANES]
            k = t * per_step + h
            if g:
                piece = acc[k] + piece
            if g < groups - 1:
                acc[k] = piece
            else:
                send_ref[k * send_rows : (k + 1) * send_rows, :] = piece[0:send_rows]

    groups = points // GROUP
    chunks = GROUP // LANES
    steps = points // TILE
    for g in range(groups + 1):
        for c in range(chunks):
            if g < groups:
                terms(g * chunks + c)
            if g > 0:
                for t in range(c * steps // chunks, (c + 1) * steps // chunks):
                    place(t, g - 1)


def spread_rows(get, freqs, dirs, points, lhs):
    rows = lhs.shape[0] // 2
    fill = jnp.ones((STRIDE - dirs - 2, LANES), F32)
    for c in range(points // LANES):
        x = get(c)
        pieces = []
        for f in range(freqs):
            one = x[f * dirs : (f + 1) * dirs]
            pieces += [one, one[0:1], fill, one[dirs - 1 : dirs]]
        high, low = split(jnp.concatenate(pieces, axis=0))
        lhs[0:rows, c * LANES : (c + 1) * LANES] = high
        lhs[rows : 2 * rows, c * LANES : (c + 1) * LANES] = low


def edge_kernel(freqs, dirs, blocks, recv_ref, first_ref, second_ref, cell_ref, lhs, fold_ref, out_ref):
    points = cell_ref.shape[1]
    label = freqs * dirs
    half = dirs // 2
    rows = lhs.shape[0] // 4
    near_rows = freqs * (half + 1) + 1
    edge = 2 * NLON
    fill = jnp.ones((rows - freqs * (half + 1), LANES), F32)
    for c in range(points // LANES):
        where = slice(c * LANES, (c + 1) * LANES)
        x = recv_ref[c * (label + 1) : (c + 1) * (label + 1), :]
        own = x[label : label + 1].astype(jnp.int32) - 1
        cell_ref[:, where] = own
        upper = own >= points - edge
        lower = (own >= 0) & (own < edge)
        fold_ref[:, where] = jnp.where(upper, own - (points - edge), jnp.where(lower, own, -1))
        for side, start, other, mine in ((0, 0, half, upper), (1, half, 0, lower)):
            pieces = []
            for f in range(freqs):
                base = f * dirs
                pieces.append(x[base + start : base + start + half])
                pieces.append(x[base + other : base + other + 1])
            high, low = split(jnp.where(mine, jnp.concatenate(pieces + [fill], axis=0), 0.0))
            lhs[side * rows : (side + 1) * rows, where] = high
            lhs[(2 + side) * rows : (3 + side) * rows, where] = low
    cells = fold_ref[...]
    even = lax.rem(snake(lax.axis_index("blk"), blocks), 2) == 0

    def keep(edge_ref, out, t, near):
        where = slice(t * TILE % NLON, t * TILE % NLON + TILE)
        if near:
            edge_ref[0:near_rows, where] = out[0:near_rows]
            return
        for f in range(freqs):
            at = near_rows + f * (half - 1)
            low = f * (half + 1) + 1
            edge_ref[at : at + half - 1, where] = out[low : low + half - 1]

    for t in range(edge // TILE):
        both = matmul_nt(lhs[...], one_hot(cells, t * TILE, points))
        out_ref[:, t * TILE : (t + 1) * TILE] = both[0 : 2 * rows] + both[2 * rows : 4 * rows]

    def store(up_ref, down_ref):
        for t in range(edge // TILE):
            out = out_ref[:, t * TILE : (t + 1) * TILE]
            second_row = t * TILE >= NLON
            keep(up_ref, out[0:rows], t, second_row)
            keep(down_ref, out[rows : 2 * rows], t, not second_row)

    @pl.when(even)
    def _():
        store(first_ref, second_ref)

    @pl.when(jnp.logical_not(even))
    def _():
        store(second_ref, first_ref)


def lanes(row):
    return slice(row * NLON, (row + 1) * NLON)


def stepper(freqs, dirs, blocks, row_count):
    band = snake(lax.axis_index("blk"), blocks)
    rows_all = row_count * blocks
    half = dirs // 2
    at = lax.broadcasted_iota(jnp.int32, (STRIDE, LANES), 0)
    j = jnp.where(at < dirs, at, jnp.where(at < STRIDE - 1, at - dirs, dirs - 1))
    angles = (2.0 * math.pi / dirs) * j.astype(F32)
    sin_a = jnp.where((j == 0) | (j == half), 0.0, jnp.sin(angles))
    cos_a = jnp.cos(angles)
    from_south = (at <= half)[:, 0:1]
    from_west = (cos_a > 0.0)[:, 0:1]
    cy_base = 0.5 * jnp.abs(sin_a)
    cx_base = 0.25 * jnp.abs(cos_a)

    index = [k if k < dirs else (k - dirs if k < STRIDE - 1 else dirs - 1) for k in range(STRIDE)]
    cosines = [math.cos(2.0 * math.pi * k / dirs) for k in index]

    def by_tile(low, high, values, mask, one, other):
        out = []
        for k in range(low, high, 8):
            signs = {v > 0 for v in values[k : k + 8] if abs(v) > 1e-9}
            if signs == {True}:
                out.append(one(k - low))
            elif signs == {False}:
                out.append(other(k - low))
            else:
                out.append(jnp.where(mask[k : k + 8], one(k - low), other(k - low)))
        return jnp.concatenate(out, axis=0)

    norths = [1 if k <= half else -1 for k in range(STRIDE)]
    latitudes = {}

    def latitude(row):
        if row not in latitudes:
            spot = (band * row_count + row).astype(F32) + 0.5
            lat = jnp.full((8, LANES), spot / rows_all * (2.0 * math.pi / 3.0) - math.pi / 3.0)
            sec = 1.0 / jnp.cos(lat)
            turn = -0.3 * cos_a * (jnp.sin(lat) * sec)[0:1]
            latitudes[row] = (
                (cx_base * sec[0:1])[:, 0:1],
                jnp.abs(turn)[:, 0:1],
                (turn > 0.0)[:, 0:1],
            )
        return latitudes[row]

    def advance(get, row, f, sea, low=0, high=STRIDE):
        part = slice(low, high)
        cx, ct, from_lower = latitude(row)
        speed = 1.0 / (1.0 + 0.25 * f)
        cy = (speed * cy_base)[part, 0:1]
        cx = (speed * cx)[part]
        ct = (speed * ct)[part]
        base = f * STRIDE + low
        x = get(row, slice(base, base + high - low))

        def rows_of(r):
            return lambda k: get(r, slice(base + k, base + k + 8))

        def turned_by(shift):
            return lambda k: pltpu.roll(x[k : k + 8], shift % NLON, 1)

        meridional = by_tile(low, high, norths, from_south, rows_of(row - 1), rows_of(row + 1))
        zonal = by_tile(low, high, cosines, from_west, turned_by(1), turned_by(-1))
        adv = (x - cy * (x - meridional) - cx * (x - zonal)) * sea
        return turned(adv, ct, from_lower[part]) * sea

    def turned(adv, ct, from_lower):
        lower = pltpu.roll(adv, 1, 0)
        upper = pltpu.roll(adv, adv.shape[0] - 1, 0)
        return adv - ct * (adv - jnp.where(from_lower, lower, upper))

    def answer(x, row, f, sea, low, high, valid):
        part = slice(low, high)
        _, ct, from_lower = latitude(row)
        speed = 1.0 / (1.0 + 0.25 * f)
        adv = jnp.where(valid[part], (speed * cy_base)[part, 0:1] * x, 0.0) * sea
        return turned(adv, (speed * ct)[part], from_lower[part]) * sea

    south_side = from_south
    north_side = jnp.logical_not(from_south) & (at <= dirs)[:, 0:1]
    return advance, answer, south_side, north_side


def repeat_ends(out, dirs):
    return jnp.concatenate(
        [out[0:dirs], out[0:1], out[dirs + 1 : STRIDE - 1], out[dirs - 1 : dirs]], axis=0
    )


def blank(row, piece):
    return jnp.zeros((piece.stop - piece.start, NLON), F32)


def pick_rows(lhs, cells, first, count, where):
    table = jnp.concatenate(
        [
            one_hot(cells[:, where], first * NLON + k * TILE, TILE)
            for k in range(count * NLON // TILE)
        ],
        axis=0,
    )
    both = jnp.dot(lhs[...], table, preferred_element_type=F32)
    half = lhs.shape[0] // 2
    return both[0:half] + both[half : 2 * half]


def place_kernel(freqs, dirs, blocks, recv_ref, cell_ref, field_ref, mid_ref, pre_ref, lhs, lhs2):
    points = cell_ref.shape[1]
    rows = freqs * STRIDE
    row_count = points // NLON
    count = freqs * dirs
    spread_rows(
        lambda c: recv_ref[c * (count + 1) : c * (count + 1) + count, :], freqs, dirs, points, lhs
    )
    cells = cell_ref[...]
    for t in range(points // TILE):
        both = matmul_nt(lhs[...], one_hot(cells, t * TILE, points))
        field_ref[:, t * TILE : (t + 1) * TILE] = both[0:rows] + both[rows : 2 * rows]
    advance = stepper(freqs, dirs, blocks, row_count)[0]

    def sea_of(row):
        return field_ref[dirs + 1 : dirs + 2, lanes(row)]

    def before(row, piece):
        if row < 0 or row >= row_count:
            return blank(row, piece)
        return field_ref[piece, lanes(row)]

    for row in range(row_count):
        for f in range(freqs):
            out = advance(before, row, f, sea_of(row))
            mid_ref[f * STRIDE : (f + 1) * STRIDE, lanes(row)] = repeat_ends(out, dirs)
    for row in range(1, row_count - 1):
        for f in range(freqs):
            out = advance(lambda r, piece: mid_ref[piece, lanes(r)], row, f, sea_of(row))
            high, low = split(out)
            base = f * STRIDE
            lhs2[base : base + STRIDE, lanes(row - 1)] = high
            lhs2[rows + base : rows + base + STRIDE, lanes(row - 1)] = low
    for t in range(points // TILE):
        where = slice(t * TILE, (t + 1) * TILE)
        pre_ref[:, where] = pick_rows(lhs2, cell_ref, 1, row_count - 2, where)


def step_kernel(
    freqs,
    dirs,
    blocks,
    field_ref,
    mid_ref,
    pre_ref,
    first_ref,
    second_ref,
    cell_ref,
    back_ref,
    south,
    north,
    outer,
    cross,
    lhs,
    lhs_low,
    lhs_high,
):
    points = field_ref.shape[1]
    rows = freqs * STRIDE
    row_count = points // NLON
    half = dirs // 2
    inside = half - 1
    near_rows = freqs * (half + 1) + 1
    top = row_count - 1

    def fill(ghost, in_ref, start):
        ghost[...] = jnp.zeros(ghost.shape, F32)
        for f in range(freqs):
            base = f * STRIDE + start
            at = f * (half + 1)
            ghost[base : base + half + 1, lanes(0)] = in_ref[at : at + half + 1, :]
            if start:
                top_row = (f + 1) * STRIDE - 1
                ghost[top_row : top_row + 1, lanes(0)] = in_ref[at + half - 1 : at + half, :]
            at = near_rows + f * inside
            ghost[base + 1 : base + half, lanes(1)] = in_ref[at : at + inside, :]
        ghost[rows : rows + 1, lanes(0)] = in_ref[near_rows - 1 : near_rows, :]

    even = lax.rem(snake(lax.axis_index("blk"), blocks), 2) == 0

    @pl.when(even)
    def _():
        fill(south, second_ref, 0)
        fill(north, first_ref, half)

    @pl.when(jnp.logical_not(even))
    def _():
        fill(south, first_ref, 0)
        fill(north, second_ref, half)

    def sea_of(row):
        if row < 0:
            return south[rows : rows + 1, lanes(0)]
        if row > top:
            return north[rows : rows + 1, lanes(0)]
        return field_ref[dirs + 1 : dirs + 2, lanes(row)]

    def before(row, piece):
        if row < 0:
            return south[piece, lanes(-1 - row)]
        if row > top:
            return north[piece, lanes(row - top - 1)]
        return field_ref[piece, lanes(row)]

    places = {-1: 0, 0: 1, top: 2, top + 1: 3}

    def between(row, piece):
        if row in places:
            return outer[piece, lanes(places[row])]
        return mid_ref[piece, lanes(row)]

    advance, answer, south_side, north_side = stepper(freqs, dirs, blocks, row_count)
    high = -(-(half + 1) // 8) * 8
    low = half // 8 * 8
    wide = STRIDE - low

    def first_step(f):
        base = f * STRIDE
        out = advance(before, -1, f, sea_of(-1), 0, high)
        outer[base : base + high, lanes(places[-1])] = out
        out = advance(before, top + 1, f, sea_of(top + 1), low, STRIDE)
        outer[base + low : base + STRIDE, lanes(places[top + 1])] = out
        spot = dirs - 1 - low
        outer[base + STRIDE - 1 : base + STRIDE, lanes(places[top + 1])] = out[spot : spot + 1]
        more = answer(
            south[base : base + high, lanes(0)], 0, f, sea_of(0), 0, high, south_side
        )
        cross[f * high : (f + 1) * high, :] = more
        old = mid_ref[base : base + STRIDE, lanes(0)]
        outer[base : base + STRIDE, lanes(places[0])] = jnp.concatenate(
            [
                old[0:high] + more,
                old[high:dirs],
                old[dirs : dirs + 1] + more[0:1],
                old[dirs + 1 : STRIDE],
            ],
            axis=0,
        )
        more = answer(
            north[base + low : base + STRIDE, lanes(0)], top, f, sea_of(top), low, STRIDE, north_side
        )
        at = freqs * high + f * wide
        cross[at : at + wide, :] = more
        old = mid_ref[base : base + STRIDE, lanes(top)]
        zero, last = more[dirs - low : dirs - low + 1], more[dirs - 1 - low : dirs - low]
        outer[base : base + STRIDE, lanes(places[top])] = jnp.concatenate(
            [
                old[0:1] + zero,
                old[1:low],
                old[low:dirs] + more[0 : dirs - low],
                old[dirs : dirs + 1] + zero,
                old[dirs + 1 : STRIDE - 1],
                old[STRIDE - 1 : STRIDE] + last,
            ],
            axis=0,
        )

    def second_step(f):
        base = f * STRIDE
        for row, out_lhs in ((0, lhs_low), (top, lhs_high)):
            upper, lower = split(advance(between, row, f, sea_of(row)))
            out_lhs[base : base + STRIDE, :] = upper
            out_lhs[rows + base : rows + base + STRIDE, :] = lower
        total = freqs * (high + wide)
        at = f * high
        upper, lower = split(
            answer(cross[at : at + high, :], 1, f, sea_of(1), 0, high, south_side)
        )
        lhs[at : at + high, :] = upper
        lhs[total + at : total + at + high, :] = lower
        at = freqs * high + f * wide
        upper, lower = split(
            answer(cross[at : at + wide, :], top - 1, f, sea_of(top - 1), low, STRIDE, north_side)
        )
        lhs[at : at + wide, :] = upper
        lhs[total + at : total + at + wide, :] = lower

    def pick(t):
        where = slice(t * TILE, (t + 1) * TILE)
        cells = cell_ref[:, where]
        out = pre_ref[:, where]
        out = out + pick_rows(lhs_low, cell_ref, 0, 1, where)
        out = out + pick_rows(lhs_high, cell_ref, top, 1, where)
        row = lax.shift_right_arithmetic(cells, NLON.bit_length() - 1)
        inside = jnp.where(
            row == 1, cells - NLON, jnp.where(row == top - 1, cells - (top - 1) * NLON, -1)
        )
        table = jnp.concatenate(
            [one_hot(inside, k * TILE, TILE) for k in range(NLON // TILE)], axis=0
        )
        both = jnp.dot(lhs[...], table, preferred_element_type=F32)
        total = freqs * (high + wide)
        both = both[0:total] + both[total : 2 * total]
        from_below = jnp.where(row == 1, both[0 : freqs * high], 0.0)
        from_above = jnp.where(row == top - 1, both[freqs * high : total], 0.0)
        for f in range(freqs):
            base = f * STRIDE
            below = from_below[f * high : (f + 1) * high]
            above = from_above[f * wide : (f + 1) * wide]
            sums = jnp.concatenate(
                [
                    out[base : base + low] + below[0:low],
                    out[base + low : base + high] + below[low:high] + above[0 : high - low],
                    out[base + high : base + STRIDE] + above[high - low : wide],
                ],
                axis=0,
            )
            first = sums[0:1] + above[dirs - low : dirs - low + 1]
            sums = jnp.concatenate([first, sums[1:dirs]], axis=0)
            for h in range(TILE // LANES):
                at = ((t * (TILE // LANES) + h) * freqs + f) * dirs
                back_ref[at : at + dirs, :] = sums[:, h * LANES : (h + 1) * LANES]

    for f in range(freqs):
        first_step(f)
    for f in range(freqs):
        second_step(f)
    for t in range(points // TILE):
        pick(t)


def pick_kernel(freqs, dirs, recv_ref, pos_ref, out_ref, result, lhs, sems):
    points = pos_ref.shape[1]
    rows = lhs.shape[0] // 2
    count = freqs * dirs
    fill = jnp.zeros((rows - count, LANES), F32)
    for c in range(points // LANES):
        x = jnp.concatenate([recv_ref[c * count : (c + 1) * count, :], fill], axis=0)
        high, low = split(x)
        lhs[0:rows, c * LANES : (c + 1) * LANES] = high
        lhs[rows : 2 * rows, c * LANES : (c + 1) * LANES] = low
    parts = []

    def body(t):
        where = slice(t * TILE, (t + 1) * TILE)
        wanted = pos_ref[:, where]
        table = jnp.concatenate(
            [one_hot(wanted, k * TILE, TILE) for k in range(points // TILE)], axis=0
        )
        both = jnp.dot(lhs[...], table, preferred_element_type=F32)
        out = both[0:rows] + both[rows : 2 * rows]
        for f in range(freqs):
            result[f, :, where] = out[f * dirs : (f + 1) * dirs]
        part = pltpu.make_async_copy(
            result.at[:, :, where], out_ref.at[:, :, where], sems.at[t]
        )
        part.start()
        parts.append(part)

    for t in range(points // TILE):
        body(t)
    for part in parts:
        part.wait()


def exchange(x, blocks, cap):
    pieces = blocks * cap // LANES
    rows = x.shape[0] // pieces
    if cap == LANES:
        parts = x.reshape(blocks, rows, 1, LANES)
        parts = lax.all_to_all(parts, "blk", split_axis=0, concat_axis=0, tiled=True)
        return parts.reshape(x.shape)
    parts = jnp.moveaxis(x.reshape(pieces, rows, LANES), 1, 0).reshape(rows, blocks, cap)
    parts = lax.all_to_all(parts, "blk", split_axis=1, concat_axis=1, tiled=True)
    return jnp.moveaxis(parts.reshape(rows, pieces, LANES), 0, 1).reshape(x.shape)


def per_device(spectrum, wind_vector, dest_cell, counts, sea_mask, dia_shift):
    blocks = lax.axis_size("blk")
    freqs, dirs, points = spectrum.shape
    cap = points // blocks
    pieces = points // LANES
    rows = freqs * STRIDE
    lhs_rows = -(-(freqs * dirs + 1) // 8) * 8
    near_rows = freqs * (dirs // 2 + 1) + 1
    far_rows = freqs * (dirs // 2 - 1)
    edge_rows = -(-(near_rows + far_rows) // 8) * 8
    edge_lhs = -(-near_rows // 8) * 8
    vmem = pl.BlockSpec(memory_space=pltpu.VMEM)
    hbm = pl.BlockSpec(memory_space=pltpu.HBM)
    params = pltpu.CompilerParams(vmem_limit_bytes=VMEM_LIMIT)

    def arr(shape, dtype=F32):
        return jax.ShapeDtypeStruct(shape, dtype)

    send, position = pl.pallas_call(
        functools.partial(source_kernel, blocks, cap),
        out_shape=(arr((pieces * (freqs * dirs + 1), LANES)), arr((1, points), jnp.int32)),
        in_specs=[hbm] * 5,
        out_specs=(vmem, vmem),
        scratch_shapes=[
            pltpu.SMEM(dia_shift.shape, jnp.int32),
            pltpu.SMEM(counts.shape, jnp.int32),
            pltpu.VMEM(spectrum.shape, F32),
            pltpu.VMEM(wind_vector.shape, F32),
            pltpu.VMEM((1, points), jnp.int32),
            pltpu.VMEM((freqs, 2 * dirs, points), F32),
            pltpu.VMEM((2 * lhs_rows, points), BF16),
            pltpu.VMEM((pieces, lhs_rows, LANES), F32),
            pltpu.SemaphoreType.DMA((5,)),
        ],
        compiler_params=pltpu.CompilerParams(vmem_limit_bytes=SOURCE_LIMIT),
        name="source",
    )(dia_shift, counts, spectrum, wind_vector, dest_cell.reshape(1, points))
    arrived = exchange(send, blocks, cap)
    first, second, cells = pl.pallas_call(
        functools.partial(edge_kernel, freqs, dirs, blocks),
        out_shape=(
            arr((edge_rows, NLON)),
            arr((edge_rows, NLON)),
            arr((1, points), jnp.int32),
        ),
        in_specs=[vmem],
        out_specs=(vmem,) * 3,
        scratch_shapes=[
            pltpu.VMEM((4 * edge_lhs, points), BF16),
            pltpu.VMEM((1, points), jnp.int32),
            pltpu.VMEM((2 * edge_lhs, 2 * NLON), F32),
        ],
        compiler_params=params,
        name="edges",
    )(arrived)
    inner, outer = halo_swaps(blocks)
    mine, theirs = lax.ppermute(first, "blk", inner), lax.ppermute(second, "blk", outer)
    field, middle, inner_part = pl.pallas_call(
        functools.partial(place_kernel, freqs, dirs, blocks),
        out_shape=(arr((rows, points)),) * 3,
        in_specs=[vmem] * 2,
        out_specs=(vmem,) * 3,
        scratch_shapes=[
            pltpu.VMEM((2 * rows, points), BF16),
            pltpu.VMEM((2 * rows, points - 2 * NLON), BF16),
        ],
        compiler_params=params,
        cost_estimate=pl.CostEstimate(
            flops=6 * rows * points * points, bytes_accessed=8 * rows * points, transcendentals=0
        ),
        name="place",
    )(arrived, cells)
    half = dirs // 2
    cross_rows = freqs * (-(-(half + 1) // 8) * 8 + STRIDE - half // 8 * 8)
    back = pl.pallas_call(
        functools.partial(step_kernel, freqs, dirs, blocks),
        out_shape=arr((pieces * freqs * dirs, LANES)),
        in_specs=[vmem] * 6,
        out_specs=vmem,
        scratch_shapes=[
            pltpu.VMEM((rows + 8, 2 * NLON), F32),
            pltpu.VMEM((rows + 8, 2 * NLON), F32),
            pltpu.VMEM((rows, 4 * NLON), F32),
            pltpu.VMEM((cross_rows, NLON), F32),
            pltpu.VMEM((2 * cross_rows, NLON), BF16),
            pltpu.VMEM((2 * rows, NLON), BF16),
            pltpu.VMEM((2 * rows, NLON), BF16),
        ],
        compiler_params=params,
        name="step",
    )(field, middle, inner_part, mine, theirs, cells)
    returned = exchange(back, blocks, cap)
    return pl.pallas_call(
        functools.partial(pick_kernel, freqs, dirs),
        out_shape=arr((freqs, dirs, points)),
        in_specs=[vmem, vmem],
        out_specs=hbm,
        scratch_shapes=[
            pltpu.VMEM((freqs, dirs, points), F32),
            pltpu.VMEM((2 * lhs_rows, points), BF16),
            pltpu.SemaphoreType.DMA((points // TILE,)),
        ],
        compiler_params=params,
        name="pick",
    )(returned, position)


def solution(mesh):
    placed = (
        P(None, None, ("groups", "blk")),
        P(None, ("groups", "blk")),
        P(("groups", "blk")),
        P(("groups", "blk")),
        P(("groups", "blk")),
        P(),
    )
    return jax.shard_map(
        per_device,
        mesh=mesh,
        in_specs=placed,
        out_specs=P(None, None, ("groups", "blk")),
        check_vma=False,
    )
```
